32 devices in a mesh: grp: 2 (over y), ep: 16 (over z, x, core).
Axes of the slice: x: 2, y: 2, z: 4, core: 2. Of those that a mesh axis runs over, the one named last changes fastest.
Arguments:
- hidden_in: bfloat16 [1024, 2048], P('ep'), may hold values from -45 to 45
- query_nope: bfloat16 [1024, 2048], P('ep', 'grp'), may hold values from -6 to 6
- query_rope: bfloat16 [1024, 1024], P('ep', 'grp'), may hold values from -56 to 56
- new_latent: bfloat16 [256, 2304], P('ep'), may hold values from -6 to 6
- latent_cache: bfloat16 [1024, 9216], P('ep'), may hold values from -6 to 6
- key_absorb: bfloat16 [16, 128, 512], P('grp'), may hold values from -0.5 to 0.5
- value_absorb: bfloat16 [16, 512, 128], P('grp'), may hold values from -1 to 1
- output_proj: bfloat16 [2048, 2048], P('grp'), may hold values from -0.125 to 0.125
- norm_gain: bfloat16 [2048], replicated, may hold values from 0.099609375 to 1.8984375
- router_proj: bfloat16 [2048, 16], replicated, may hold values from -0.125 to 0.125
- expert_ids: int32 [1024, 6], P('ep'), may hold values from 0 to 15, all different within a row; in each aligned block of 64 rows (0 to 63, 64 to 127, ...) at most 32 rows name the same one
- expert_gate: bfloat16 [16, 2048, 1408], P('ep', None, 'grp'), may hold values from -0.125 to 0.125
- expert_up: bfloat16 [16, 2048, 1408], P('ep', None, 'grp'), may hold values from -0.125 to 0.125
- expert_down: bfloat16 [16, 1408, 2048], P('ep', 'grp'), may hold values from -0.15625 to 0.15625
- block_table: int32 [256, 64], P('ep'), may hold values from 0 to 95, as said below
- lengths: int32 [256], P('ep'), may hold values from 1 to 1024
- subtree_moves: int32 [16, 16, 2], P('ep'), may hold values from -1 to 63, as said below
Outputs:
- mixed: bfloat16 [1024, 2048], P('ep', 'grp')
The draws below stay inside these ranges and needn't reach their ends.
Inputs may be any that keep to these rules, and one draw needn't show every extreme that they name: `expert_ids`: within the rows of one ep index no expert is named by more than 32 entries, a bound that some block reaches. `subtree_moves`: never the source itself; a live entry is a block id of the source; for every destination the rank after it sends 2 live blocks. `block_table`: an address names a resident block or a live moved block of that request's rank; the addresses of one request are distinct; the requests of a rank share a leading run of moved blocks.
All inputs are finite; a program needn't handle non-finite values.
Results may differ from the reference program's by a relative error of at most 0.0074.
Values may be sent and summed in bfloat16 or wider, within the bound.
No kernel may reach another device: no remote copies, remote signals or barrier semaphores. Data moves between devices by JAX's collectives and lax.ppermute only.
A program may use at most 64 MiB of HBM per device.

```python
import math
import jax
import jax.numpy as jnp
import numpy as np
from jax import lax

D = 2048
H = 16
DN = 128
DR = 64
LAT = 512
DV = 128
FF = 1408
TOP = 6
STEPS = 4
BS = 16
MIG = 2
REQ = 16
TBL = 64
NB_RES = 64
EXPERTS = 16
REQS = 256
ROWS = 1024
SLOTS_PER_RANK = 96
CAP = 32
N_EP = 16


def subtree_lists(key):
    key_live, key_blocks = jax.random.split(jax.random.fold_in(key, 101))
    live_slots = jax.random.randint(key_live, (N_EP, N_EP, MIG), 0, 2)
    ranks = jnp.arange(N_EP, dtype=jnp.int32)
    forced = (ranks[:, None] == (ranks[None, :] + 1) % N_EP)[:, :, None]
    diagonal = (ranks[:, None] == ranks[None, :])[:, :, None]
    live_slots = jnp.where(forced, 1, jnp.where(diagonal, 0, live_slots))
    block_ids = jax.random.randint(key_blocks, (N_EP, N_EP, MIG), 0, NB_RES)
    return jnp.where(live_slots == 1, block_ids, -1).astype(jnp.int32)


def order_slots(key, valid_mask, item_count):
    slot_addresses = jnp.arange(SLOTS_PER_RANK, dtype=jnp.int32)
    score_values = jax.random.randint(key, (item_count, SLOTS_PER_RANK), 0, 2 ** 20) * SLOTS_PER_RANK + slot_addresses[None, :]
    masked = jnp.where(valid_mask, score_values, -1)
    return jnp.argsort(-masked, axis=1).astype(jnp.int32)


def draw_subtree_moves(key, part):
    return subtree_lists(key)


def draw_block_table(key, part):
    moves = subtree_lists(key)
    key = jax.random.fold_in(key, 7)
    key_shared, key_own, key_span = jax.random.split(key, 3)
    incoming = jnp.transpose(moves >= 0, (1, 0, 2)).reshape(N_EP, N_EP * MIG)
    valid_in = jnp.concatenate([jnp.zeros((N_EP, NB_RES), bool), incoming], axis=1)
    valid_all = jnp.concatenate([jnp.ones((N_EP, NB_RES), bool), incoming], axis=1)
    shared_order = order_slots(key_shared, valid_in, N_EP)
    live_count = jnp.sum(incoming.astype(jnp.int32), axis=1)
    span = jnp.minimum(jax.random.randint(key_span, (N_EP,), TBL // 4, TBL // 2 + 1), live_count).astype(jnp.int32)
    rank_of_slot = jnp.argsort(shared_order, axis=1).astype(jnp.int32)
    in_shared = valid_in & (rank_of_slot < span[:, None])
    owner_rank = jnp.arange(REQS, dtype=jnp.int32) // REQ
    own_valid = valid_all[owner_rank] & jnp.logical_not(in_shared[owner_rank])
    own_order = order_slots(key_own, own_valid, REQS)
    position = jnp.arange(TBL, dtype=jnp.int32)
    request_span = span[owner_rank][:, None]
    from_shared = shared_order[owner_rank][:, :TBL]
    own_index = jnp.clip(position[None, :] - request_span, 0, TBL - 1).astype(jnp.int32)
    from_own = jnp.take_along_axis(own_order, own_index, axis=1)
    return jnp.where(position[None, :] < request_span, from_shared, from_own).astype(jnp.int32)


def draw_lengths(key, part):
    key = jax.random.fold_in(key, 11)
    sizes = jax.random.randint(key, (REQS,), 1, TBL * BS + 1)
    return sizes.at[0].set(TBL * BS).astype(jnp.int32)


def draw_new_latent(key, part):
    key = jax.random.fold_in(key, 3)
    values = jax.random.truncated_normal(key, -6.0, 6.0, (REQS, STEPS, LAT + DR), jnp.float32)
    return values.reshape(REQS, STEPS * (LAT + DR)).astype(jnp.bfloat16)


def draw_query_rope(key, part):
    key = jax.random.fold_in(key, 5)
    values = jax.random.truncated_normal(key, -6.0, 6.0, (REQS, STEPS, H, DR), jnp.float32)
    return values.reshape(REQS * STEPS, H * DR).astype(jnp.bfloat16)


def draw_hidden_in(key, part):
    key = jax.random.fold_in(key, 9)
    key_row, key_col, key_value = jax.random.split(key, 3)
    row_scale = jnp.exp(jax.random.uniform(key_row, (ROWS, 1), jnp.float32, math.log(0.3), math.log(3.0)))
    col_scale = jnp.exp(jax.random.uniform(key_col, (1, D), jnp.float32, math.log(0.3), math.log(3.0)))
    values = jax.random.truncated_normal(key_value, -4.0, 4.0, (ROWS, D), jnp.float32)
    return (values * row_scale * col_scale).astype(jnp.bfloat16)


def steps_of(own_key, shape, cuts, least, largest):
    gain = 1.0
    for dim, blocks in cuts:
        heights = jax.random.uniform(jax.random.fold_in(jax.random.fold_in(own_key, 6), dim), (blocks,), jnp.float32, least / len(cuts), largest / len(cuts))
        gain = gain * jnp.repeat(jnp.exp(heights), shape[dim] // blocks).reshape((-1,) + (1,) * (len(shape) - 1 - dim))
    return gain


def deal_out(rng, own, number, rows, amount, top, bound, slope):
    ranking = jax.random.permutation(rng, amount)
    crowded, usual = load_shares(amount, rows * top, bound, slope, True), load_shares(amount, rows * top, bound, slope, False)
    places = jnp.arange(amount)

    def named(sizes, rotation):
        used = int((sizes > 0).sum())
        fixed = max(1, used // 4)
        shifted = fixed + (places - fixed + rotation * (used - fixed)) % max(1, amount - fixed)
        return jnp.zeros((amount,), jnp.int32).at[ranking[jnp.where(places < fixed, places, shifted)]].set(jnp.asarray(sizes, jnp.int32))

    sizes = jnp.where(number % 4 == 0, named(crowded, number // 4), named(usual, number - number // 4 - 1))
    mixed = jax.random.permutation(jax.random.fold_in(own, 3), amount)
    source_of, sink = mixed[0:amount // 2 * 2:2], mixed[1:amount // 2 * 2:2]
    margin = jnp.minimum(sizes[source_of] - 1, bound - sizes[sink]) // 2
    margin = jnp.where((source_of == ranking[0]) | (sink == ranking[0]) | (sizes[sink] == 0), 0, jnp.maximum(margin, 0))
    shifted = jax.random.randint(jax.random.fold_in(own, 4), (amount // 2,), 0, 1 << 20) % (margin + 1)
    sizes = sizes.at[source_of].add(-shifted).at[sink].add(shifted)
    labels = jnp.searchsorted(jnp.cumsum(sizes), jnp.arange(rows * top), side="right").astype(jnp.int32)
    grid = labels.reshape(top, rows).T
    grid = grid[jax.random.permutation(jax.random.fold_in(own, 1), rows)]
    rotation = jax.random.randint(jax.random.fold_in(own, 2), (rows, 1), 0, top)
    return jnp.take_along_axis(grid, (jnp.arange(top)[None, :] + rotation) % top, axis=1)


def load_shares(amount, total, most, slope, full):
    loads = [(1 << 20) // math.isqrt(rank ** slope) + 1 for rank in range(1, amount + 1)]
    largest = most if full else min(most, max(-(-total // amount), total * loads[0] // sum(loads)))
    least = 1 if total - largest >= amount - 1 else 0
    given, spare = [largest] + [least] * (amount - 1), total - largest - least * (amount - 1)
    while spare > 0:
        free = [i for i in range(1, amount) if given[i] < largest] or [i for i in range(1, amount) if given[i] < most]
        pool, budget = sum([loads[i] for i in free]), spare
        for i in free:
            more = min(most - given[i], max(1, budget * loads[i] // pool), spare)
            given[i] = given[i] + more
            spare = spare - more
    return np.array(given)


def centred(rng, dims, spread, bound, cuts=(), held_as=jnp.bfloat16):
    array = jax.random.normal(rng, dims, jnp.float32) * spread
    if len(cuts) > 0:
        array = steps_of(rng, dims, cuts, -0.22, 0.18) * array
    return jnp.clip(array, min=-bound, max=bound).astype(held_as)


def setup_inputs(seed: int = 0) -> dict:
    splits = jax.random.split(jax.random.key(seed), 18)
    hidden_in = draw_hidden_in(jax.random.fold_in(splits[17], 71), 0)
    query_nope = centred(splits[1], (ROWS, H * DN), 1.0, 6.0, ((0, 16), (1, 2)))
    query_rope = draw_query_rope(jax.random.fold_in(splits[17], 71), 0)
    new_latent = draw_new_latent(jax.random.fold_in(splits[17], 71), 0)
    latent_cache = centred(splits[4], (N_EP * NB_RES, BS * (LAT + DR)), 1.0, 6.0, ((0, 16),))
    key_absorb = centred(splits[5], (H, DN, LAT), DN ** -0.5, 0.5, ((0, 2),))
    value_absorb = centred(splits[6], (H, LAT, DV), 32 ** -0.5, 1.0, ((0, 2),))
    output_proj = centred(splits[7], (H * DV, D), (H * DV) ** -0.5, 0.125, ((0, 2),))
    norm_gain = jnp.clip(1.0 + 0.18 * jax.random.normal(splits[8], (D,), jnp.float32), 0.099609375, 1.8984375).astype(jnp.bfloat16)
    router_proj = centred(splits[9], (D, EXPERTS), D ** -0.5, 0.125)
    expert_ids_keys = jax.random.split(jax.random.fold_in(splits[10], 1), ROWS // (REQ * STEPS))
    expert_ids_turns = jax.random.permutation(jax.random.fold_in(splits[10], 3), ROWS // (REQ * STEPS))
    expert_ids = jax.vmap(lambda own, number: deal_out(jax.random.fold_in(splits[10], 2), own, number, REQ * STEPS, EXPERTS, TOP, CAP, 2))(expert_ids_keys, expert_ids_turns).reshape((ROWS, TOP))
    expert_gate = centred(splits[11], (EXPERTS, D, FF), D ** -0.5, 0.125, ((0, 16), (2, 2)))
    expert_up = centred(splits[12], (EXPERTS, D, FF), D ** -0.5, 0.125, ((0, 16), (2, 2)))
    expert_down = centred(splits[13], (EXPERTS, FF, D), FF ** -0.5, 0.15625, ((0, 16), (1, 2)))
    block_table = draw_block_table(jax.random.fold_in(splits[17], 71), 0)
    lengths = draw_lengths(jax.random.fold_in(splits[17], 71), 0)
    subtree_moves = draw_subtree_moves(jax.random.fold_in(splits[17], 71), 0)
    return {"hidden_in": hidden_in, "query_nope": query_nope, "query_rope": query_rope, "new_latent": new_latent, "latent_cache": latent_cache, "key_absorb": key_absorb, "value_absorb": value_absorb, "output_proj": output_proj, "norm_gain": norm_gain, "router_proj": router_proj, "expert_ids": expert_ids, "expert_gate": expert_gate, "expert_up": expert_up, "expert_down": expert_down, "block_table": block_table, "lengths": lengths, "subtree_moves": subtree_moves}


def reference(hidden_in, query_nope, query_rope, new_latent, latent_cache, key_absorb, value_absorb, output_proj, norm_gain, router_proj, expert_ids, expert_gate, expert_up, expert_down, block_table, lengths, subtree_moves):
    key_width = LAT + DR
    scale_of_scores = (DN + DR) ** (-0.5)
    blocks = latent_cache.reshape(N_EP * NB_RES, BS, key_width)
    owner_rank = (jnp.arange(REQS, dtype=jnp.int32) // REQ)[:, None]
    offset = jnp.maximum(block_table - NB_RES, 0).astype(jnp.int32)
    source = offset // MIG
    within = offset % MIG
    moved_ids = subtree_moves[source, jnp.broadcast_to(owner_rank, source.shape), within]
    global_ids = jnp.where(block_table < NB_RES, owner_rank * NB_RES + block_table, source * NB_RES + moved_ids).astype(jnp.int32)
    q_latent = jnp.einsum('rhc,hcl->rhl', query_nope.reshape(ROWS, H, DN).astype(jnp.float32), key_absorb.astype(jnp.float32)).astype(jnp.bfloat16)
    queries = jnp.concatenate([q_latent, query_rope.reshape(ROWS, H, DR)], axis=2).reshape(REQS, STEPS * H, key_width)
    fresh_keys = new_latent.reshape(REQS, STEPS, key_width)
    cached = TBL * BS
    key_pos = jnp.arange(cached + STEPS, dtype=jnp.int32)
    row_step = jnp.arange(STEPS * H, dtype=jnp.int32) // H

    def attend(request):
        key_rows = jnp.concatenate([blocks[global_ids[request]].reshape(cached, key_width), fresh_keys[request]], axis=0)
        score_values = jnp.dot(queries[request], key_rows.T, preferred_element_type=jnp.float32) * scale_of_scores
        visible = jnp.where(key_pos[None, :] < cached, key_pos[None, :] < lengths[request], key_pos[None, :] - cached <= row_step[:, None])
        score_values = jnp.where(visible, score_values, -1e+30)
        row_peak = lax.optimization_barrier(jnp.max(score_values, axis=1, keepdims=True))
        exp_scores = jnp.exp(score_values - row_peak)
        attention = (exp_scores / lax.optimization_barrier(jnp.sum(exp_scores, axis=1, keepdims=True))).astype(jnp.bfloat16)
        return jnp.dot(attention, key_rows[:, :LAT], preferred_element_type=jnp.float32).astype(jnp.bfloat16)
    latent_out = lax.map(attend, jnp.arange(REQS, dtype=jnp.int32)).reshape(ROWS, H, LAT)
    head_out = jnp.einsum('rhl,hlv->rhv', latent_out.astype(jnp.float32), value_absorb.astype(jnp.float32)).astype(jnp.bfloat16).reshape(ROWS, H * DV)
    attention_out = jnp.dot(head_out, output_proj, preferred_element_type=jnp.float32)
    residual_state = hidden_in.astype(jnp.float32) + attention_out
    normed = (residual_state * lax.rsqrt(lax.optimization_barrier(jnp.mean(residual_state * residual_state, axis=1, keepdims=True)) + 1e-06) * norm_gain.astype(jnp.float32)).astype(jnp.bfloat16)
    logits = jnp.dot(normed, router_proj, preferred_element_type=jnp.float32)
    chosen = jax.nn.sigmoid(jnp.take_along_axis(logits, expert_ids, axis=1))
    gate_weights = chosen / lax.optimization_barrier(jnp.sum(chosen, axis=1, keepdims=True))
    flat_ids = expert_ids.reshape(N_EP, REQ * STEPS * TOP)
    onehot = (flat_ids[:, :, None] == jnp.arange(EXPERTS, dtype=jnp.int32)[None, None, :]).astype(jnp.int32)
    slot_index = lax.optimization_barrier(jnp.sum((jnp.cumsum(onehot, axis=1) - 1) * onehot, axis=2))
    target = (flat_ids * (N_EP * CAP) + jnp.arange(N_EP, dtype=jnp.int32)[:, None] * CAP + slot_index).reshape(ROWS * TOP).astype(jnp.int32)
    inputs = jnp.zeros((EXPERTS * N_EP * CAP, D), jnp.bfloat16).at[target].set(jnp.repeat(normed, TOP, axis=0))
    inputs = inputs.reshape(EXPERTS, N_EP * CAP, D)

    def expert_index(operands):
        expert_rows, gate_matrix, up_matrix, down_weight = operands
        gate_proj = jnp.dot(expert_rows, gate_matrix, preferred_element_type=jnp.float32)
        up_proj = jnp.dot(expert_rows, up_matrix, preferred_element_type=jnp.float32)
        activated = (jax.nn.silu(gate_proj) * up_proj).astype(jnp.bfloat16)
        return jnp.dot(activated, down_weight, preferred_element_type=jnp.float32)
    outputs = lax.map(expert_index, (inputs, expert_gate, expert_up, expert_down)).reshape(EXPERTS * N_EP * CAP, D)
    picked = outputs[target].reshape(ROWS, TOP, D)
    expert_mix = lax.optimization_barrier(jnp.sum(gate_weights[:, :, None] * picked, axis=1))
    return (residual_state + expert_mix).astype(jnp.bfloat16)
```

```python
import functools

import jax
import jax.numpy as jnp
from jax import lax
from jax.experimental import pallas as pl
from jax.experimental.pallas import tpu as pltpu
from jax.sharding import PartitionSpec as P

F32 = jnp.float32
BF16 = jnp.bfloat16
HIDDEN = -1e30
VMEM = pltpu.VMEM
ANY = pl.BlockSpec(memory_space=pl.ANY)
WHOLE = pl.BlockSpec(memory_space=pltpu.VMEM)


def dot(a, b):
    return jnp.dot(a, b, preferred_element_type=F32)


def dot_rows(a, b):
    return lax.dot_general(a, b, (((1,), (1,)), ((), ())), preferred_element_type=F32)


def cost(products, moved_bytes):
    return pl.CostEstimate(flops=2 * products, bytes_accessed=moved_bytes, transcendentals=0)


def fetch_all(sources, buffers, sems):
    copies = []
    for at, (source, buffer) in enumerate(zip(sources, buffers)):
        copy = pltpu.make_async_copy(source, buffer, sems.at[at])
        copy.start()
        copies.append(copy)
    return copies


def lay_tokens(keys, start, ref, tokens, width):
    count = ref.shape[0]
    for token in range(tokens):
        keys[start : start + count, :width] = ref[:, token * width : (token + 1) * width]
        start += count
    return start


def resident_kernel(
    dims, nope, rope_rows, fresh, cache, absorb, bias_ref,
    query_ref, mixed_ref,
    keys,
):
    head_count, nope_dim, latent, rope, block_size, steps = dims
    width = latent + rope
    rows = nope.shape[0]
    padding = keys.shape[1] - width
    keys[:, latent:] = jnp.zeros((keys.shape[0], keys.shape[1] - latent), BF16)
    start = lay_tokens(keys, 0, cache, block_size, width)
    lay_tokens(keys, start, fresh, steps, width)
    for head in range(head_count):
        q_latent = dot(nope[:, head * nope_dim : (head + 1) * nope_dim], absorb[head])
        q_rope = rope_rows[:, head * rope : (head + 1) * rope]
        fill = jnp.zeros((rows, padding), BF16)
        query_ref[head * rows : (head + 1) * rows, :] = jnp.concatenate(
            [q_latent.astype(BF16), q_rope, fill], axis=1
        )
    scale = (nope_dim + rope) ** (-0.5)
    part = min(4, head_count) * rows
    for first in range(0, head_count * rows, part):
        score = dot_rows(query_ref[first : first + part, :], keys[...])
        score = score.reshape(part // rows, rows, -1) * scale + bias_ref[...][None]
        score = score.reshape(part, -1)
        peak = jnp.max(score, axis=1, keepdims=True)
        weight = jnp.exp(score - peak)
        total = jnp.sum(weight, axis=1, keepdims=True)
        mixed_ref[first : first + part, :latent] = dot(weight.astype(BF16), keys[:, :latent])
        lane = lax.broadcasted_iota(jnp.int32, (part, 128), 1)
        mixed_ref[first : first + part, latent:] = jnp.where(lane < 64, peak, total)


def moved_kernel(
    dims, moved_any, query_any, bias_any, mixed_any, value_any, proj_any,
    share_ref,
    moved, query, bias, mixed, value, proj, keys, heads_out, sems,
):
    head_count, nope_dim, latent, rope, block_size, steps = dims
    width = latent + rope
    rows = heads_out.shape[0]
    got = fetch_all(
        (moved_any, query_any, bias_any, mixed_any, value_any, proj_any),
        (moved, query, bias, mixed, value, proj),
        sems,
    )
    keys[:, latent:] = jnp.zeros((keys.shape[0], keys.shape[1] - latent), BF16)
    scale = (nope_dim + rope) ** (-0.5)
    value_dim = value.shape[2]
    got[0].wait()
    count = moved.shape[0] * moved.shape[1]
    for half in range(2):
        part = moved[:, :, half * width : (half + 1) * width]
        keys[half * count : (half + 1) * count, :width] = part.reshape(count, width)
    got[1].wait()
    got[2].wait()
    group = min(4, head_count)
    for first in range(0, head_count, group):
        at = slice(first * rows, (first + group) * rows)
        score = dot_rows(query[at, :], keys[...])
        score = score.reshape(group, rows, -1) * scale + bias[...][None]
        score = score.reshape(group * rows, -1)
        if first == 0:
            got[3].wait()
        before = mixed[at, latent : latent + 1]
        peak = jnp.maximum(jnp.max(score, axis=1, keepdims=True), before)
        weight = jnp.exp(score - peak)
        keep = jnp.exp(before - peak)
        total = jnp.sum(weight, axis=1, keepdims=True) + mixed[at, latent + 64 : latent + 65] * keep
        joined = dot(weight.astype(BF16), keys[:, :latent]) + mixed[at, :latent] * keep
        joined = (joined / total).astype(BF16)
        if first == 0:
            got[4].wait()
        for head in range(first, first + group):
            own = joined[(head - first) * rows : (head - first + 1) * rows]
            heads_out[:, head * value_dim : (head + 1) * value_dim] = dot(own, value[head]).astype(BF16)
    got[5].wait()
    share_ref[...] = dot(heads_out[...], proj[...]).astype(BF16)


def own_columns(ref, shift):
    groups = lax.axis_size("grp")
    columns = ref.shape[1] // groups
    first = (lax.axis_index("grp") + shift) % groups * columns
    return ref[:, pl.ds(pl.multiple_of(first, 128), columns)]


def norm_kernel(experts, hidden_any, gain_ref, router_ref, ids_ref, *refs):
    parts, (state_ref, packet_ref, hidden, whole, sem) = refs[:-5], refs[-5:]
    copy = pltpu.make_async_copy(hidden_any, hidden, sem)
    copy.start()
    rows, model = hidden.shape
    state = parts[0][...].astype(F32)
    for part in parts[1:]:
        state = state + part[...].astype(F32)
    copy.wait()
    state = state + hidden[...].astype(F32)
    whole[...] = state
    state_ref[...] = own_columns(whole, 0)
    square = jnp.mean(state * state, axis=1, keepdims=True)
    normed = (state * lax.rsqrt(square + 1e-06) * gain_ref[...].astype(F32)).astype(BF16)
    packet_ref[:, :model] = normed
    logits = dot_rows(router_ref[...], normed)
    names = lax.broadcasted_iota(jnp.int32, (experts, rows), 0)
    named = names == ids_ref[0:1, :]
    for k in range(1, ids_ref.shape[0]):
        named = named | (names == ids_ref[k : k + 1, :])
    chosen = jnp.where(named, jax.nn.sigmoid(logits), 0.0)
    weight = chosen / jnp.sum(chosen, axis=0, keepdims=True)
    high = weight.astype(BF16)
    low = (weight - high.astype(F32)).astype(BF16)
    extra = packet_ref.shape[1] - model
    both = jnp.concatenate([high, low], axis=0)
    place = lax.broadcasted_iota(jnp.int32, (2 * experts, extra), 0)
    lane = lax.broadcasted_iota(jnp.int32, (2 * experts, extra), 1)
    turned = lax.dot_general(
        both, (place == lane).astype(BF16), (((0,), (0,)), ((), ())), preferred_element_type=F32
    )
    packet_ref[:, model:] = turned.astype(BF16)


def expert_kernel(experts, *refs):
    rows_refs, (gate_ref, up_ref, down_ref, near_ref, far_ref) = refs[:-5], refs[-5:]
    model = gate_ref.shape[1]
    packet = jnp.concatenate([ref[...] for ref in rows_refs], axis=0)
    rows = packet[:, :model]
    extra = packet[:, model:].astype(F32)
    names = lax.broadcasted_iota(jnp.int32, extra.shape, 1)
    me = lax.axis_index("ep")
    mine = (names == me) | (names == me + experts)
    weight = jnp.sum(jnp.where(mine, extra, 0.0), axis=1, keepdims=True)
    gate = dot_rows(rows, gate_ref[...])
    up = dot_rows(rows, up_ref[...])
    inner = (gate * jax.nn.sigmoid(gate) * up * weight).astype(BF16)
    result = dot(inner, down_ref[...]).astype(BF16)
    half = near_ref.shape[0]
    near_ref[...] = result[:half]
    far_ref[...] = result[half:]


def own_kernel(state_ref, own_ref, over_ref, base_ref, other_ref, whole):
    whole[...] = own_ref[...] + over_ref[...].astype(F32)
    base_ref[...] = state_ref[...] + own_columns(whole, 0)
    other_ref[...] = own_columns(whole, 1).astype(BF16)


def near_kernel(near_ref, far_ref, side_ref, two_ref, mine_ref, other_ref, whole):
    total = near_ref[...] + far_ref[...].astype(F32)
    whole[...] = total + side_ref[...].astype(F32) + two_ref[...].astype(F32)
    mine_ref[...] = own_columns(whole, 0).astype(BF16)
    other_ref[...] = own_columns(whole, 1).astype(BF16)


def local(
    hidden_in,
    query_nope,
    query_rope,
    new_latent,
    latent_cache,
    key_absorb,
    value_absorb,
    output_proj,
    norm_gain,
    router_proj,
    expert_ids,
    expert_gate,
    expert_up,
    expert_down,
    block_table,
    lengths,
    subtree_moves,
):
    head_count, nope_dim, latent = key_absorb.shape
    rope = query_rope.shape[1] // head_count
    width = latent + rope
    requests, table_len = block_table.shape
    steps = new_latent.shape[1] // width
    row_count, model = hidden_in.shape
    block_size = latent_cache.shape[1] // width
    resident = latent_cache.shape[0]
    experts = router_proj.shape[1]
    groups = lax.axis_size("grp")
    group = lax.axis_index("grp")
    ranks = lax.axis_size("ep")
    me = lax.axis_index("ep")
    ring = ranks // 4
    core_swap = [(i, i ^ 1) for i in range(ranks)]
    side_swap = [(i, i ^ 2) for i in range(ranks)]
    ring_next = [(i, (i + 4) % ranks) for i in range(ranks)]
    both_axes = ("grp", "ep")

    def turn(by):
        return [(g, (g + by) % groups) for g in range(groups)]

    sent = jnp.clip(subtree_moves.reshape(-1), 0, resident - 1)
    slots = subtree_moves.shape[2]
    pick = (sent[:, None] == jnp.arange(resident, dtype=jnp.int32)[None, :]).astype(BF16)
    pieces = block_size // 2
    outgoing = dot(pick, latent_cache).astype(BF16).reshape(ranks, slots * pieces, 2 * width)
    arrived = lax.all_to_all(outgoing, "ep", split_axis=0, concat_axis=0, tiled=True)

    place = jnp.arange(table_len, dtype=jnp.int32)
    usable = jnp.clip(lengths[:, None] - place[None, :] * block_size, 0, block_size)
    blocks = jnp.arange(resident + ranks * slots, dtype=jnp.int32)
    limit = jnp.sum(
        jnp.where(block_table[:, :, None] == blocks[None, None, :], usable[:, :, None], 0), axis=1
    )
    token = jnp.arange(block_size, dtype=jnp.int32)
    row = jnp.arange(row_count, dtype=jnp.int32)
    fresh = jnp.arange(steps * requests, dtype=jnp.int32)
    fresh_open = ((row // steps)[:, None] == (fresh % requests)[None, :]) & (
        (fresh // requests)[None, :] <= (row % steps)[:, None]
    )
    near_open = (limit[:, None, :resident] > token[None, :, None]).reshape(requests, -1)
    near_open = jnp.concatenate([jnp.repeat(near_open, steps, axis=0), fresh_open], axis=1)
    near_bias = jnp.where(near_open, 0.0, HIDDEN).astype(F32)
    by_key = jnp.repeat(limit[:, resident:], pieces, axis=1)
    at_token = 2 * (jnp.arange(ranks * slots * pieces, dtype=jnp.int32) % pieces)
    moved_open = jnp.concatenate([by_key > at_token[None], by_key > at_token[None] + 1], axis=1)
    moved_bias = jnp.repeat(jnp.where(moved_open, 0.0, HIDDEN).astype(F32), steps, axis=0)

    padded = -(-width // 128) * 128
    query_rows = head_count * row_count
    dims = (head_count, nope_dim, latent, rope, block_size, steps)
    query, mixed = pl.pallas_call(
        functools.partial(resident_kernel, dims),
        out_shape=(
            jax.ShapeDtypeStruct((query_rows, padded), BF16),
            jax.ShapeDtypeStruct((query_rows, latent + 128), F32),
        ),
        scratch_shapes=[VMEM((near_bias.shape[1], padded), BF16)],
        compiler_params=pltpu.CompilerParams(vmem_limit_bytes=16 * 2**20),
        cost_estimate=cost(query_rows * near_bias.shape[1] * (padded + latent), 8 * 2**20),
        name="attend_resident",
    )(query_nope, query_rope, new_latent, latent_cache, key_absorb, near_bias)
    share = pl.pallas_call(
        functools.partial(moved_kernel, dims),
        out_shape=jax.ShapeDtypeStruct((row_count, model), BF16),
        in_specs=[ANY] * 6,
        scratch_shapes=[
            VMEM(arrived.shape, BF16),
            VMEM(query.shape, BF16),
            VMEM(moved_bias.shape, F32),
            VMEM(mixed.shape, F32),
            VMEM(value_absorb.shape, BF16),
            VMEM(output_proj.shape, BF16),
            VMEM((moved_bias.shape[1], padded), BF16),
            VMEM((row_count, head_count * value_absorb.shape[2]), BF16),
            pltpu.SemaphoreType.DMA((6,)),
        ],
        compiler_params=pltpu.CompilerParams(vmem_limit_bytes=60 * 2**20),
        cost_estimate=cost(query_rows * moved_bias.shape[1] * (padded + latent), 10 * 2**20),
        name="attend_moved",
    )(arrived, query, moved_bias, mixed, value_absorb, output_proj)
    shares = [share]
    shares += [lax.ppermute(share, "grp", turn(by)) for by in range(1, groups)]

    extra = -(-2 * experts // 128) * 128
    columns = model // groups
    state, packet = pl.pallas_call(
        functools.partial(norm_kernel, experts),
        out_shape=(
            jax.ShapeDtypeStruct((row_count, columns), F32),
            jax.ShapeDtypeStruct((row_count, model + extra), BF16),
        ),
        in_specs=[ANY] + [WHOLE] * (3 + groups),
        scratch_shapes=[
            VMEM((row_count, model), BF16),
            VMEM((row_count, model), F32),
            pltpu.SemaphoreType.DMA(()),
        ],
        compiler_params=pltpu.CompilerParams(vmem_limit_bytes=16 * 2**20),
        cost_estimate=cost(row_count * model * 128, 4 * 2**20),
        name="norm",
    )(hidden_in, norm_gain[None, :], router_proj.T, expert_ids.T, *shares)

    gate_rows = jnp.swapaxes(expert_gate[0], 0, 1)
    up_rows = jnp.swapaxes(expert_up[0], 0, 1)

    def run_expert(rows):
        half = len(rows) * row_count
        out = jax.ShapeDtypeStruct((half, model), BF16)
        across = [lax.ppermute(part, "ep", core_swap) for part in rows]
        near, far = pl.pallas_call(
            functools.partial(expert_kernel, experts),
            out_shape=(out, out),
            in_specs=[WHOLE] * (2 * len(rows) + 3),
            compiler_params=pltpu.CompilerParams(vmem_limit_bytes=16 * 2**20),
            cost_estimate=cost(6 * half * model * gate_rows.shape[0], 12 * 2**20),
            name="expert",
        )(*rows, *across, gate_rows, up_rows, expert_down[0])
        return near.astype(F32) + lax.ppermute(far, "ep", core_swap).astype(F32)

    def send(value, axes, pairs):
        return lax.ppermute(value.astype(BF16), axes, pairs).astype(F32)

    if ring == 4 and groups == 2:
        def ring_step(sign):
            return [
                (g * ranks + i, g * ranks + (i + sign * 4 * (1 - 2 * g)) % ranks)
                for g in range(2)
                for i in range(ranks)
            ]

        onward, backward, plane_swap = ring_step(1), ring_step(-1), [(0, 1), (1, 0)]
        near = lax.ppermute(packet, both_axes, onward)
        side = lax.ppermute(packet, "ep", side_swap)
        two = lax.ppermute(near, both_axes, onward)
        near_side = lax.ppermute(near, "ep", side_swap)
        far = lax.ppermute(near, "grp", plane_swap)
        two_side = lax.ppermute(two, "ep", side_swap)
        far_side = lax.ppermute(near_side, "grp", plane_swap)
        cut = row_count
        own_sum = run_expert([side, packet])
        near_sum = run_expert([near_side, near])
        ahead_sum = run_expert([far, two])
        ahead_side = run_expert([far_side, two_side])
        far_side_in = lax.ppermute(ahead_side[:cut].astype(BF16), "grp", plane_swap)
        two_side_in = send(ahead_side[cut:], "ep", side_swap)
        far_in = lax.ppermute(ahead_sum[:cut].astype(BF16), "grp", plane_swap)
        own_in = lax.ppermute(own_sum[:cut].astype(BF16), "ep", side_swap)
        near_side = near_sum[:cut] + far_side_in.astype(F32)
        near_side_in = lax.ppermute(near_side.astype(BF16), "ep", side_swap)
        two_in = lax.ppermute((ahead_sum[cut:] + two_side_in).astype(BF16), both_axes, backward)
        part = (row_count, columns)

        def by_columns(kernel, first_type, *operands):
            return pl.pallas_call(
                kernel,
                out_shape=(
                    jax.ShapeDtypeStruct(part, first_type),
                    jax.ShapeDtypeStruct(part, BF16),
                ),
                scratch_shapes=[VMEM((row_count, model), F32)],
                compiler_params=pltpu.CompilerParams(vmem_limit_bytes=16 * 2**20),
                cost_estimate=cost(row_count * model, 2**20),
                name=kernel.__name__,
            )(*operands)

        base, own_other = by_columns(own_kernel, F32, state, own_sum[cut:], own_in)
        own_over = lax.ppermute(own_other, "grp", plane_swap)
        mine, other = by_columns(near_kernel, BF16, near_sum[cut:], far_in, near_side_in, two_in)
        crossed = [(source, (target + ranks) % (2 * ranks)) for source, target in backward]
        result = base + own_over.astype(F32)
        result = result + send(mine, both_axes, backward) + send(other, both_axes, crossed)
        return result.astype(BF16)

    line = [packet]
    for _ in range(1, ring):
        line.append(lax.ppermute(line[-1], "ep", ring_next))
    totals = []
    for part in line:
        both = run_expert([lax.ppermute(part, "ep", side_swap), part])
        totals.append(both[row_count:] + send(both[:row_count], "ep", side_swap))
    moving = totals[1 % ring]
    for hop in list(range(2, ring)) + [0]:
        moving = totals[hop] + send(moving, "ep", ring_next)

    result = state + lax.dynamic_slice_in_dim(moving, group * columns, columns, 1)
    for by in range(1, groups):
        to = (group + by) % groups
        part = lax.dynamic_slice_in_dim(moving, to * columns, columns, 1)
        result = result + send(part, "grp", turn(by))
    return result.astype(BF16)


def solution(mesh):
    in_specs = (
        P("ep", None),
        P("ep", "grp"),
        P("ep", "grp"),
        P("ep", None),
        P("ep", None),
        P("grp", None, None),
        P("grp", None, None),
        P("grp", None),
        P(),
        P(),
        P("ep", None),
        P("ep", None, "grp"),
        P("ep", None, "grp"),
        P("ep", "grp", None),
        P("ep", None),
        P("ep"),
        P("ep", None, None),
    )
    out_specs = P("ep", "grp")
    return jax.shard_map(local, mesh=mesh, in_specs=in_specs, out_specs=out_specs, check_vma=False)
```

```python
import functools

import jax
import jax.numpy as jnp
from jax import lax
from jax.experimental import pallas as pl
from jax.experimental.pallas import tpu as pltpu
from jax.sharding import PartitionSpec as P

F32 = jnp.float32
BF16 = jnp.bfloat16
HIDDEN = -1e30
VMEM = pltpu.VMEM
ANY = pl.BlockSpec(memory_space=pl.ANY)
WHOLE = pl.BlockSpec(memory_space=pltpu.VMEM)


def dot(a, b):
    return jnp.dot(a, b, preferred_element_type=F32)


def dot_rows(a, b):
    return lax.dot_general(a, b, (((1,), (1,)), ((), ())), preferred_element_type=F32)


def cost(products, moved_bytes):
    return pl.CostEstimate(flops=2 * products, bytes_accessed=moved_bytes, transcendentals=0)


def fetch_all(sources, buffers, sems):
    copies = []
    for at, (source, buffer) in enumerate(zip(sources, buffers)):
        copy = pltpu.make_async_copy(source, buffer, sems.at[at])
        copy.start()
        copies.append(copy)
    return copies


def lay_tokens(keys, start, ref, tokens, width):
    count = ref.shape[0]
    for token in range(tokens):
        keys[start : start + count, :width] = ref[:, token * width : (token + 1) * width]
        start += count
    return start


def resident_kernel(
    dims, nope, rope_rows, fresh, cache, absorb, bias_ref,
    query_ref, mixed_ref,
    keys,
):
    head_count, nope_dim, latent, rope, block_size, steps = dims
    width = latent + rope
    rows = nope.shape[0]
    padding = keys.shape[1] - width
    keys[:, latent:] = jnp.zeros((keys.shape[0], keys.shape[1] - latent), BF16)
    start = lay_tokens(keys, 0, cache, block_size, width)
    lay_tokens(keys, start, fresh, steps, width)
    for head in range(head_count):
        q_latent = dot(nope[:, head * nope_dim : (head + 1) * nope_dim], absorb[head])
        q_rope = rope_rows[:, head * rope : (head + 1) * rope]
        fill = jnp.zeros((rows, padding), BF16)
        query_ref[head * rows : (head + 1) * rows, :] = jnp.concatenate(
            [q_latent.astype(BF16), q_rope, fill], axis=1
        )
    scale = (nope_dim + rope) ** (-0.5)
    part = min(4, head_count) * rows
    for first in range(0, head_count * rows, part):
        score = dot_rows(query_ref[first : first + part, :], keys[...])
        score = score.reshape(part // rows, rows, -1) * scale + bias_ref[...][None]
        score = score.reshape(part, -1)
        peak = jnp.max(score, axis=1, keepdims=True)
        weight = jnp.exp(score - peak)
        total = jnp.sum(weight, axis=1, keepdims=True)
        mixed_ref[first : first + part, :latent] = dot(weight.astype(BF16), keys[:, :latent])
        lane = lax.broadcasted_iota(jnp.int32, (part, 128), 1)
        mixed_ref[first : first + part, latent:] = jnp.where(lane < 64, peak, total)


def moved_kernel(
    dims, moved_any, query_any, bias_any, mixed_any, value_any, proj_any,
    share_ref,
    moved, query, bias, mixed, value, proj, keys, heads_out, sems,
):
    head_count, nope_dim, latent, rope, block_size, steps = dims
    width = latent + rope
    rows = heads_out.shape[0]
    got = fetch_all(
        (moved_any, query_any, bias_any, mixed_any, value_any, proj_any),
        (moved, query, bias, mixed, value, proj),
        sems,
    )
    keys[:, latent:] = jnp.zeros((keys.shape[0], keys.shape[1] - latent), BF16)
    scale = (nope_dim + rope) ** (-0.5)
    value_dim = value.shape[2]
    got[0].wait()
    count = moved.shape[0] * moved.shape[1]
    for half in range(2):
        part = moved[:, :, half * width : (half + 1) * width]
        keys[half * count : (half + 1) * count, :width] = part.reshape(count, width)
    got[1].wait()
    got[2].wait()
    group = min(4, head_count)
    for first in range(0, head_count, group):
        at = slice(first * rows, (first + group) * rows)
        score = dot_rows(query[at, :], keys[...])
        score = score.reshape(group, rows, -1) * scale + bias[...][None]
        score = score.reshape(group * rows, -1)
        if first == 0:
            got[3].wait()
        before = mixed[at, latent : latent + 1]
        peak = jnp.maximum(jnp.max(score, axis=1, keepdims=True), before)
        weight = jnp.exp(score - peak)
        keep = jnp.exp(before - peak)
        total = jnp.sum(weight, axis=1, keepdims=True) + mixed[at, latent + 64 : latent + 65] * keep
        joined = dot(weight.astype(BF16), keys[:, :latent]) + mixed[at, :latent] * keep
        joined = (joined / total).astype(BF16)
        if first == 0:
            got[4].wait()
        for head in range(first, first + group):
            own = joined[(head - first) * rows : (head - first + 1) * rows]
            heads_out[:, head * value_dim : (head + 1) * value_dim] = dot(own, value[head]).astype(BF16)
    got[5].wait()
    share_ref[...] = dot(heads_out[...], proj[...]).astype(BF16)


def own_columns(ref, shift):
    groups = lax.axis_size("grp")
    columns = ref.shape[1] // groups
    first = (lax.axis_index("grp") + shift) % groups * columns
    return ref[:, pl.ds(pl.multiple_of(first, 128), columns)]


def norm_kernel(experts, own_any, hidden_any, loaded_any, gain_ref, router_ref, ids_ref, *refs):
    parts, (state_ref, packet_ref, own, hidden, whole, sems) = refs[:-6], refs[-6:]
    got = fetch_all((own_any, hidden_any), (own, hidden), sems)
    rows, model = hidden.shape
    state = parts[0][...].astype(F32)
    for part in parts[1:]:
        state = state + part[...].astype(F32)
    for copy in got:
        copy.wait()
    state = state + own[...].astype(F32) + hidden[...].astype(F32)
    whole[...] = state
    state_ref[...] = own_columns(whole, 0)
    square = jnp.mean(state * state, axis=1, keepdims=True)
    normed = (state * lax.rsqrt(square + 1e-06) * gain_ref[...].astype(F32)).astype(BF16)
    packet_ref[:, :model] = normed
    logits = dot_rows(router_ref[...], normed)
    names = lax.broadcasted_iota(jnp.int32, (experts, rows), 0)
    named = names == ids_ref[0:1, :]
    for k in range(1, ids_ref.shape[0]):
        named = named | (names == ids_ref[k : k + 1, :])
    chosen = jnp.where(named, jax.nn.sigmoid(logits), 0.0)
    weight = chosen / jnp.sum(chosen, axis=0, keepdims=True)
    high = weight.astype(BF16)
    low = (weight - high.astype(F32)).astype(BF16)
    extra = packet_ref.shape[1] - model
    both = jnp.concatenate([high, low], axis=0)
    place = lax.broadcasted_iota(jnp.int32, (2 * experts, extra), 0)
    lane = lax.broadcasted_iota(jnp.int32, (2 * experts, extra), 1)
    turned = lax.dot_general(
        both, (place == lane).astype(BF16), (((0,), (0,)), ((), ())), preferred_element_type=F32
    )
    packet_ref[:, model:] = turned.astype(BF16)


def load_kernel(after_any, gate_any, up_any, down_any, gate_ref, up_ref, down_ref, sems):
    sources, targets = (gate_any, up_any, down_any), (gate_ref, up_ref, down_ref)
    for copy in fetch_all(sources, targets, sems):
        copy.wait()


def pack_kernel(after_any, *refs):
    out_ref = refs[-1]
    count = refs[0].shape[0]
    for at, ref in enumerate(refs[:-1]):
        out_ref[at * count : (at + 1) * count, :] = ref[...]


def expert_kernel(experts, here_ref, across_ref, gate_ref, up_ref, down_ref, near_ref, far_ref):
    model = gate_ref.shape[1]
    packet = jnp.concatenate([here_ref[...], across_ref[...]], axis=0)
    rows = packet[:, :model]
    extra = packet[:, model:].astype(F32)
    names = lax.broadcasted_iota(jnp.int32, extra.shape, 1)
    me = lax.axis_index("ep")
    mine = (names == me) | (names == me + experts)
    weight = jnp.sum(jnp.where(mine, extra, 0.0), axis=1, keepdims=True)
    gate = dot_rows(rows, gate_ref[...])
    up = dot_rows(rows, up_ref[...])
    inner = (gate * jax.nn.sigmoid(gate) * up * weight).astype(BF16)
    result = dot(inner, down_ref[...]).astype(BF16)
    half = near_ref.shape[0]
    near_ref[...] = result[:half]
    far_ref[...] = result[half:]


def join_kernel(first, after_count, near_ref, back_ref, *refs):
    out_refs = refs[after_count:]
    count = out_refs[0].shape[0]
    for at, ref in enumerate(out_refs, first):
        rows = slice(at * count, (at + 1) * count)
        ref[...] = (near_ref[rows, :].astype(F32) + back_ref[rows, :].astype(F32)).astype(ref.dtype)


def own_kernel(state_ref, own_ref, base_ref, other_ref):
    base_ref[...] = state_ref[...] + own_columns(own_ref, 0)
    other_ref[...] = own_columns(own_ref, 1).astype(BF16)


def sum_kernel(*refs):
    parts, (mine_ref, other_ref) = refs[:-2], refs[-2:]
    for shift, ref in ((0, mine_ref), (1, other_ref)):
        total = own_columns(parts[0], shift).astype(F32)
        for part in parts[1:]:
            total = total + own_columns(part, shift).astype(F32)
        ref[...] = total.astype(BF16)


def local(
    hidden_in,
    query_nope,
    query_rope,
    new_latent,
    latent_cache,
    key_absorb,
    value_absorb,
    output_proj,
    norm_gain,
    router_proj,
    expert_ids,
    expert_gate,
    expert_up,
    expert_down,
    block_table,
    lengths,
    subtree_moves,
):
    head_count, nope_dim, latent = key_absorb.shape
    rope = query_rope.shape[1] // head_count
    width = latent + rope
    requests, table_len = block_table.shape
    steps = new_latent.shape[1] // width
    row_count, model = hidden_in.shape
    block_size = latent_cache.shape[1] // width
    resident = latent_cache.shape[0]
    experts = router_proj.shape[1]
    groups = lax.axis_size("grp")
    group = lax.axis_index("grp")
    ranks = lax.axis_size("ep")
    me = lax.axis_index("ep")
    ring = ranks // 4
    core_swap = [(i, i ^ 1) for i in range(ranks)]
    side_swap = [(i, i ^ 2) for i in range(ranks)]
    ring_next = [(i, (i + 4) % ranks) for i in range(ranks)]
    both_axes = ("grp", "ep")

    def turn(by):
        return [(g, (g + by) % groups) for g in range(groups)]

    sent = jnp.clip(subtree_moves.reshape(-1), 0, resident - 1)
    slots = subtree_moves.shape[2]
    pick = (sent[:, None] == jnp.arange(resident, dtype=jnp.int32)[None, :]).astype(BF16)
    pieces = block_size // 2
    outgoing = dot(pick, latent_cache).astype(BF16).reshape(ranks, slots * pieces, 2 * width)
    arrived = lax.all_to_all(outgoing, "ep", split_axis=0, concat_axis=0, tiled=True)

    place = jnp.arange(table_len, dtype=jnp.int32)
    usable = jnp.clip(lengths[:, None] - place[None, :] * block_size, 0, block_size)
    blocks = jnp.arange(resident + ranks * slots, dtype=jnp.int32)
    limit = jnp.sum(
        jnp.where(block_table[:, :, None] == blocks[None, None, :], usable[:, :, None], 0), axis=1
    )
    token = jnp.arange(block_size, dtype=jnp.int32)
    row = jnp.arange(row_count, dtype=jnp.int32)
    fresh = jnp.arange(steps * requests, dtype=jnp.int32)
    fresh_open = ((row // steps)[:, None] == (fresh % requests)[None, :]) & (
        (fresh // requests)[None, :] <= (row % steps)[:, None]
    )
    near_open = (limit[:, None, :resident] > token[None, :, None]).reshape(requests, -1)
    near_open = jnp.concatenate([jnp.repeat(near_open, steps, axis=0), fresh_open], axis=1)
    near_bias = jnp.where(near_open, 0.0, HIDDEN).astype(F32)
    by_key = jnp.repeat(limit[:, resident:], pieces, axis=1)
    at_token = 2 * (jnp.arange(ranks * slots * pieces, dtype=jnp.int32) % pieces)
    moved_open = jnp.concatenate([by_key > at_token[None], by_key > at_token[None] + 1], axis=1)
    moved_bias = jnp.repeat(jnp.where(moved_open, 0.0, HIDDEN).astype(F32), steps, axis=0)

    padded = -(-width // 128) * 128
    query_rows = head_count * row_count
    dims = (head_count, nope_dim, latent, rope, block_size, steps)
    query, mixed = pl.pallas_call(
        functools.partial(resident_kernel, dims),
        out_shape=(
            jax.ShapeDtypeStruct((query_rows, padded), BF16),
            jax.ShapeDtypeStruct((query_rows, latent + 128), F32),
        ),
        scratch_shapes=[VMEM((near_bias.shape[1], padded), BF16)],
        compiler_params=pltpu.CompilerParams(vmem_limit_bytes=16 * 2**20),
        cost_estimate=cost(query_rows * near_bias.shape[1] * (padded + latent), 8 * 2**20),
        name="attend_resident",
    )(query_nope, query_rope, new_latent, latent_cache, key_absorb, near_bias)
    share = pl.pallas_call(
        functools.partial(moved_kernel, dims),
        out_shape=jax.ShapeDtypeStruct((row_count, model), BF16),
        in_specs=[ANY] * 6,
        scratch_shapes=[
            VMEM(arrived.shape, BF16),
            VMEM(query.shape, BF16),
            VMEM(moved_bias.shape, F32),
            VMEM(mixed.shape, F32),
            VMEM(value_absorb.shape, BF16),
            VMEM(output_proj.shape, BF16),
            VMEM((moved_bias.shape[1], padded), BF16),
            VMEM((row_count, head_count * value_absorb.shape[2]), BF16),
            pltpu.SemaphoreType.DMA((6,)),
        ],
        compiler_params=pltpu.CompilerParams(vmem_limit_bytes=60 * 2**20),
        cost_estimate=cost(query_rows * moved_bias.shape[1] * (padded + latent), 10 * 2**20),
        name="attend_moved",
    )(arrived, query, moved_bias, mixed, value_absorb, output_proj)
    shares = [lax.ppermute(share, "grp", turn(by)) for by in range(1, groups)]

    held = [jnp.swapaxes(expert_gate[0], 0, 1), jnp.swapaxes(expert_up[0], 0, 1), expert_down[0]]
    gate_rows, up_rows, down_rows = pl.pallas_call(
        load_kernel,
        out_shape=[jax.ShapeDtypeStruct(array.shape, BF16) for array in held],
        in_specs=[ANY] * 4,
        out_specs=[WHOLE] * 3,
        scratch_shapes=[pltpu.SemaphoreType.DMA((3,))],
        compiler_params=pltpu.CompilerParams(vmem_limit_bytes=44 * 2**20),
        cost_estimate=cost(0, 12 * 2**20),
        name="load",
    )(share, *held)

    extra = -(-2 * experts // 128) * 128
    columns = model // groups
    state, packet = pl.pallas_call(
        functools.partial(norm_kernel, experts),
        out_shape=(
            jax.ShapeDtypeStruct((row_count, columns), F32),
            jax.ShapeDtypeStruct((row_count, model + extra), BF16),
        ),
        in_specs=[ANY] * 3 + [WHOLE] * (2 + groups),
        scratch_shapes=[
            VMEM((row_count, model), BF16),
            VMEM((row_count, model), BF16),
            VMEM((row_count, model), F32),
            pltpu.SemaphoreType.DMA((2,)),
        ],
        compiler_params=pltpu.CompilerParams(vmem_limit_bytes=16 * 2**20),
        cost_estimate=cost(row_count * model * 128, 4 * 2**20),
        name="norm",
    )(share, hidden_in, down_rows, norm_gain[None, :], router_proj.T, expert_ids.T, *shares)

    def run_expert(rows, after):
        half = len(rows) * row_count
        out = jax.ShapeDtypeStruct((half, model), BF16)
        here = pl.pallas_call(
            pack_kernel,
            out_shape=jax.ShapeDtypeStruct((half, model + extra), BF16),
            in_specs=[ANY] + [WHOLE] * len(rows),
            compiler_params=pltpu.CompilerParams(vmem_limit_bytes=16 * 2**20),
            cost_estimate=cost(0, 2 * half * model * 2),
            name="pack",
        )(after, *rows)
        across = lax.ppermute(here, "ep", core_swap)
        near, far = pl.pallas_call(
            functools.partial(expert_kernel, experts),
            out_shape=(out, out),
            in_specs=[WHOLE] * 5,
            compiler_params=pltpu.CompilerParams(vmem_limit_bytes=24 * 2**20),
            cost_estimate=cost(6 * half * model * gate_rows.shape[0], 12 * 2**20),
            name="expert",
        )(here, across, gate_rows, up_rows, down_rows)
        return near, lax.ppermute(far, "ep", core_swap)

    def join(near, back, types, first=0, after=()):
        return pl.pallas_call(
            functools.partial(join_kernel, first, len(after)),
            out_shape=[jax.ShapeDtypeStruct((row_count, model), kind) for kind in types],
            in_specs=[WHOLE] * 2 + [ANY] * len(after),
            compiler_params=pltpu.CompilerParams(vmem_limit_bytes=16 * 2**20),
            cost_estimate=cost(row_count * model, 2**20),
            name="join",
        )(near, back, *after)

    def send(value, axes, pairs):
        return lax.ppermute(value.astype(BF16), axes, pairs).astype(F32)

    if ring == 4 and groups == 2:
        def ring_step(sign):
            return [
                (g * ranks + i, g * ranks + (i + sign * 4 * (1 - 2 * g)) % ranks)
                for g in range(2)
                for i in range(ranks)
            ]

        onward, backward, plane_swap = ring_step(1), ring_step(-1), [(0, 1), (1, 0)]
        near = lax.ppermute(packet, both_axes, onward)
        side = lax.ppermute(packet, "ep", side_swap)
        two = lax.ppermute(near, both_axes, onward)
        near_side = lax.ppermute(near, "ep", side_swap)
        far = lax.ppermute(near, "grp", plane_swap)
        two_side = lax.ppermute(two, "ep", side_swap)
        far_side = lax.ppermute(near_side, "grp", plane_swap)
        early = run_expert([packet, side, near], packet)
        later = run_expert([near_side, two, far], early[0])
        last = run_expert([far_side, two_side], later[0])
        own_sum, side_sum, near_sum = join(*early, [F32, BF16, F32])
        near_side_sum, two_sum = join(*later, [F32, F32])
        far_side_sum, two_side_sum = join(*last, [BF16, BF16])
        far_side_in = lax.ppermute(far_side_sum, "grp", plane_swap)
        two_side_in = lax.ppermute(two_side_sum, "ep", side_swap)
        [near_side_sum] = join(near_side_sum, far_side_in, [BF16])
        [two_sum] = join(two_sum, two_side_in, [BF16])
        near_side_in = lax.ppermute(near_side_sum, "ep", side_swap)
        two_in = lax.ppermute(two_sum, both_axes, backward)
        [far_sum] = join(*later, [BF16], 2, [far_side_in])
        far_in = lax.ppermute(far_sum, "grp", plane_swap)
        part = (row_count, columns)

        def by_columns(kernel, first_type, *operands):
            return pl.pallas_call(
                kernel,
                out_shape=(
                    jax.ShapeDtypeStruct(part, first_type),
                    jax.ShapeDtypeStruct(part, BF16),
                ),
                compiler_params=pltpu.CompilerParams(vmem_limit_bytes=16 * 2**20),
                cost_estimate=cost(row_count * model, 2**20),
                name=kernel.__name__,
            )(*operands)

        def crossed(pairs):
            return [(source, (target + ranks) % (2 * ranks)) for source, target in pairs]

        sideways = [(i, i ^ 2) for i in range(2 * ranks)]
        base, own_other = by_columns(own_kernel, F32, state, own_sum)
        side_mine, side_other = by_columns(sum_kernel, BF16, side_sum)
        near_mine, near_other = by_columns(
            sum_kernel, BF16, near_sum, far_in, near_side_in, two_in
        )
        result = base + send(own_other, "grp", plane_swap)
        result = result + send(side_mine, both_axes, sideways)
        result = result + send(side_other, both_axes, crossed(sideways))
        result = result + send(near_mine, both_axes, backward)
        result = result + send(near_other, both_axes, crossed(backward))
        return result.astype(BF16)

    line = [packet]
    for _ in range(1, ring):
        line.append(lax.ppermute(line[-1], "ep", ring_next))
    totals = []
    for part in line:
        sums = run_expert([lax.ppermute(part, "ep", side_swap), part], packet)
        over, here = join(*sums, [BF16, F32])
        totals.append(here + send(over, "ep", side_swap))
    moving = totals[1 % ring]
    for hop in list(range(2, ring)) + [0]:
        moving = totals[hop] + send(moving, "ep", ring_next)

    result = state + lax.dynamic_slice_in_dim(moving, group * columns, columns, 1)
    for by in range(1, groups):
        to = (group + by) % groups
        part = lax.dynamic_slice_in_dim(moving, to * columns, columns, 1)
        result = result + send(part, "grp", turn(by))
    return result.astype(BF16)


def solution(mesh):
    in_specs = (
        P("ep", None),
        P("ep", "grp"),
        P("ep", "grp"),
        P("ep", None),
        P("ep", None),
        P("grp", None, None),
        P("grp", None, None),
        P("grp", None),
        P(),
        P(),
        P("ep", None),
        P("ep", None, "grp"),
        P("ep", None, "grp"),
        P("ep", "grp", None),
        P("ep", None),
        P("ep"),
        P("ep", None, None),
    )
    out_specs = P("ep", "grp")
    return jax.shard_map(local, mesh=mesh, in_specs=in_specs, out_specs=out_specs, check_vma=False)
```

```python
import functools

import jax
import jax.numpy as jnp
from jax import lax
from jax.experimental import pallas as pl
from jax.experimental.pallas import tpu as pltpu
from jax.sharding import PartitionSpec as P

F32 = jnp.float32
BF16 = jnp.bfloat16
HIDDEN = -1e30
VMEM = pltpu.VMEM
ANY = pl.BlockSpec(memory_space=pl.ANY)
WHOLE = pl.BlockSpec(memory_space=pltpu.VMEM)


def dot(a, b):
    return jnp.dot(a, b, preferred_element_type=F32)


def dot_rows(a, b):
    return lax.dot_general(a, b, (((1,), (1,)), ((), ())), preferred_element_type=F32)


def cost(products, moved_bytes):
    return pl.CostEstimate(flops=2 * products, bytes_accessed=moved_bytes, transcendentals=0)


def fetch_all(sources, buffers, sems):
    copies = []
    for at, (source, buffer) in enumerate(zip(sources, buffers)):
        copy = pltpu.make_async_copy(source, buffer, sems.at[at])
        copy.start()
        copies.append(copy)
    return copies


def lay_tokens(keys, start, ref, tokens, width):
    count = ref.shape[0]
    for token in range(tokens):
        keys[start : start + count, :width] = ref[:, token * width : (token + 1) * width]
        start += count
    return start


def pick_kernel(pieces, moves_ref, cache_any, out_ref, cache, stacked, sems):
    [copy] = fetch_all((cache_any,), (cache,), sems)
    ranks, per_rank, wide = out_ref.shape
    slots = moves_ref.shape[0]
    resident = cache.shape[0]
    rows = ranks * per_rank
    row = lax.broadcasted_iota(jnp.int32, (rows, ranks), 0)
    rank = lax.broadcasted_iota(jnp.int32, (rows, ranks), 1)
    chosen = jnp.zeros((rows, ranks), jnp.int32)
    for slot in range(slots):
        here = (row // per_rank == rank) & (row % per_rank // pieces == slot)
        chosen = chosen + jnp.where(here, moves_ref[slot : slot + 1, :], 0)
    block = jnp.clip(jnp.sum(chosen, axis=1, keepdims=True), 0, resident - 1)
    at = lax.broadcasted_iota(jnp.int32, (rows, pieces * resident), 0)
    source = lax.broadcasted_iota(jnp.int32, (rows, pieces * resident), 1)
    pick = (source // resident == at % pieces) & (source % resident == block)
    copy.wait()
    for piece in range(pieces):
        stacked[piece * resident : (piece + 1) * resident, :] = cache[:, piece * wide : (piece + 1) * wide]
    picked = dot(pick.astype(F32).astype(BF16), stacked[...]).astype(BF16)
    out_ref[...] = picked.reshape(ranks, per_rank, wide)


def resident_kernel(
    dims, nope, rope_rows, fresh, cache, absorb, bias_ref,
    query_ref, mixed_ref,
    keys,
):
    head_count, nope_dim, latent, rope, block_size, steps = dims
    width = latent + rope
    rows = nope.shape[0]
    padding = keys.shape[1] - width
    keys[:, latent:] = jnp.zeros((keys.shape[0], keys.shape[1] - latent), BF16)
    start = lay_tokens(keys, 0, cache, block_size, width)
    lay_tokens(keys, start, fresh, steps, width)
    for head in range(head_count):
        q_latent = dot(nope[:, head * nope_dim : (head + 1) * nope_dim], absorb[head])
        q_rope = rope_rows[:, head * rope : (head + 1) * rope]
        fill = jnp.zeros((rows, padding), BF16)
        query_ref[head * rows : (head + 1) * rows, :] = jnp.concatenate(
            [q_latent.astype(BF16), q_rope, fill], axis=1
        )
    scale = (nope_dim + rope) ** (-0.5)
    part = min(4, head_count) * rows
    for first in range(0, head_count * rows, part):
        score = dot_rows(query_ref[first : first + part, :], keys[...])
        score = score.reshape(part // rows, rows, -1) * scale + bias_ref[...][None]
        score = score.reshape(part, -1)
        peak = jnp.max(score, axis=1, keepdims=True)
        weight = jnp.exp(score - peak)
        total = jnp.sum(weight, axis=1, keepdims=True)
        mixed_ref[first : first + part, :latent] = dot(weight.astype(BF16), keys[:, :latent])
        lane = lax.broadcasted_iota(jnp.int32, (part, 128), 1)
        mixed_ref[first : first + part, latent:] = jnp.where(lane < 64, peak, total)


def moved_kernel(
    dims, moved_any, query_any, bias_any, mixed_any, value_any, proj_any,
    share_ref,
    moved, query, bias, mixed, value, proj, keys, heads_out, sems,
):
    head_count, nope_dim, latent, rope, block_size, steps = dims
    width = latent + rope
    rows = heads_out.shape[0]
    got = fetch_all((moved_any, query_any, bias_any), (moved, query, bias), sems)
    keys[:, latent:] = jnp.zeros((keys.shape[0], keys.shape[1] - latent), BF16)
    scale = (nope_dim + rope) ** (-0.5)
    value_dim = value.shape[2]
    got[0].wait()
    got += fetch_all((mixed_any, value_any, proj_any), (mixed, value, proj), sems.at[pl.ds(3, 3)])
    count = moved.shape[0] * moved.shape[1]
    for half in range(2):
        part = moved[:, :, half * width : (half + 1) * width]
        keys[half * count : (half + 1) * count, :width] = part.reshape(count, width)
    got[1].wait()
    got[2].wait()
    group = min(4, head_count)
    for first in range(0, head_count, group):
        at = slice(first * rows, (first + group) * rows)
        score = dot_rows(query[at, :], keys[...])
        score = score.reshape(group, rows, -1) * scale + bias[...][None]
        score = score.reshape(group * rows, -1)
        if first == 0:
            got[3].wait()
        before = mixed[at, latent : latent + 1]
        peak = jnp.maximum(jnp.max(score, axis=1, keepdims=True), before)
        weight = jnp.exp(score - peak)
        keep = jnp.exp(before - peak)
        total = jnp.sum(weight, axis=1, keepdims=True) + mixed[at, latent + 64 : latent + 65] * keep
        joined = dot(weight.astype(BF16), keys[:, :latent]) + mixed[at, :latent] * keep
        joined = (joined / total).astype(BF16)
        if first == 0:
            got[4].wait()
        for head in range(first, first + group):
            own = joined[(head - first) * rows : (head - first + 1) * rows]
            heads_out[:, head * value_dim : (head + 1) * value_dim] = dot(own, value[head]).astype(BF16)
    got[5].wait()
    share_ref[...] = dot(heads_out[...], proj[...]).astype(BF16)


def own_columns(ref, shift):
    groups = lax.axis_size("grp")
    columns = ref.shape[1] // groups
    first = (lax.axis_index("grp") + shift) % groups * columns
    return ref[:, pl.ds(pl.multiple_of(first, 128), columns)]


def norm_kernel(experts, own_any, hidden_any, loaded_any, gain_ref, router_ref, ids_ref, *refs):
    parts, (state_ref, packet_ref, own, hidden, whole, sems) = refs[:-6], refs[-6:]
    got = fetch_all((own_any, hidden_any), (own, hidden), sems)
    rows, model = hidden.shape
    state = parts[0][...].astype(F32)
    for part in parts[1:]:
        state = state + part[...].astype(F32)
    for copy in got:
        copy.wait()
    state = state + own[...].astype(F32) + hidden[...].astype(F32)
    whole[...] = state
    state_ref[...] = own_columns(whole, 0)
    square = jnp.mean(state * state, axis=1, keepdims=True)
    normed = (state * lax.rsqrt(square + 1e-06) * gain_ref[...].astype(F32)).astype(BF16)
    packet_ref[:, :model] = normed
    logits = dot_rows(router_ref[...], normed)
    names = lax.broadcasted_iota(jnp.int32, (experts, rows), 0)
    named = names == ids_ref[0:1, :]
    for k in range(1, ids_ref.shape[0]):
        named = named | (names == ids_ref[k : k + 1, :])
    chosen = jnp.where(named, jax.nn.sigmoid(logits), 0.0)
    weight = chosen / jnp.sum(chosen, axis=0, keepdims=True)
    high = weight.astype(BF16)
    low = (weight - high.astype(F32)).astype(BF16)
    extra = packet_ref.shape[1] - model
    both = jnp.concatenate([high, low], axis=0)
    place = lax.broadcasted_iota(jnp.int32, (2 * experts, extra), 0)
    lane = lax.broadcasted_iota(jnp.int32, (2 * experts, extra), 1)
    turned = lax.dot_general(
        both, (place == lane).astype(BF16), (((0,), (0,)), ((), ())), preferred_element_type=F32
    )
    packet_ref[:, model:] = turned.astype(BF16)


def load_kernel(after_any, gate_any, up_any, down_any, gate_ref, up_ref, down_ref, sems):
    sources, targets = (gate_any, up_any, down_any), (gate_ref, up_ref, down_ref)
    for copy in fetch_all(sources, targets, sems):
        copy.wait()


def pack_kernel(after_any, *refs):
    out_ref = refs[-1]
    count = refs[0].shape[0]
    for at, ref in enumerate(refs[:-1]):
        out_ref[at * count : (at + 1) * count, :] = ref[...]


def expert_kernel(experts, here_ref, across_ref, gate_ref, up_ref, down_ref, near_ref, far_ref):
    model = gate_ref.shape[1]
    packet = jnp.concatenate([here_ref[...], across_ref[...]], axis=0)
    rows = packet[:, :model]
    extra = packet[:, model:].astype(F32)
    names = lax.broadcasted_iota(jnp.int32, extra.shape, 1)
    me = lax.axis_index("ep")
    mine = (names == me) | (names == me + experts)
    weight = jnp.sum(jnp.where(mine, extra, 0.0), axis=1, keepdims=True)
    gate = dot_rows(rows, gate_ref[...])
    up = dot_rows(rows, up_ref[...])
    inner = (gate * jax.nn.sigmoid(gate) * up * weight).astype(BF16)
    result = dot(inner, down_ref[...]).astype(BF16)
    half = near_ref.shape[0]
    near_ref[...] = result[:half]
    far_ref[...] = result[half:]


def join_kernel(first, after_count, near_ref, back_ref, *refs):
    out_refs = refs[after_count:]
    count = out_refs[0].shape[0]
    for at, ref in enumerate(out_refs, first):
        rows = slice(at * count, (at + 1) * count)
        ref[...] = (near_ref[rows, :].astype(F32) + back_ref[rows, :].astype(F32)).astype(ref.dtype)


def own_kernel(state_ref, own_ref, base_ref, other_ref):
    base_ref[...] = state_ref[...] + own_columns(own_ref, 0)
    other_ref[...] = own_columns(own_ref, 1).astype(BF16)


def sum_kernel(*refs):
    parts, (mine_ref, other_ref) = refs[:-2], refs[-2:]
    for shift, ref in ((0, mine_ref), (1, other_ref)):
        total = own_columns(parts[0], shift).astype(F32)
        for part in parts[1:]:
            total = total + own_columns(part, shift).astype(F32)
        ref[...] = total.astype(BF16)


def local(
    hidden_in,
    query_nope,
    query_rope,
    new_latent,
    latent_cache,
    key_absorb,
    value_absorb,
    output_proj,
    norm_gain,
    router_proj,
    expert_ids,
    expert_gate,
    expert_up,
    expert_down,
    block_table,
    lengths,
    subtree_moves,
):
    head_count, nope_dim, latent = key_absorb.shape
    rope = query_rope.shape[1] // head_count
    width = latent + rope
    requests, table_len = block_table.shape
    steps = new_latent.shape[1] // width
    row_count, model = hidden_in.shape
    block_size = latent_cache.shape[1] // width
    resident = latent_cache.shape[0]
    experts = router_proj.shape[1]
    groups = lax.axis_size("grp")
    group = lax.axis_index("grp")
    ranks = lax.axis_size("ep")
    me = lax.axis_index("ep")
    ring = ranks // 4
    core_swap = [(i, i ^ 1) for i in range(ranks)]
    side_swap = [(i, i ^ 2) for i in range(ranks)]
    ring_next = [(i, (i + 4) % ranks) for i in range(ranks)]
    both_axes = ("grp", "ep")

    def turn(by):
        return [(g, (g + by) % groups) for g in range(groups)]

    slots = subtree_moves.shape[2]
    pieces = block_size // 2
    outgoing = pl.pallas_call(
        functools.partial(pick_kernel, pieces),
        out_shape=jax.ShapeDtypeStruct((ranks, slots * pieces, 2 * width), BF16),
        in_specs=[WHOLE, ANY],
        scratch_shapes=[
            VMEM(latent_cache.shape, BF16),
            VMEM((pieces * resident, 2 * width), BF16),
            pltpu.SemaphoreType.DMA((1,)),
        ],
        compiler_params=pltpu.CompilerParams(vmem_limit_bytes=16 * 2**20),
        cost_estimate=cost(0, 4 * 2**20),
        name="pick",
    )(subtree_moves[0].T, latent_cache)
    arrived = lax.all_to_all(outgoing, "ep", split_axis=0, concat_axis=0, tiled=True)

    place = jnp.arange(table_len, dtype=jnp.int32)
    usable = jnp.clip(lengths[:, None] - place[None, :] * block_size, 0, block_size)
    blocks = jnp.arange(resident + ranks * slots, dtype=jnp.int32)
    limit = jnp.sum(
        jnp.where(block_table[:, :, None] == blocks[None, None, :], usable[:, :, None], 0), axis=1
    )
    token = jnp.arange(block_size, dtype=jnp.int32)
    row = jnp.arange(row_count, dtype=jnp.int32)
    fresh = jnp.arange(steps * requests, dtype=jnp.int32)
    fresh_open = ((row // steps)[:, None] == (fresh % requests)[None, :]) & (
        (fresh // requests)[None, :] <= (row % steps)[:, None]
    )
    near_open = (limit[:, None, :resident] > token[None, :, None]).reshape(requests, -1)
    near_open = jnp.concatenate([jnp.repeat(near_open, steps, axis=0), fresh_open], axis=1)
    near_bias = jnp.where(near_open, 0.0, HIDDEN).astype(F32)
    by_key = jnp.repeat(limit[:, resident:], pieces, axis=1)
    at_token = 2 * (jnp.arange(ranks * slots * pieces, dtype=jnp.int32) % pieces)
    moved_open = jnp.concatenate([by_key > at_token[None], by_key > at_token[None] + 1], axis=1)
    moved_bias = jnp.repeat(jnp.where(moved_open, 0.0, HIDDEN).astype(F32), steps, axis=0)

    padded = -(-width // 128) * 128
    query_rows = head_count * row_count
    dims = (head_count, nope_dim, latent, rope, block_size, steps)
    query, mixed = pl.pallas_call(
        functools.partial(resident_kernel, dims),
        out_shape=(
            jax.ShapeDtypeStruct((query_rows, padded), BF16),
            jax.ShapeDtypeStruct((query_rows, latent + 128), F32),
        ),
        scratch_shapes=[VMEM((near_bias.shape[1], padded), BF16)],
        compiler_params=pltpu.CompilerParams(vmem_limit_bytes=16 * 2**20),
        cost_estimate=cost(query_rows * near_bias.shape[1] * (padded + latent), 8 * 2**20),
        name="attend_resident",
    )(query_nope, query_rope, new_latent, latent_cache, key_absorb, near_bias)
    share = pl.pallas_call(
        functools.partial(moved_kernel, dims),
        out_shape=jax.ShapeDtypeStruct((row_count, model), BF16),
        in_specs=[ANY] * 6,
        scratch_shapes=[
            VMEM(arrived.shape, BF16),
            VMEM(query.shape, BF16),
            VMEM(moved_bias.shape, F32),
            VMEM(mixed.shape, F32),
            VMEM(value_absorb.shape, BF16),
            VMEM(output_proj.shape, BF16),
            VMEM((moved_bias.shape[1], padded), BF16),
            VMEM((row_count, head_count * value_absorb.shape[2]), BF16),
            pltpu.SemaphoreType.DMA((6,)),
        ],
        compiler_params=pltpu.CompilerParams(vmem_limit_bytes=60 * 2**20),
        cost_estimate=cost(query_rows * moved_bias.shape[1] * (padded + latent), 10 * 2**20),
        name="attend_moved",
    )(arrived, query, moved_bias, mixed, value_absorb, output_proj)
    shares = [lax.ppermute(share, "grp", turn(by)) for by in range(1, groups)]

    held = [jnp.swapaxes(expert_gate[0], 0, 1), jnp.swapaxes(expert_up[0], 0, 1), expert_down[0]]
    gate_rows, up_rows, down_rows = pl.pallas_call(
        load_kernel,
        out_shape=[jax.ShapeDtypeStruct(array.shape, BF16) for array in held],
        in_specs=[ANY] * 4,
        out_specs=[WHOLE] * 3,
        scratch_shapes=[pltpu.SemaphoreType.DMA((3,))],
        compiler_params=pltpu.CompilerParams(vmem_limit_bytes=44 * 2**20),
        cost_estimate=cost(0, 12 * 2**20),
        name="load",
    )(share, *held)

    extra = -(-2 * experts // 128) * 128
    columns = model // groups
    state, packet = pl.pallas_call(
        functools.partial(norm_kernel, experts),
        out_shape=(
            jax.ShapeDtypeStruct((row_count, columns), F32),
            jax.ShapeDtypeStruct((row_count, model + extra), BF16),
        ),
        in_specs=[ANY] * 3 + [WHOLE] * (2 + groups),
        scratch_shapes=[
            VMEM((row_count, model), BF16),
            VMEM((row_count, model), BF16),
            VMEM((row_count, model), F32),
            pltpu.SemaphoreType.DMA((2,)),
        ],
        compiler_params=pltpu.CompilerParams(vmem_limit_bytes=16 * 2**20),
        cost_estimate=cost(row_count * model * 128, 4 * 2**20),
        name="norm",
    )(share, hidden_in, down_rows, norm_gain[None, :], router_proj.T, expert_ids.T, *shares)

    def run_expert(rows, after):
        half = len(rows) * row_count
        out = jax.ShapeDtypeStruct((half, model), BF16)
        here = pl.pallas_call(
            pack_kernel,
            out_shape=jax.ShapeDtypeStruct((half, model + extra), BF16),
            in_specs=[ANY] + [WHOLE] * len(rows),
            compiler_params=pltpu.CompilerParams(vmem_limit_bytes=16 * 2**20),
            cost_estimate=cost(0, 2 * half * model * 2),
            name="pack",
        )(after, *rows)
        across = lax.ppermute(here, "ep", core_swap)
        near, far = pl.pallas_call(
            functools.partial(expert_kernel, experts),
            out_shape=(out, out),
            in_specs=[WHOLE] * 5,
            compiler_params=pltpu.CompilerParams(vmem_limit_bytes=24 * 2**20),
            cost_estimate=cost(6 * half * model * gate_rows.shape[0], 12 * 2**20),
            name="expert",
        )(here, across, gate_rows, up_rows, down_rows)
        return near, lax.ppermute(far, "ep", core_swap)

    def join(near, back, types, first=0, after=()):
        return pl.pallas_call(
            functools.partial(join_kernel, first, len(after)),
            out_shape=[jax.ShapeDtypeStruct((row_count, model), kind) for kind in types],
            in_specs=[WHOLE] * 2 + [ANY] * len(after),
            compiler_params=pltpu.CompilerParams(vmem_limit_bytes=16 * 2**20),
            cost_estimate=cost(row_count * model, 2**20),
            name="join",
        )(near, back, *after)

    def send(value, axes, pairs):
        return lax.ppermute(value.astype(BF16), axes, pairs).astype(F32)

    if ring == 4 and groups == 2:
        def ring_step(sign):
            return [
                (g * ranks + i, g * ranks + (i + sign * 4 * (1 - 2 * g)) % ranks)
                for g in range(2)
                for i in range(ranks)
            ]

        onward, backward, plane_swap = ring_step(1), ring_step(-1), [(0, 1), (1, 0)]
        near = lax.ppermute(packet, both_axes, onward)
        side = lax.ppermute(packet, "ep", side_swap)
        two = lax.ppermute(near, both_axes, onward)
        near_side = lax.ppermute(near, "ep", side_swap)
        far = lax.ppermute(near, "grp", plane_swap)
        two_side = lax.ppermute(two, "ep", side_swap)
        far_side = lax.ppermute(near_side, "grp", plane_swap)
        early = run_expert([packet, side, near], packet)
        later = run_expert([near_side, two, far], early[0])
        last = run_expert([far_side, two_side], later[0])
        near_side_sum, two_sum = join(*later, [F32, F32])
        far_side_sum, two_side_sum = join(*last, [BF16, BF16])
        far_side_in = lax.ppermute(far_side_sum, "grp", plane_swap)
        two_side_in = lax.ppermute(two_side_sum, "ep", side_swap)
        [near_side_sum] = join(near_side_sum, far_side_in, [BF16])
        [two_sum] = join(two_sum, two_side_in, [BF16])
        near_side_in = lax.ppermute(near_side_sum, "ep", side_swap)
        two_in = lax.ppermute(two_sum, both_axes, backward)
        [far_sum] = join(*later, [BF16], 2, [far_side_in])
        far_in = lax.ppermute(far_sum, "grp", plane_swap)
        part = (row_count, columns)

        def by_columns(kernel, first_type, *operands):
            return pl.pallas_call(
                kernel,
                out_shape=(
                    jax.ShapeDtypeStruct(part, first_type),
                    jax.ShapeDtypeStruct(part, BF16),
                ),
                compiler_params=pltpu.CompilerParams(vmem_limit_bytes=16 * 2**20),
                cost_estimate=cost(row_count * model, 2**20),
                name=kernel.__name__,
            )(*operands)

        def crossed(pairs):
            return [(source, (target + ranks) % (2 * ranks)) for source, target in pairs]

        sideways = [(i, i ^ 2) for i in range(2 * ranks)]
        [near_sum] = join(*early, [F32], 2)
        near_mine, near_other = by_columns(
            sum_kernel, BF16, near_sum, far_in, near_side_in, two_in
        )
        own_sum, side_sum = join(*early, [F32, BF16], 0, [near_other])
        base, own_other = by_columns(own_kernel, F32, state, own_sum)
        side_mine, side_other = by_columns(sum_kernel, BF16, side_sum)
        result = base + send(own_other, "grp", plane_swap)
        result = result + send(side_mine, both_axes, sideways)
        result = result + send(side_other, both_axes, crossed(sideways))
        result = result + send(near_mine, both_axes, backward)
        result = result + send(near_other, both_axes, crossed(backward))
        return result.astype(BF16)

    line = [packet]
    for _ in range(1, ring):
        line.append(lax.ppermute(line[-1], "ep", ring_next))
    totals = []
    for part in line:
        sums = run_expert([lax.ppermute(part, "ep", side_swap), part], packet)
        over, here = join(*sums, [BF16, F32])
        totals.append(here + send(over, "ep", side_swap))
    moving = totals[1 % ring]
    for hop in list(range(2, ring)) + [0]:
        moving = totals[hop] + send(moving, "ep", ring_next)

    result = state + lax.dynamic_slice_in_dim(moving, group * columns, columns, 1)
    for by in range(1, groups):
        to = (group + by) % groups
        part = lax.dynamic_slice_in_dim(moving, to * columns, columns, 1)
        result = result + send(part, "grp", turn(by))
    return result.astype(BF16)


def solution(mesh):
    in_specs = (
        P("ep", None),
        P("ep", "grp"),
        P("ep", "grp"),
        P("ep", None),
        P("ep", None),
        P("grp", None, None),
        P("grp", None, None),
        P("grp", None),
        P(),
        P(),
        P("ep", None),
        P("ep", None, "grp"),
        P("ep", None, "grp"),
        P("ep", "grp", None),
        P("ep", None),
        P("ep"),
        P("ep", None, None),
    )
    out_specs = P("ep", "grp")
    return jax.shard_map(local, mesh=mesh, in_specs=in_specs, out_specs=out_specs, check_vma=False)
```

```python
import functools

import jax
import jax.numpy as jnp
from jax import lax
from jax.experimental import pallas as pl
from jax.experimental.pallas import tpu as pltpu
from jax.sharding import PartitionSpec as P

F32 = jnp.float32
BF16 = jnp.bfloat16
HIDDEN = -1e30
VMEM = pltpu.VMEM
ANY = pl.BlockSpec(memory_space=pl.ANY)
WHOLE = pl.BlockSpec(memory_space=pltpu.VMEM)


def dot(a, b):
    return jnp.dot(a, b, preferred_element_type=F32)


def dot_rows(a, b):
    return lax.dot_general(a, b, (((1,), (1,)), ((), ())), preferred_element_type=F32)


def cost(products, moved_bytes):
    return pl.CostEstimate(flops=2 * products, bytes_accessed=moved_bytes, transcendentals=0)


def fetch_all(sources, buffers, sems):
    copies = []
    for at, (source, buffer) in enumerate(zip(sources, buffers)):
        copy = pltpu.make_async_copy(source, buffer, sems.at[at])
        copy.start()
        copies.append(copy)
    return copies


def lay_tokens(keys, start, ref, tokens, width):
    count = ref.shape[0]
    for token in range(tokens):
        keys[start : start + count, :width] = ref[:, token * width : (token + 1) * width]
        start += count
    return start


def pick_kernel(pieces, moves_any, cache_any, out_ref, moves_ref, cache, stacked, sems):
    got = fetch_all((moves_any, cache_any), (moves_ref, cache), sems)
    ranks, per_rank, wide = out_ref.shape
    slots = moves_ref.shape[0]
    resident = cache.shape[0]
    rows = ranks * per_rank
    row = lax.broadcasted_iota(jnp.int32, (rows, ranks), 0)
    rank = lax.broadcasted_iota(jnp.int32, (rows, ranks), 1)
    chosen = jnp.zeros((rows, ranks), jnp.int32)
    got[0].wait()
    for slot in range(slots):
        here = (row // per_rank == rank) & (row % per_rank // pieces == slot)
        chosen = chosen + jnp.where(here, moves_ref[slot : slot + 1, :], 0)
    block = jnp.clip(jnp.sum(chosen, axis=1, keepdims=True), 0, resident - 1)
    at = lax.broadcasted_iota(jnp.int32, (rows, pieces * resident), 0)
    source = lax.broadcasted_iota(jnp.int32, (rows, pieces * resident), 1)
    pick = (source // resident == at % pieces) & (source % resident == block)
    got[1].wait()
    for piece in range(pieces):
        stacked[piece * resident : (piece + 1) * resident, :] = cache[:, piece * wide : (piece + 1) * wide]
    picked = dot(pick.astype(F32).astype(BF16), stacked[...]).astype(BF16)
    out_ref[...] = picked.reshape(ranks, per_rank, wide)


def resident_kernel(
    dims, nope, rope_rows, fresh, cache, absorb, bias_ref,
    query_ref, mixed_ref,
    keys,
):
    head_count, nope_dim, latent, rope, block_size, steps = dims
    width = latent + rope
    rows = nope.shape[0]
    padding = keys.shape[1] - width
    keys[:, latent:] = jnp.zeros((keys.shape[0], keys.shape[1] - latent), BF16)
    start = lay_tokens(keys, 0, cache, block_size, width)
    lay_tokens(keys, start, fresh, steps, width)
    for head in range(head_count):
        q_latent = dot(nope[:, head * nope_dim : (head + 1) * nope_dim], absorb[head])
        q_rope = rope_rows[:, head * rope : (head + 1) * rope]
        fill = jnp.zeros((rows, padding), BF16)
        query_ref[head * rows : (head + 1) * rows, :] = jnp.concatenate(
            [q_latent.astype(BF16), q_rope, fill], axis=1
        )
    scale = (nope_dim + rope) ** (-0.5)
    part = min(4, head_count) * rows
    for first in range(0, head_count * rows, part):
        score = dot_rows(query_ref[first : first + part, :], keys[...])
        score = score.reshape(part // rows, rows, -1) * scale + bias_ref[...][None]
        score = score.reshape(part, -1)
        peak = jnp.max(score, axis=1, keepdims=True)
        weight = jnp.exp(score - peak)
        total = jnp.sum(weight, axis=1, keepdims=True)
        mixed_ref[first : first + part, :latent] = dot(weight.astype(BF16), keys[:, :latent])
        lane = lax.broadcasted_iota(jnp.int32, (part, 128), 1)
        mixed_ref[first : first + part, latent:] = jnp.where(lane < 64, peak, total)


def moved_kernel(
    dims, moved_any, query_any, bias_any, mixed_any, value_any, proj_any,
    share_ref,
    moved, query, bias, mixed, value, proj, keys, heads_out, sems,
):
    head_count, nope_dim, latent, rope, block_size, steps = dims
    width = latent + rope
    rows = heads_out.shape[0]
    got = fetch_all(
        (moved_any, query_any, bias_any, mixed_any, value_any, proj_any),
        (moved, query, bias, mixed, value, proj),
        sems,
    )
    keys[:, latent:] = jnp.zeros((keys.shape[0], keys.shape[1] - latent), BF16)
    scale = (nope_dim + rope) ** (-0.5)
    value_dim = value.shape[2]
    got[0].wait()
    count = moved.shape[0] * moved.shape[1]
    for half in range(2):
        part = moved[:, :, half * width : (half + 1) * width]
        keys[half * count : (half + 1) * count, :width] = part.reshape(count, width)
    got[1].wait()
    got[2].wait()
    group = min(4, head_count)
    for first in range(0, head_count, group):
        at = slice(first * rows, (first + group) * rows)
        score = dot_rows(query[at, :], keys[...])
        score = score.reshape(group, rows, -1) * scale + bias[...][None]
        score = score.reshape(group * rows, -1)
        if first == 0:
            got[3].wait()
        before = mixed[at, latent : latent + 1]
        peak = jnp.maximum(jnp.max(score, axis=1, keepdims=True), before)
        weight = jnp.exp(score - peak)
        keep = jnp.exp(before - peak)
        total = jnp.sum(weight, axis=1, keepdims=True) + mixed[at, latent + 64 : latent + 65] * keep
        joined = dot(weight.astype(BF16), keys[:, :latent]) + mixed[at, :latent] * keep
        joined = (joined / total).astype(BF16)
        if first == 0:
            got[4].wait()
        for head in range(first, first + group):
            own = joined[(head - first) * rows : (head - first + 1) * rows]
            heads_out[:, head * value_dim : (head + 1) * value_dim] = dot(own, value[head]).astype(BF16)
    got[5].wait()
    share_ref[...] = dot(heads_out[...], proj[...]).astype(BF16)


def own_columns(ref, shift):
    groups = lax.axis_size("grp")
    columns = ref.shape[1] // groups
    first = (lax.axis_index("grp") + shift) % groups * columns
    return ref[:, pl.ds(pl.multiple_of(first, 128), columns)]


def norm_kernel(experts, own_any, hidden_any, loaded_any, gain_ref, router_ref, ids_ref, *refs):
    parts, (state_ref, packet_ref, own, hidden, whole, sems) = refs[:-6], refs[-6:]
    got = fetch_all((own_any, hidden_any), (own, hidden), sems)
    rows, model = hidden.shape
    state = parts[0][...].astype(F32)
    for part in parts[1:]:
        state = state + part[...].astype(F32)
    for copy in got:
        copy.wait()
    state = state + own[...].astype(F32) + hidden[...].astype(F32)
    whole[...] = state
    state_ref[...] = own_columns(whole, 0)
    square = jnp.mean(state * state, axis=1, keepdims=True)
    normed = (state * lax.rsqrt(square + 1e-06) * gain_ref[...].astype(F32)).astype(BF16)
    packet_ref[:, :model] = normed
    logits = dot_rows(router_ref[...], normed)
    names = lax.broadcasted_iota(jnp.int32, (experts, rows), 0)
    named = names == ids_ref[0:1, :]
    for k in range(1, ids_ref.shape[0]):
        named = named | (names == ids_ref[k : k + 1, :])
    chosen = jnp.where(named, jax.nn.sigmoid(logits), 0.0)
    weight = chosen / jnp.sum(chosen, axis=0, keepdims=True)
    high = weight.astype(BF16)
    low = (weight - high.astype(F32)).astype(BF16)
    extra = packet_ref.shape[1] - model
    both = jnp.concatenate([high, low], axis=0)
    place = lax.broadcasted_iota(jnp.int32, (2 * experts, extra), 0)
    lane = lax.broadcasted_iota(jnp.int32, (2 * experts, extra), 1)
    turned = lax.dot_general(
        both, (place == lane).astype(BF16), (((0,), (0,)), ((), ())), preferred_element_type=F32
    )
    packet_ref[:, model:] = turned.astype(BF16)


def load_kernel(after_any, gate_any, up_any, down_any, gate_ref, up_ref, down_ref, sems):
    sources, targets = (gate_any, up_any, down_any), (gate_ref, up_ref, down_ref)
    for copy in fetch_all(sources, targets, sems):
        copy.wait()


def pack_kernel(after_count, *refs):
    rows_refs, out_ref = refs[after_count:-1], refs[-1]
    count = rows_refs[0].shape[0]
    for at, ref in enumerate(rows_refs):
        out_ref[at * count : (at + 1) * count, :] = ref[...]


def expert_kernel(experts, here_ref, across_ref, gate_ref, up_ref, down_ref, near_ref, far_ref):
    model = gate_ref.shape[1]
    packet = jnp.concatenate([here_ref[...], across_ref[...]], axis=0)
    rows = packet[:, :model]
    extra = packet[:, model:].astype(F32)
    names = lax.broadcasted_iota(jnp.int32, extra.shape, 1)
    me = lax.axis_index("ep")
    mine = (names == me) | (names == me + experts)
    weight = jnp.sum(jnp.where(mine, extra, 0.0), axis=1, keepdims=True)
    gate = dot_rows(rows, gate_ref[...])
    up = dot_rows(rows, up_ref[...])
    inner = (gate * jax.nn.sigmoid(gate) * up * weight).astype(BF16)
    result = dot(inner, down_ref[...]).astype(BF16)
    half = near_ref.shape[0]
    near_ref[...] = result[:half]
    far_ref[...] = result[half:]


def join_kernel(first, after_count, near_ref, back_ref, *refs):
    out_refs = refs[after_count:]
    count = out_refs[0].shape[0]
    for at, ref in enumerate(out_refs, first):
        rows = slice(at * count, (at + 1) * count)
        ref[...] = (near_ref[rows, :].astype(F32) + back_ref[rows, :].astype(F32)).astype(ref.dtype)


def own_kernel(state_ref, own_ref, side_ref, base_ref, other_ref):
    mine, other = (own_columns(own_ref, by) + own_columns(side_ref, by).astype(F32) for by in (0, 1))
    base_ref[...] = state_ref[...] + mine
    other_ref[...] = other.astype(BF16)


def sum_kernel(*refs):
    parts, (mine_ref, other_ref) = refs[:-2], refs[-2:]
    for shift, ref in ((0, mine_ref), (1, other_ref)):
        total = own_columns(parts[0], shift).astype(F32)
        for part in parts[1:]:
            total = total + own_columns(part, shift).astype(F32)
        ref[...] = total.astype(BF16)


def local(
    hidden_in,
    query_nope,
    query_rope,
    new_latent,
    latent_cache,
    key_absorb,
    value_absorb,
    output_proj,
    norm_gain,
    router_proj,
    expert_ids,
    expert_gate,
    expert_up,
    expert_down,
    block_table,
    lengths,
    subtree_moves,
):
    head_count, nope_dim, latent = key_absorb.shape
    rope = query_rope.shape[1] // head_count
    width = latent + rope
    requests, table_len = block_table.shape
    steps = new_latent.shape[1] // width
    row_count, model = hidden_in.shape
    block_size = latent_cache.shape[1] // width
    resident = latent_cache.shape[0]
    experts = router_proj.shape[1]
    groups = lax.axis_size("grp")
    group = lax.axis_index("grp")
    ranks = lax.axis_size("ep")
    me = lax.axis_index("ep")
    ring = ranks // 4
    core_swap = [(i, i ^ 1) for i in range(ranks)]
    side_swap = [(i, i ^ 2) for i in range(ranks)]
    ring_next = [(i, (i + 4) % ranks) for i in range(ranks)]
    both_axes = ("grp", "ep")

    def turn(by):
        return [(g, (g + by) % groups) for g in range(groups)]

    slots = subtree_moves.shape[2]
    pieces = block_size // 2
    outgoing = pl.pallas_call(
        functools.partial(pick_kernel, pieces),
        out_shape=jax.ShapeDtypeStruct((ranks, slots * pieces, 2 * width), BF16),
        in_specs=[ANY] * 2,
        scratch_shapes=[
            VMEM((slots, ranks), jnp.int32),
            VMEM(latent_cache.shape, BF16),
            VMEM((pieces * resident, 2 * width), BF16),
            pltpu.SemaphoreType.DMA((2,)),
        ],
        compiler_params=pltpu.CompilerParams(vmem_limit_bytes=60 * 2**20),
        cost_estimate=cost(0, 4 * 2**20),
        name="pick",
    )(subtree_moves[0].T, latent_cache)
    arrived = lax.all_to_all(outgoing, "ep", split_axis=0, concat_axis=0, tiled=True)

    place = jnp.arange(table_len, dtype=jnp.int32)
    usable = jnp.clip(lengths[:, None] - place[None, :] * block_size, 0, block_size)
    blocks = jnp.arange(resident + ranks * slots, dtype=jnp.int32)
    limit = jnp.sum(
        jnp.where(block_table[:, :, None] == blocks[None, None, :], usable[:, :, None], 0), axis=1
    )
    token = jnp.arange(block_size, dtype=jnp.int32)
    row = jnp.arange(row_count, dtype=jnp.int32)
    fresh = jnp.arange(steps * requests, dtype=jnp.int32)
    fresh_open = ((row // steps)[:, None] == (fresh % requests)[None, :]) & (
        (fresh // requests)[None, :] <= (row % steps)[:, None]
    )
    near_open = (limit[:, None, :resident] > token[None, :, None]).reshape(requests, -1)
    near_open = jnp.concatenate([jnp.repeat(near_open, steps, axis=0), fresh_open], axis=1)
    near_bias = jnp.where(near_open, 0.0, HIDDEN).astype(F32)
    by_key = jnp.repeat(limit[:, resident:], pieces, axis=1)
    at_token = 2 * (jnp.arange(ranks * slots * pieces, dtype=jnp.int32) % pieces)
    moved_open = jnp.concatenate([by_key > at_token[None], by_key > at_token[None] + 1], axis=1)
    moved_bias = jnp.repeat(jnp.where(moved_open, 0.0, HIDDEN).astype(F32), steps, axis=0)

    padded = -(-width // 128) * 128
    query_rows = head_count * row_count
    dims = (head_count, nope_dim, latent, rope, block_size, steps)
    query, mixed = pl.pallas_call(
        functools.partial(resident_kernel, dims),
        out_shape=(
            jax.ShapeDtypeStruct((query_rows, padded), BF16),
            jax.ShapeDtypeStruct((query_rows, latent + 128), F32),
        ),
        scratch_shapes=[VMEM((near_bias.shape[1], padded), BF16)],
        compiler_params=pltpu.CompilerParams(vmem_limit_bytes=16 * 2**20),
        cost_estimate=cost(query_rows * near_bias.shape[1] * (padded + latent), 8 * 2**20),
        name="attend_resident",
    )(query_nope, query_rope, new_latent, latent_cache, key_absorb, near_bias)
    share = pl.pallas_call(
        functools.partial(moved_kernel, dims),
        out_shape=jax.ShapeDtypeStruct((row_count, model), BF16),
        in_specs=[ANY] * 6,
        scratch_shapes=[
            VMEM(arrived.shape, BF16),
            VMEM(query.shape, BF16),
            VMEM(moved_bias.shape, F32),
            VMEM(mixed.shape, F32),
            VMEM(value_absorb.shape, BF16),
            VMEM(output_proj.shape, BF16),
            VMEM((moved_bias.shape[1], padded), BF16),
            VMEM((row_count, head_count * value_absorb.shape[2]), BF16),
            pltpu.SemaphoreType.DMA((6,)),
        ],
        compiler_params=pltpu.CompilerParams(vmem_limit_bytes=60 * 2**20),
        cost_estimate=cost(query_rows * moved_bias.shape[1] * (padded + latent), 10 * 2**20),
        name="attend_moved",
    )(arrived, query, moved_bias, mixed, value_absorb, output_proj)
    shares = [lax.ppermute(share, "grp", turn(by)) for by in range(1, groups)]

    held = [jnp.swapaxes(expert_gate[0], 0, 1), jnp.swapaxes(expert_up[0], 0, 1), expert_down[0]]
    gate_rows, up_rows, down_rows = pl.pallas_call(
        load_kernel,
        out_shape=[jax.ShapeDtypeStruct(array.shape, BF16) for array in held],
        in_specs=[ANY] * 4,
        out_specs=[WHOLE] * 3,
        scratch_shapes=[pltpu.SemaphoreType.DMA((3,))],
        compiler_params=pltpu.CompilerParams(vmem_limit_bytes=44 * 2**20),
        cost_estimate=cost(0, 12 * 2**20),
        name="load",
    )(share, *held)

    extra = -(-2 * experts // 128) * 128
    columns = model // groups
    state, packet = pl.pallas_call(
        functools.partial(norm_kernel, experts),
        out_shape=(
            jax.ShapeDtypeStruct((row_count, columns), F32),
            jax.ShapeDtypeStruct((row_count, model + extra), BF16),
        ),
        in_specs=[ANY] * 3 + [WHOLE] * (2 + groups),
        scratch_shapes=[
            VMEM((row_count, model), BF16),
            VMEM((row_count, model), BF16),
            VMEM((row_count, model), F32),
            pltpu.SemaphoreType.DMA((2,)),
        ],
        compiler_params=pltpu.CompilerParams(vmem_limit_bytes=16 * 2**20),
        cost_estimate=cost(row_count * model * 128, 4 * 2**20),
        name="norm",
    )(share, hidden_in, down_rows, norm_gain[None, :], router_proj.T, expert_ids.T, *shares)

    def run_expert(rows, *after):
        half = len(rows) * row_count
        out = jax.ShapeDtypeStruct((half, model), BF16)
        here = pl.pallas_call(
            functools.partial(pack_kernel, len(after)),
            out_shape=jax.ShapeDtypeStruct((half, model + extra), BF16),
            in_specs=[ANY] * len(after) + [WHOLE] * len(rows),
            compiler_params=pltpu.CompilerParams(vmem_limit_bytes=16 * 2**20),
            cost_estimate=cost(0, 2 * half * model * 2),
            name="pack",
        )(*after, *rows)
        across = lax.ppermute(here, "ep", core_swap)
        near, far = pl.pallas_call(
            functools.partial(expert_kernel, experts),
            out_shape=(out, out),
            in_specs=[WHOLE] * 5,
            compiler_params=pltpu.CompilerParams(vmem_limit_bytes=24 * 2**20),
            cost_estimate=cost(6 * half * model * gate_rows.shape[0], 12 * 2**20),
            name="expert",
        )(here, across, gate_rows, up_rows, down_rows)
        return near, lax.ppermute(far, "ep", core_swap)

    def join(near, back, types, first=0, after=()):
        return pl.pallas_call(
            functools.partial(join_kernel, first, len(after)),
            out_shape=[jax.ShapeDtypeStruct((row_count, model), kind) for kind in types],
            in_specs=[WHOLE] * 2 + [ANY] * len(after),
            compiler_params=pltpu.CompilerParams(vmem_limit_bytes=16 * 2**20),
            cost_estimate=cost(row_count * model, 2**20),
            name="join",
        )(near, back, *after)

    def send(value, axes, pairs):
        return lax.ppermute(value.astype(BF16), axes, pairs).astype(F32)

    if ring == 4 and groups == 2:
        def ring_step(sign):
            return [
                (g * ranks + i, g * ranks + (i + sign * 4 * (1 - 2 * g)) % ranks)
                for g in range(2)
                for i in range(ranks)
            ]

        onward, backward, plane_swap = ring_step(1), ring_step(-1), [(0, 1), (1, 0)]
        near = lax.ppermute(packet, both_axes, onward)
        side = lax.ppermute(packet, "ep", side_swap)
        two = lax.ppermute(near, both_axes, onward)
        near_side = lax.ppermute(near, "ep", side_swap)
        far = lax.ppermute(near, "grp", plane_swap)
        two_side = lax.ppermute(two, "ep", side_swap)
        far_side = lax.ppermute(near_side, "grp", plane_swap)
        early = run_expert([packet, side, near], packet)
        later = run_expert([far, near_side, two], early[0])
        own_sum, side_sum, near_sum = join(*early, [F32, BF16, F32])
        side_in = lax.ppermute(side_sum, "ep", side_swap)
        last = run_expert([far_side, two_side], later[0], side_in)
        near_side_sum, two_sum = join(*later, [F32, F32], 1)
        far_side_sum, two_side_sum = join(*last, [BF16, BF16])
        far_side_in = lax.ppermute(far_side_sum, "grp", plane_swap)
        two_side_in = lax.ppermute(two_side_sum, "ep", side_swap)
        [near_side_sum] = join(near_side_sum, far_side_in, [BF16])
        [two_sum] = join(two_sum, two_side_in, [BF16])
        near_side_in = lax.ppermute(near_side_sum, "ep", side_swap)
        two_in = lax.ppermute(two_sum, both_axes, backward)
        [far_sum] = join(*later, [BF16], 0, [far_side_in])
        far_in = lax.ppermute(far_sum, "grp", plane_swap)
        part = (row_count, columns)

        def by_columns(kernel, first_type, *operands):
            return pl.pallas_call(
                kernel,
                out_shape=(
                    jax.ShapeDtypeStruct(part, first_type),
                    jax.ShapeDtypeStruct(part, BF16),
                ),
                compiler_params=pltpu.CompilerParams(vmem_limit_bytes=16 * 2**20),
                cost_estimate=cost(row_count * model, 2**20),
                name=kernel.__name__,
            )(*operands)

        def crossed(pairs):
            return [(source, (target + ranks) % (2 * ranks)) for source, target in pairs]

        base, own_other = by_columns(own_kernel, F32, state, own_sum, side_in)
        near_mine, near_other = by_columns(
            sum_kernel, BF16, near_sum, far_in, near_side_in, two_in
        )
        result = base + send(own_other, "grp", plane_swap)
        result = result + send(near_mine, both_axes, backward)
        result = result + send(near_other, both_axes, crossed(backward))
        return result.astype(BF16)

    line = [packet]
    for _ in range(1, ring):
        line.append(lax.ppermute(line[-1], "ep", ring_next))
    totals = []
    for part in line:
        sums = run_expert([lax.ppermute(part, "ep", side_swap), part], packet)
        over, here = join(*sums, [BF16, F32])
        totals.append(here + send(over, "ep", side_swap))
    moving = totals[1 % ring]
    for hop in list(range(2, ring)) + [0]:
        moving = totals[hop] + send(moving, "ep", ring_next)

    result = state + lax.dynamic_slice_in_dim(moving, group * columns, columns, 1)
    for by in range(1, groups):
        to = (group + by) % groups
        part = lax.dynamic_slice_in_dim(moving, to * columns, columns, 1)
        result = result + send(part, "grp", turn(by))
    return result.astype(BF16)


def solution(mesh):
    in_specs = (
        P("ep", None),
        P("ep", "grp"),
        P("ep", "grp"),
        P("ep", None),
        P("ep", None),
        P("grp", None, None),
        P("grp", None, None),
        P("grp", None),
        P(),
        P(),
        P("ep", None),
        P("ep", None, "grp"),
        P("ep", None, "grp"),
        P("ep", "grp", None),
        P("ep", None),
        P("ep"),
        P("ep", None, None),
    )
    out_specs = P("ep", "grp")
    return jax.shard_map(local, mesh=mesh, in_specs=in_specs, out_specs=out_specs, check_vma=False)
```

```python
import functools

import jax
import jax.numpy as jnp
from jax import lax
from jax.experimental import pallas as pl
from jax.experimental.pallas import tpu as pltpu
from jax.sharding import PartitionSpec as P

F32 = jnp.float32
BF16 = jnp.bfloat16
HIDDEN = -1e30
VMEM = pltpu.VMEM
ANY = pl.BlockSpec(memory_space=pl.ANY)
WHOLE = pl.BlockSpec(memory_space=pltpu.VMEM)


def dot(a, b):
    return jnp.dot(a, b, preferred_element_type=F32)


def dot_rows(a, b):
    return lax.dot_general(a, b, (((1,), (1,)), ((), ())), preferred_element_type=F32)


def cost(products, moved_bytes):
    return pl.CostEstimate(flops=2 * products, bytes_accessed=moved_bytes, transcendentals=0)


def fetch_all(sources, buffers, sems):
    copies = []
    for at, (source, buffer) in enumerate(zip(sources, buffers)):
        copy = pltpu.make_async_copy(source, buffer, sems.at[at])
        copy.start()
        copies.append(copy)
    return copies


def lay_tokens(keys, start, ref, tokens, width):
    count = ref.shape[0]
    for token in range(tokens):
        keys[start : start + count, :width] = ref[:, token * width : (token + 1) * width]
        start += count
    return start


def pick_kernel(pieces, moves_any, cache_any, out_ref, moves_ref, cache, stacked, sems):
    got = fetch_all((moves_any, cache_any), (moves_ref, cache), sems)
    ranks, per_rank, wide = out_ref.shape
    slots = moves_ref.shape[0]
    resident = cache.shape[0]
    rows = ranks * per_rank
    row = lax.broadcasted_iota(jnp.int32, (rows, ranks), 0)
    rank = lax.broadcasted_iota(jnp.int32, (rows, ranks), 1)
    chosen = jnp.zeros((rows, ranks), jnp.int32)
    got[0].wait()
    for slot in range(slots):
        here = (row // per_rank == rank) & (row % per_rank // pieces == slot)
        chosen = chosen + jnp.where(here, moves_ref[slot : slot + 1, :], 0)
    block = jnp.clip(jnp.sum(chosen, axis=1, keepdims=True), 0, resident - 1)
    at = lax.broadcasted_iota(jnp.int32, (rows, pieces * resident), 0)
    source = lax.broadcasted_iota(jnp.int32, (rows, pieces * resident), 1)
    pick = (source // resident == at % pieces) & (source % resident == block)
    got[1].wait()
    for piece in range(pieces):
        stacked[piece * resident : (piece + 1) * resident, :] = cache[:, piece * wide : (piece + 1) * wide]
    picked = dot(pick.astype(F32).astype(BF16), stacked[...]).astype(BF16)
    out_ref[...] = picked.reshape(ranks, per_rank, wide)


def resident_kernel(
    dims, nope, rope_rows, fresh, cache, absorb, bias_ref,
    query_ref, mixed_ref,
    keys,
):
    head_count, nope_dim, latent, rope, block_size, steps = dims
    width = latent + rope
    rows = nope.shape[0]
    padding = keys.shape[1] - width
    keys[:, latent:] = jnp.zeros((keys.shape[0], keys.shape[1] - latent), BF16)
    start = lay_tokens(keys, 0, cache, block_size, width)
    lay_tokens(keys, start, fresh, steps, width)
    for head in range(head_count):
        q_latent = dot(nope[:, head * nope_dim : (head + 1) * nope_dim], absorb[head])
        q_rope = rope_rows[:, head * rope : (head + 1) * rope]
        fill = jnp.zeros((rows, padding), BF16)
        query_ref[head * rows : (head + 1) * rows, :] = jnp.concatenate(
            [q_latent.astype(BF16), q_rope, fill], axis=1
        )
    scale = (nope_dim + rope) ** (-0.5)
    part = min(4, head_count) * rows
    for first in range(0, head_count * rows, part):
        score = dot_rows(query_ref[first : first + part, :], keys[...])
        score = score.reshape(part // rows, rows, -1) * scale + bias_ref[...][None]
        score = score.reshape(part, -1)
        peak = jnp.max(score, axis=1, keepdims=True)
        weight = jnp.exp(score - peak)
        total = jnp.sum(weight, axis=1, keepdims=True)
        mixed_ref[first : first + part, :latent] = dot(weight.astype(BF16), keys[:, :latent])
        lane = lax.broadcasted_iota(jnp.int32, (part, 128), 1)
        mixed_ref[first : first + part, latent:] = jnp.where(lane < 64, peak, total)


def moved_kernel(
    dims, moved_any, query_any, bias_any, mixed_any, value_any, proj_any,
    share_ref,
    moved, query, bias, mixed, value, proj, keys, heads_out, sems,
):
    head_count, nope_dim, latent, rope, block_size, steps = dims
    width = latent + rope
    rows = heads_out.shape[0]
    got = fetch_all(
        (moved_any, query_any, bias_any, mixed_any, value_any, proj_any),
        (moved, query, bias, mixed, value, proj),
        sems,
    )
    keys[:, latent:] = jnp.zeros((keys.shape[0], keys.shape[1] - latent), BF16)
    scale = (nope_dim + rope) ** (-0.5)
    value_dim = value.shape[2]
    got[0].wait()
    count = moved.shape[0] * moved.shape[1]
    for half in range(2):
        part = moved[:, :, half * width : (half + 1) * width]
        keys[half * count : (half + 1) * count, :width] = part.reshape(count, width)
    got[1].wait()
    got[2].wait()
    group = min(4, head_count)
    for first in range(0, head_count, group):
        at = slice(first * rows, (first + group) * rows)
        score = dot_rows(query[at, :], keys[...])
        score = score.reshape(group, rows, -1) * scale + bias[...][None]
        score = score.reshape(group * rows, -1)
        if first == 0:
            got[3].wait()
        before = mixed[at, latent : latent + 1]
        peak = jnp.maximum(jnp.max(score, axis=1, keepdims=True), before)
        weight = jnp.exp(score - peak)
        keep = jnp.exp(before - peak)
        total = jnp.sum(weight, axis=1, keepdims=True) + mixed[at, latent + 64 : latent + 65] * keep
        joined = dot(weight.astype(BF16), keys[:, :latent]) + mixed[at, :latent] * keep
        joined = (joined / total).astype(BF16)
        if first == 0:
            got[4].wait()
        for head in range(first, first + group):
            own = joined[(head - first) * rows : (head - first + 1) * rows]
            heads_out[:, head * value_dim : (head + 1) * value_dim] = dot(own, value[head]).astype(BF16)
    got[5].wait()
    share_ref[...] = dot(heads_out[...], proj[...]).astype(BF16)


def own_columns(ref, shift):
    groups = lax.axis_size("grp")
    columns = ref.shape[1] // groups
    first = (lax.axis_index("grp") + shift) % groups * columns
    return ref[:, pl.ds(pl.multiple_of(first, 128), columns)]


def norm_kernel(experts, own_any, hidden_any, loaded_any, gain_ref, router_ref, ids_ref, *refs):
    parts, (state_ref, packet_ref, own, hidden, whole, sems) = refs[:-6], refs[-6:]
    got = fetch_all((own_any, hidden_any), (own, hidden), sems)
    rows, model = hidden.shape
    state = parts[0][...].astype(F32)
    for part in parts[1:]:
        state = state + part[...].astype(F32)
    for copy in got:
        copy.wait()
    state = state + own[...].astype(F32) + hidden[...].astype(F32)
    whole[...] = state
    state_ref[...] = own_columns(whole, 0)
    square = jnp.mean(state * state, axis=1, keepdims=True)
    normed = (state * lax.rsqrt(square + 1e-06) * gain_ref[...].astype(F32)).astype(BF16)
    packet_ref[:, :model] = normed
    logits = dot_rows(router_ref[...], normed)
    names = lax.broadcasted_iota(jnp.int32, (experts, rows), 0)
    named = names == ids_ref[0:1, :]
    for k in range(1, ids_ref.shape[0]):
        named = named | (names == ids_ref[k : k + 1, :])
    chosen = jnp.where(named, jax.nn.sigmoid(logits), 0.0)
    weight = chosen / jnp.sum(chosen, axis=0, keepdims=True)
    high = weight.astype(BF16)
    low = (weight - high.astype(F32)).astype(BF16)
    extra = packet_ref.shape[1] - model
    both = jnp.concatenate([high, low], axis=0)
    place = lax.broadcasted_iota(jnp.int32, (2 * experts, extra), 0)
    lane = lax.broadcasted_iota(jnp.int32, (2 * experts, extra), 1)
    turned = lax.dot_general(
        both, (place == lane).astype(BF16), (((0,), (0,)), ((), ())), preferred_element_type=F32
    )
    packet_ref[:, model:] = turned.astype(BF16)


def load_kernel(after_any, gate_any, up_any, down_any, gate_ref, up_ref, down_ref, sems):
    sources, targets = (gate_any, up_any, down_any), (gate_ref, up_ref, down_ref)
    for copy in fetch_all(sources, targets, sems):
        copy.wait()


def pack_kernel(after_any, *refs):
    rows_refs, out_ref = refs[:-1], refs[-1]
    count = rows_refs[0].shape[0]
    for at, ref in enumerate(rows_refs):
        out_ref[at * count : (at + 1) * count, :] = ref[...]


def expert_kernel(experts, after_any, here_ref, across_ref, gate_ref, up_ref, down_ref, near_ref, *far_refs):
    model = gate_ref.shape[1]
    packet = jnp.concatenate([here_ref[...], across_ref[...]], axis=0)
    rows = packet[:, :model]
    extra = packet[:, model:].astype(F32)
    names = lax.broadcasted_iota(jnp.int32, extra.shape, 1)
    me = lax.axis_index("ep")
    mine = (names == me) | (names == me + experts)
    weight = jnp.sum(jnp.where(mine, extra, 0.0), axis=1, keepdims=True)
    gate = dot_rows(rows, gate_ref[...])
    up = dot_rows(rows, up_ref[...])
    inner = (gate * jax.nn.sigmoid(gate) * up * weight).astype(BF16)
    result = dot(inner, down_ref[...]).astype(BF16)
    half = near_ref.shape[0]
    near_ref[...] = result[:half]
    count = half // len(far_refs)
    for at, far_ref in enumerate(far_refs):
        far_ref[...] = result[half + at * count : half + (at + 1) * count]


def join_kernel(first, back_count, after_count, near_ref, *refs):
    back_refs, out_refs = refs[after_count : after_count + back_count], refs[after_count + back_count :]
    count = out_refs[0].shape[0]
    height = back_refs[0].shape[0]
    step = min(count, height)
    for at, ref in enumerate(out_refs, first):
        for row in range(at * count, (at + 1) * count, step):
            back = back_refs[row // height][row % height : row % height + step, :].astype(F32)
            total = near_ref[row : row + step, :].astype(F32) + back
            ref[row - at * count : row - at * count + step, :] = total.astype(ref.dtype)


def own_kernel(state_ref, own_ref, side_ref, base_ref, other_ref):
    mine, other = (own_columns(own_ref, by) + own_columns(side_ref, by).astype(F32) for by in (0, 1))
    base_ref[...] = state_ref[...] + mine
    other_ref[...] = other.astype(BF16)


def sum_kernel(*refs):
    parts, (mine_ref, other_ref) = refs[:-2], refs[-2:]
    for shift, ref in ((0, mine_ref), (1, other_ref)):
        total = own_columns(parts[0], shift).astype(F32)
        for part in parts[1:]:
            total = total + own_columns(part, shift).astype(F32)
        ref[...] = total.astype(BF16)


def local(
    hidden_in,
    query_nope,
    query_rope,
    new_latent,
    latent_cache,
    key_absorb,
    value_absorb,
    output_proj,
    norm_gain,
    router_proj,
    expert_ids,
    expert_gate,
    expert_up,
    expert_down,
    block_table,
    lengths,
    subtree_moves,
):
    head_count, nope_dim, latent = key_absorb.shape
    rope = query_rope.shape[1] // head_count
    width = latent + rope
    requests, table_len = block_table.shape
    steps = new_latent.shape[1] // width
    row_count, model = hidden_in.shape
    block_size = latent_cache.shape[1] // width
    resident = latent_cache.shape[0]
    experts = router_proj.shape[1]
    groups = lax.axis_size("grp")
    group = lax.axis_index("grp")
    ranks = lax.axis_size("ep")
    me = lax.axis_index("ep")
    ring = ranks // 4
    core_swap = [(i, i ^ 1) for i in range(ranks)]
    side_swap = [(i, i ^ 2) for i in range(ranks)]
    ring_next = [(i, (i + 4) % ranks) for i in range(ranks)]
    both_axes = ("grp", "ep")

    def turn(by):
        return [(g, (g + by) % groups) for g in range(groups)]

    slots = subtree_moves.shape[2]
    pieces = block_size // 2
    outgoing = pl.pallas_call(
        functools.partial(pick_kernel, pieces),
        out_shape=jax.ShapeDtypeStruct((ranks, slots * pieces, 2 * width), BF16),
        in_specs=[ANY] * 2,
        scratch_shapes=[
            VMEM((slots, ranks), jnp.int32),
            VMEM(latent_cache.shape, BF16),
            VMEM((pieces * resident, 2 * width), BF16),
            pltpu.SemaphoreType.DMA((2,)),
        ],
        compiler_params=pltpu.CompilerParams(vmem_limit_bytes=60 * 2**20),
        cost_estimate=cost(0, 4 * 2**20),
        name="pick",
    )(subtree_moves[0].T, latent_cache)
    arrived = lax.all_to_all(outgoing, "ep", split_axis=0, concat_axis=0, tiled=True)

    place = jnp.arange(table_len, dtype=jnp.int32)
    usable = jnp.clip(lengths[:, None] - place[None, :] * block_size, 0, block_size)
    blocks = jnp.arange(resident + ranks * slots, dtype=jnp.int32)
    limit = jnp.sum(
        jnp.where(block_table[:, :, None] == blocks[None, None, :], usable[:, :, None], 0), axis=1
    )
    token = jnp.arange(block_size, dtype=jnp.int32)
    row = jnp.arange(row_count, dtype=jnp.int32)
    fresh = jnp.arange(steps * requests, dtype=jnp.int32)
    fresh_open = ((row // steps)[:, None] == (fresh % requests)[None, :]) & (
        (fresh // requests)[None, :] <= (row % steps)[:, None]
    )
    near_open = (limit[:, None, :resident] > token[None, :, None]).reshape(requests, -1)
    near_open = jnp.concatenate([jnp.repeat(near_open, steps, axis=0), fresh_open], axis=1)
    near_bias = jnp.where(near_open, 0.0, HIDDEN).astype(F32)
    by_key = jnp.repeat(limit[:, resident:], pieces, axis=1)
    at_token = 2 * (jnp.arange(ranks * slots * pieces, dtype=jnp.int32) % pieces)
    moved_open = jnp.concatenate([by_key > at_token[None], by_key > at_token[None] + 1], axis=1)
    moved_bias = jnp.repeat(jnp.where(moved_open, 0.0, HIDDEN).astype(F32), steps, axis=0)

    padded = -(-width // 128) * 128
    query_rows = head_count * row_count
    dims = (head_count, nope_dim, latent, rope, block_size, steps)
    query, mixed = pl.pallas_call(
        functools.partial(resident_kernel, dims),
        out_shape=(
            jax.ShapeDtypeStruct((query_rows, padded), BF16),
            jax.ShapeDtypeStruct((query_rows, latent + 128), F32),
        ),
        scratch_shapes=[VMEM((near_bias.shape[1], padded), BF16)],
        compiler_params=pltpu.CompilerParams(vmem_limit_bytes=16 * 2**20),
        cost_estimate=cost(query_rows * near_bias.shape[1] * (padded + latent), 8 * 2**20),
        name="attend_resident",
    )(query_nope, query_rope, new_latent, latent_cache, key_absorb, near_bias)
    share = pl.pallas_call(
        functools.partial(moved_kernel, dims),
        out_shape=jax.ShapeDtypeStruct((row_count, model), BF16),
        in_specs=[ANY] * 6,
        scratch_shapes=[
            VMEM(arrived.shape, BF16),
            VMEM(query.shape, BF16),
            VMEM(moved_bias.shape, F32),
            VMEM(mixed.shape, F32),
            VMEM(value_absorb.shape, BF16),
            VMEM(output_proj.shape, BF16),
            VMEM((moved_bias.shape[1], padded), BF16),
            VMEM((row_count, head_count * value_absorb.shape[2]), BF16),
            pltpu.SemaphoreType.DMA((6,)),
        ],
        compiler_params=pltpu.CompilerParams(vmem_limit_bytes=60 * 2**20),
        cost_estimate=cost(query_rows * moved_bias.shape[1] * (padded + latent), 10 * 2**20),
        name="attend_moved",
    )(arrived, query, moved_bias, mixed, value_absorb, output_proj)
    shares = [lax.ppermute(share, "grp", turn(by)) for by in range(1, groups)]

    held = [jnp.swapaxes(expert_gate[0], 0, 1), jnp.swapaxes(expert_up[0], 0, 1), expert_down[0]]
    gate_rows, up_rows, down_rows = pl.pallas_call(
        load_kernel,
        out_shape=[jax.ShapeDtypeStruct(array.shape, BF16) for array in held],
        in_specs=[ANY] * 4,
        out_specs=[WHOLE] * 3,
        scratch_shapes=[pltpu.SemaphoreType.DMA((3,))],
        compiler_params=pltpu.CompilerParams(vmem_limit_bytes=44 * 2**20),
        cost_estimate=cost(0, 12 * 2**20),
        name="load",
    )(share, *held)

    extra = -(-2 * experts // 128) * 128
    columns = model // groups
    state, packet = pl.pallas_call(
        functools.partial(norm_kernel, experts),
        out_shape=(
            jax.ShapeDtypeStruct((row_count, columns), F32),
            jax.ShapeDtypeStruct((row_count, model + extra), BF16),
        ),
        in_specs=[ANY] * 3 + [WHOLE] * (2 + groups),
        scratch_shapes=[
            VMEM((row_count, model), BF16),
            VMEM((row_count, model), BF16),
            VMEM((row_count, model), F32),
            pltpu.SemaphoreType.DMA((2,)),
        ],
        compiler_params=pltpu.CompilerParams(vmem_limit_bytes=16 * 2**20),
        cost_estimate=cost(row_count * model * 128, 4 * 2**20),
        name="norm",
    )(share, hidden_in, down_rows, norm_gain[None, :], router_proj.T, expert_ids.T, *shares)

    def run_expert(rows, after, run_after, pieces=1):
        half = len(rows) * row_count
        out = [jax.ShapeDtypeStruct((half // cuts, model), BF16) for cuts in [1] + [pieces] * pieces]
        here = pl.pallas_call(
            pack_kernel,
            out_shape=jax.ShapeDtypeStruct((half, model + extra), BF16),
            in_specs=[ANY] + [WHOLE] * len(rows),
            compiler_params=pltpu.CompilerParams(vmem_limit_bytes=16 * 2**20),
            cost_estimate=cost(0, 2 * half * model * 2),
            name="pack",
        )(after, *rows)
        across = lax.ppermute(here, "ep", core_swap)
        near, *far = pl.pallas_call(
            functools.partial(expert_kernel, experts),
            out_shape=out,
            in_specs=[ANY] + [WHOLE] * 5,
            compiler_params=pltpu.CompilerParams(vmem_limit_bytes=24 * 2**20),
            cost_estimate=cost(6 * half * model * gate_rows.shape[0], 12 * 2**20),
            name="expert",
        )(run_after, here, across, gate_rows, up_rows, down_rows)
        return near, [lax.ppermute(part, "ep", core_swap) for part in far]

    def join(near, back, types, first=0, after=()):
        return pl.pallas_call(
            functools.partial(join_kernel, first, len(back), len(after)),
            out_shape=[jax.ShapeDtypeStruct((row_count, model), kind) for kind in types],
            in_specs=[WHOLE] + [ANY] * len(after) + [WHOLE] * len(back),
            compiler_params=pltpu.CompilerParams(vmem_limit_bytes=16 * 2**20),
            cost_estimate=cost(row_count * model, 2**20),
            name="join",
        )(near, *after, *back)

    def send(value, axes, pairs):
        return lax.ppermute(value.astype(BF16), axes, pairs).astype(F32)

    if ring == 4 and groups == 2:
        def ring_step(sign):
            return [
                (g * ranks + i, g * ranks + (i + sign * 4 * (1 - 2 * g)) % ranks)
                for g in range(2)
                for i in range(ranks)
            ]

        onward, backward, plane_swap = ring_step(1), ring_step(-1), [(0, 1), (1, 0)]
        near = lax.ppermute(packet, both_axes, onward)
        side = lax.ppermute(packet, "ep", side_swap)
        two = lax.ppermute(near, both_axes, onward)
        near_side = lax.ppermute(near, "ep", side_swap)
        far = lax.ppermute(near, "grp", plane_swap)
        two_side = lax.ppermute(two, "ep", side_swap)
        far_side = lax.ppermute(near_side, "grp", plane_swap)
        early = run_expert([packet, side, near], packet, packet)
        later = run_expert([far, near_side, two], early[0], packet)
        own_sum, side_sum, near_sum = join(*early, [F32, BF16, F32])
        side_in = lax.ppermute(side_sum, "ep", side_swap)
        far_sum, near_side_sum, two_sum = join(*later, [BF16, F32, F32])
        far_in = lax.ppermute(far_sum, "grp", plane_swap)
        last = run_expert([far_side, two_side], later[0], far_sum, 4)
        far_side_sum, two_side_sum = join(*last, [BF16, BF16], 0, [side_in, far_in])
        far_side_in = lax.ppermute(far_side_sum, "grp", plane_swap)
        two_side_in = lax.ppermute(two_side_sum, "ep", side_swap)
        [near_side_sum] = join(near_side_sum, [far_side_in], [BF16])
        [two_sum] = join(two_sum, [two_side_in], [BF16])
        near_side_in = lax.ppermute(near_side_sum, "ep", side_swap)
        two_in = lax.ppermute(two_sum, both_axes, backward)
        part = (row_count, columns)

        def by_columns(kernel, first_type, *operands):
            return pl.pallas_call(
                kernel,
                out_shape=(
                    jax.ShapeDtypeStruct(part, first_type),
                    jax.ShapeDtypeStruct(part, BF16),
                ),
                compiler_params=pltpu.CompilerParams(vmem_limit_bytes=16 * 2**20),
                cost_estimate=cost(row_count * model, 2**20),
                name=kernel.__name__,
            )(*operands)

        def crossed(pairs):
            return [(source, (target + ranks) % (2 * ranks)) for source, target in pairs]

        base, own_other = by_columns(own_kernel, F32, state, own_sum, side_in)
        near_mine, near_other = by_columns(
            sum_kernel, BF16, near_sum, far_in, near_side_in, two_in
        )
        result = base + send(own_other, "grp", plane_swap)
        result = result + send(near_mine, both_axes, backward)
        result = result + send(near_other, both_axes, crossed(backward))
        return result.astype(BF16)

    line = [packet]
    for _ in range(1, ring):
        line.append(lax.ppermute(line[-1], "ep", ring_next))
    totals = []
    for part in line:
        sums = run_expert([lax.ppermute(part, "ep", side_swap), part], packet, packet)
        over, here = join(*sums, [BF16, F32])
        totals.append(here + send(over, "ep", side_swap))
    moving = totals[1 % ring]
    for hop in list(range(2, ring)) + [0]:
        moving = totals[hop] + send(moving, "ep", ring_next)

    result = state + lax.dynamic_slice_in_dim(moving, group * columns, columns, 1)
    for by in range(1, groups):
        to = (group + by) % groups
        part = lax.dynamic_slice_in_dim(moving, to * columns, columns, 1)
        result = result + send(part, "grp", turn(by))
    return result.astype(BF16)


def solution(mesh):
    in_specs = (
        P("ep", None),
        P("ep", "grp"),
        P("ep", "grp"),
        P("ep", None),
        P("ep", None),
        P("grp", None, None),
        P("grp", None, None),
        P("grp", None),
        P(),
        P(),
        P("ep", None),
        P("ep", None, "grp"),
        P("ep", None, "grp"),
        P("ep", "grp", None),
        P("ep", None),
        P("ep"),
        P("ep", None, None),
    )
    out_specs = P("ep", "grp")
    return jax.shard_map(local, mesh=mesh, in_specs=in_specs, out_specs=out_specs, check_vma=False)
```

```python
import functools

import jax
import jax.numpy as jnp
from jax import lax
from jax.experimental import pallas as pl
from jax.experimental.pallas import tpu as pltpu
from jax.sharding import PartitionSpec as P

F32 = jnp.float32
BF16 = jnp.bfloat16
HIDDEN = -1e30
VMEM = pltpu.VMEM
ANY = pl.BlockSpec(memory_space=pl.ANY)
WHOLE = pl.BlockSpec(memory_space=pltpu.VMEM)


def dot(a, b):
    return jnp.dot(a, b, preferred_element_type=F32)


def dot_rows(a, b):
    return lax.dot_general(a, b, (((1,), (1,)), ((), ())), preferred_element_type=F32)


def cost(products, moved_bytes):
    return pl.CostEstimate(flops=2 * products, bytes_accessed=moved_bytes, transcendentals=0)


def fetch_all(sources, buffers, sems):
    copies = []
    for at, (source, buffer) in enumerate(zip(sources, buffers)):
        copy = pltpu.make_async_copy(source, buffer, sems.at[at])
        copy.start()
        copies.append(copy)
    return copies


def lay_tokens(keys, start, ref, tokens, width):
    count = ref.shape[0]
    for token in range(tokens):
        keys[start : start + count, :width] = ref[:, token * width : (token + 1) * width]
        start += count
    return start


def pick_kernel(pieces, moves_any, cache_any, out_ref, moves_ref, cache, stacked, sems):
    got = fetch_all((moves_any, cache_any), (moves_ref, cache), sems)
    ranks, per_rank, wide = out_ref.shape
    slots = moves_ref.shape[0]
    resident = cache.shape[0]
    rows = ranks * per_rank
    row = lax.broadcasted_iota(jnp.int32, (rows, ranks), 0)
    rank = lax.broadcasted_iota(jnp.int32, (rows, ranks), 1)
    chosen = jnp.zeros((rows, ranks), jnp.int32)
    got[0].wait()
    for slot in range(slots):
        here = (row // per_rank == rank) & (row % per_rank // pieces == slot)
        chosen = chosen + jnp.where(here, moves_ref[slot : slot + 1, :], 0)
    block = jnp.clip(jnp.sum(chosen, axis=1, keepdims=True), 0, resident - 1)
    at = lax.broadcasted_iota(jnp.int32, (rows, pieces * resident), 0)
    source = lax.broadcasted_iota(jnp.int32, (rows, pieces * resident), 1)
    pick = (source // resident == at % pieces) & (source % resident == block)
    got[1].wait()
    for piece in range(pieces):
        stacked[piece * resident : (piece + 1) * resident, :] = cache[:, piece * wide : (piece + 1) * wide]
    picked = dot(pick.astype(F32).astype(BF16), stacked[...]).astype(BF16)
    out_ref[...] = picked.reshape(ranks, per_rank, wide)


def resident_kernel(
    dims, nope, rope_rows, fresh, cache, absorb, bias_ref,
    query_ref, mixed_ref,
    keys,
):
    head_count, nope_dim, latent, rope, block_size, steps = dims
    width = latent + rope
    rows = nope.shape[0]
    padding = keys.shape[1] - width
    keys[:, latent:] = jnp.zeros((keys.shape[0], keys.shape[1] - latent), BF16)
    start = lay_tokens(keys, 0, cache, block_size, width)
    lay_tokens(keys, start, fresh, steps, width)
    for head in range(head_count):
        q_latent = dot(nope[:, head * nope_dim : (head + 1) * nope_dim], absorb[head])
        q_rope = rope_rows[:, head * rope : (head + 1) * rope]
        fill = jnp.zeros((rows, padding), BF16)
        query_ref[head * rows : (head + 1) * rows, :] = jnp.concatenate(
            [q_latent.astype(BF16), q_rope, fill], axis=1
        )
    scale = (nope_dim + rope) ** (-0.5)
    part = min(4, head_count) * rows
    for first in range(0, head_count * rows, part):
        score = dot_rows(query_ref[first : first + part, :], keys[...])
        score = score.reshape(part // rows, rows, -1) * scale + bias_ref[...][None]
        score = score.reshape(part, -1)
        peak = jnp.max(score, axis=1, keepdims=True)
        weight = jnp.exp(score - peak)
        total = jnp.sum(weight, axis=1, keepdims=True)
        mixed_ref[first : first + part, :latent] = dot(weight.astype(BF16), keys[:, :latent])
        lane = lax.broadcasted_iota(jnp.int32, (part, 128), 1)
        mixed_ref[first : first + part, latent:] = jnp.where(lane < 64, peak, total)


def moved_kernel(
    dims, moved_any, query_any, bias_any, mixed_any, value_any, proj_any,
    share_ref,
    moved, query, bias, mixed, value, proj, keys, heads_out, sems,
):
    head_count, nope_dim, latent, rope, block_size, steps = dims
    width = latent + rope
    rows = heads_out.shape[0]
    got = fetch_all(
        (moved_any, query_any, bias_any, mixed_any, value_any, proj_any),
        (moved, query, bias, mixed, value, proj),
        sems,
    )
    keys[:, latent:] = jnp.zeros((keys.shape[0], keys.shape[1] - latent), BF16)
    scale = (nope_dim + rope) ** (-0.5)
    value_dim = value.shape[2]
    got[0].wait()
    count = moved.shape[0] * moved.shape[1]
    for half in range(2):
        part = moved[:, :, half * width : (half + 1) * width]
        keys[half * count : (half + 1) * count, :width] = part.reshape(count, width)
    got[1].wait()
    got[2].wait()
    group = min(4, head_count)
    for first in range(0, head_count, group):
        at = slice(first * rows, (first + group) * rows)
        score = dot_rows(query[at, :], keys[...])
        score = score.reshape(group, rows, -1) * scale + bias[...][None]
        score = score.reshape(group * rows, -1)
        if first == 0:
            got[3].wait()
        before = mixed[at, latent : latent + 1]
        peak = jnp.maximum(jnp.max(score, axis=1, keepdims=True), before)
        weight = jnp.exp(score - peak)
        keep = jnp.exp(before - peak)
        total = jnp.sum(weight, axis=1, keepdims=True) + mixed[at, latent + 64 : latent + 65] * keep
        joined = dot(weight.astype(BF16), keys[:, :latent]) + mixed[at, :latent] * keep
        joined = (joined / total).astype(BF16)
        if first == 0:
            got[4].wait()
        for head in range(first, first + group):
            own = joined[(head - first) * rows : (head - first + 1) * rows]
            heads_out[:, head * value_dim : (head + 1) * value_dim] = dot(own, value[head]).astype(BF16)
    got[5].wait()
    share_ref[...] = dot(heads_out[...], proj[...]).astype(BF16)


def own_columns(ref, shift):
    groups = lax.axis_size("grp")
    columns = ref.shape[1] // groups
    first = (lax.axis_index("grp") + shift) % groups * columns
    return ref[:, pl.ds(pl.multiple_of(first, 128), columns)]


def norm_kernel(experts, own_any, hidden_any, loaded_any, gain_ref, router_ref, ids_ref, *refs):
    parts, (state_ref, packet_ref, own, hidden, whole, sems) = refs[:-6], refs[-6:]
    got = fetch_all((own_any, hidden_any), (own, hidden), sems)
    rows, model = hidden.shape
    state = parts[0][...].astype(F32)
    for part in parts[1:]:
        state = state + part[...].astype(F32)
    for copy in got:
        copy.wait()
    state = state + own[...].astype(F32) + hidden[...].astype(F32)
    whole[...] = state
    state_ref[...] = own_columns(whole, 0)
    square = jnp.mean(state * state, axis=1, keepdims=True)
    normed = (state * lax.rsqrt(square + 1e-06) * gain_ref[...].astype(F32)).astype(BF16)
    packet_ref[:, :model] = normed
    logits = dot_rows(router_ref[...], normed)
    names = lax.broadcasted_iota(jnp.int32, (experts, rows), 0)
    named = names == ids_ref[0:1, :]
    for k in range(1, ids_ref.shape[0]):
        named = named | (names == ids_ref[k : k + 1, :])
    chosen = jnp.where(named, jax.nn.sigmoid(logits), 0.0)
    weight = chosen / jnp.sum(chosen, axis=0, keepdims=True)
    high = weight.astype(BF16)
    low = (weight - high.astype(F32)).astype(BF16)
    extra = packet_ref.shape[1] - model
    both = jnp.concatenate([high, low], axis=0)
    place = lax.broadcasted_iota(jnp.int32, (2 * experts, extra), 0)
    lane = lax.broadcasted_iota(jnp.int32, (2 * experts, extra), 1)
    turned = lax.dot_general(
        both, (place == lane).astype(BF16), (((0,), (0,)), ((), ())), preferred_element_type=F32
    )
    packet_ref[:, model:] = turned.astype(BF16)


def load_kernel(after_any, gate_any, up_any, down_any, gate_ref, up_ref, down_ref, sems):
    sources, targets = (gate_any, up_any, down_any), (gate_ref, up_ref, down_ref)
    for copy in fetch_all(sources, targets, sems):
        copy.wait()


def pack_kernel(after_any, *refs):
    count = refs[0].shape[0]
    for at, ref in enumerate(refs[:-1]):
        refs[-1][at * count : (at + 1) * count, :] = ref[...]


def expert_kernel(experts, after_any, here_ref, across_ref, gate_ref, up_ref, down_ref, *out_refs):
    near_ref, *far_refs = out_refs
    model = gate_ref.shape[1]
    packet = jnp.concatenate([here_ref[...], across_ref[...]], axis=0)
    rows = packet[:, :model]
    extra = packet[:, model:].astype(F32)
    names = lax.broadcasted_iota(jnp.int32, extra.shape, 1)
    me = lax.axis_index("ep")
    mine = (names == me) | (names == me + experts)
    weight = jnp.sum(jnp.where(mine, extra, 0.0), axis=1, keepdims=True)
    gate = dot_rows(rows, gate_ref[...])
    up = dot_rows(rows, up_ref[...])
    inner = (gate * jax.nn.sigmoid(gate) * up * weight).astype(BF16)
    result = dot(inner, down_ref[...]).astype(BF16)
    half = near_ref.shape[0]
    near_ref[...] = result[:half]
    height = half // len(far_refs)
    for at, far_ref in enumerate(far_refs):
        far_ref[...] = result[half + at * height : half + (at + 1) * height]


def join_kernel(first, back_count, after_count, near_ref, *refs):
    back_refs, out_refs = refs[after_count : after_count + back_count], refs[after_count + back_count :]
    count = out_refs[0].shape[0]
    height = back_refs[0].shape[0]
    step = min(count, height)
    for at, ref in enumerate(out_refs, first):
        for row in range(at * count, (at + 1) * count, step):
            back = back_refs[row // height][row % height : row % height + step, :].astype(F32)
            total = near_ref[row : row + step, :].astype(F32) + back
            ref[row - at * count : row - at * count + step, :] = total.astype(ref.dtype)


def own_kernel(state_ref, own_ref, side_ref, base_ref, other_ref):
    mine, other = (own_columns(own_ref, by) + own_columns(side_ref, by).astype(F32) for by in (0, 1))
    base_ref[...] = state_ref[...] + mine
    other_ref[...] = other.astype(BF16)


def last_kernel(base_ref, *refs):
    total = base_ref[...]
    for ref in refs[:-1]:
        total = total + ref[...].astype(F32)
    refs[-1][...] = total.astype(BF16)


def sum_kernel(*refs):
    parts, (mine_ref, other_ref) = refs[:-2], refs[-2:]
    for shift, ref in ((0, mine_ref), (1, other_ref)):
        total = own_columns(parts[0], shift).astype(F32)
        for part in parts[1:]:
            total = total + own_columns(part, shift).astype(F32)
        ref[...] = total.astype(BF16)


def local(
    hidden_in,
    query_nope,
    query_rope,
    new_latent,
    latent_cache,
    key_absorb,
    value_absorb,
    output_proj,
    norm_gain,
    router_proj,
    expert_ids,
    expert_gate,
    expert_up,
    expert_down,
    block_table,
    lengths,
    subtree_moves,
):
    head_count, nope_dim, latent = key_absorb.shape
    rope = query_rope.shape[1] // head_count
    width = latent + rope
    requests, table_len = block_table.shape
    steps = new_latent.shape[1] // width
    row_count, model = hidden_in.shape
    block_size = latent_cache.shape[1] // width
    resident = latent_cache.shape[0]
    experts = router_proj.shape[1]
    groups = lax.axis_size("grp")
    group = lax.axis_index("grp")
    ranks = lax.axis_size("ep")
    me = lax.axis_index("ep")
    ring = ranks // 4
    core_swap = [(i, i ^ 1) for i in range(ranks)]
    side_swap = [(i, i ^ 2) for i in range(ranks)]
    ring_next = [(i, (i + 4) % ranks) for i in range(ranks)]
    both_axes = ("grp", "ep")

    def turn(by):
        return [(g, (g + by) % groups) for g in range(groups)]

    slots = subtree_moves.shape[2]
    pieces = block_size // 2
    outgoing = pl.pallas_call(
        functools.partial(pick_kernel, pieces),
        out_shape=jax.ShapeDtypeStruct((ranks, slots * pieces, 2 * width), BF16),
        in_specs=[ANY] * 2,
        scratch_shapes=[
            VMEM((slots, ranks), jnp.int32),
            VMEM(latent_cache.shape, BF16),
            VMEM((pieces * resident, 2 * width), BF16),
            pltpu.SemaphoreType.DMA((2,)),
        ],
        compiler_params=pltpu.CompilerParams(vmem_limit_bytes=60 * 2**20),
        cost_estimate=cost(0, 4 * 2**20),
        name="pick",
    )(subtree_moves[0].T, latent_cache)
    arrived = lax.all_to_all(outgoing, "ep", split_axis=0, concat_axis=0, tiled=True)

    place = jnp.arange(table_len, dtype=jnp.int32)
    usable = jnp.clip(lengths[:, None] - place[None, :] * block_size, 0, block_size)
    blocks = jnp.arange(resident + ranks * slots, dtype=jnp.int32)
    limit = jnp.sum(
        jnp.where(block_table[:, :, None] == blocks[None, None, :], usable[:, :, None], 0), axis=1
    )
    token = jnp.arange(block_size, dtype=jnp.int32)
    row = jnp.arange(row_count, dtype=jnp.int32)
    fresh = jnp.arange(steps * requests, dtype=jnp.int32)
    fresh_open = ((row // steps)[:, None] == (fresh % requests)[None, :]) & (
        (fresh // requests)[None, :] <= (row % steps)[:, None]
    )
    near_open = (limit[:, None, :resident] > token[None, :, None]).reshape(requests, -1)
    near_open = jnp.concatenate([jnp.repeat(near_open, steps, axis=0), fresh_open], axis=1)
    near_bias = jnp.where(near_open, 0.0, HIDDEN).astype(F32)
    by_key = jnp.repeat(limit[:, resident:], pieces, axis=1)
    at_token = 2 * (jnp.arange(ranks * slots * pieces, dtype=jnp.int32) % pieces)
    moved_open = jnp.concatenate([by_key > at_token[None], by_key > at_token[None] + 1], axis=1)
    moved_bias = jnp.repeat(jnp.where(moved_open, 0.0, HIDDEN).astype(F32), steps, axis=0)

    padded = -(-width // 128) * 128
    query_rows = head_count * row_count
    dims = (head_count, nope_dim, latent, rope, block_size, steps)
    query, mixed = pl.pallas_call(
        functools.partial(resident_kernel, dims),
        out_shape=(
            jax.ShapeDtypeStruct((query_rows, padded), BF16),
            jax.ShapeDtypeStruct((query_rows, latent + 128), F32),
        ),
        scratch_shapes=[VMEM((near_bias.shape[1], padded), BF16)],
        compiler_params=pltpu.CompilerParams(vmem_limit_bytes=16 * 2**20),
        cost_estimate=cost(query_rows * near_bias.shape[1] * (padded + latent), 8 * 2**20),
        name="attend_resident",
    )(query_nope, query_rope, new_latent, latent_cache, key_absorb, near_bias)
    share = pl.pallas_call(
        functools.partial(moved_kernel, dims),
        out_shape=jax.ShapeDtypeStruct((row_count, model), BF16),
        in_specs=[ANY] * 6,
        scratch_shapes=[
            VMEM(arrived.shape, BF16),
            VMEM(query.shape, BF16),
            VMEM(moved_bias.shape, F32),
            VMEM(mixed.shape, F32),
            VMEM(value_absorb.shape, BF16),
            VMEM(output_proj.shape, BF16),
            VMEM((moved_bias.shape[1], padded), BF16),
            VMEM((row_count, head_count * value_absorb.shape[2]), BF16),
            pltpu.SemaphoreType.DMA((6,)),
        ],
        compiler_params=pltpu.CompilerParams(vmem_limit_bytes=60 * 2**20),
        cost_estimate=cost(query_rows * moved_bias.shape[1] * (padded + latent), 10 * 2**20),
        name="attend_moved",
    )(arrived, query, moved_bias, mixed, value_absorb, output_proj)
    shares = [lax.ppermute(share, "grp", turn(by)) for by in range(1, groups)]

    held = [jnp.swapaxes(expert_gate[0], 0, 1), jnp.swapaxes(expert_up[0], 0, 1), expert_down[0]]
    gate_rows, up_rows, down_rows = pl.pallas_call(
        load_kernel,
        out_shape=[jax.ShapeDtypeStruct(array.shape, BF16) for array in held],
        in_specs=[ANY] * 4,
        out_specs=[WHOLE] * 3,
        scratch_shapes=[pltpu.SemaphoreType.DMA((3,))],
        compiler_params=pltpu.CompilerParams(vmem_limit_bytes=44 * 2**20),
        cost_estimate=cost(0, 12 * 2**20),
        name="load",
    )(share, *held)

    extra = -(-2 * experts // 128) * 128
    columns = model // groups
    state, packet = pl.pallas_call(
        functools.partial(norm_kernel, experts),
        out_shape=(
            jax.ShapeDtypeStruct((row_count, columns), F32),
            jax.ShapeDtypeStruct((row_count, model + extra), BF16),
        ),
        in_specs=[ANY] * 3 + [WHOLE] * (2 + groups),
        scratch_shapes=[
            VMEM((row_count, model), BF16),
            VMEM((row_count, model), BF16),
            VMEM((row_count, model), F32),
            pltpu.SemaphoreType.DMA((2,)),
        ],
        compiler_params=pltpu.CompilerParams(vmem_limit_bytes=16 * 2**20),
        cost_estimate=cost(row_count * model * 128, 4 * 2**20),
        name="norm",
    )(share, hidden_in, down_rows, norm_gain[None, :], router_proj.T, expert_ids.T, *shares)

    def run_expert(rows, after, run_after, back=1):
        half = len(rows) * row_count
        here = pl.pallas_call(
            pack_kernel,
            out_shape=jax.ShapeDtypeStruct((half, model + extra), BF16),
            in_specs=[ANY] + [WHOLE] * len(rows),
            compiler_params=pltpu.CompilerParams(vmem_limit_bytes=16 * 2**20),
            cost_estimate=cost(0, 2 * half * model * 2),
            name="pack",
        )(after, *rows)
        across = lax.ppermute(here, "ep", core_swap)
        near, *far = pl.pallas_call(
            functools.partial(expert_kernel, experts),
            out_shape=[
                jax.ShapeDtypeStruct((half // cuts, model), BF16) for cuts in [1] + [back] * back
            ],
            in_specs=[ANY] + [WHOLE] * 5,
            compiler_params=pltpu.CompilerParams(vmem_limit_bytes=24 * 2**20),
            cost_estimate=cost(6 * half * model * gate_rows.shape[0], 12 * 2**20),
            name="expert",
        )(run_after, here, across, gate_rows, up_rows, down_rows)
        return near, [lax.ppermute(part, "ep", core_swap) for part in far]

    def join(near, back, types, first=0, after=()):
        return pl.pallas_call(
            functools.partial(join_kernel, first, len(back), len(after)),
            out_shape=[jax.ShapeDtypeStruct((row_count, model), kind) for kind in types],
            in_specs=[WHOLE] + [ANY] * len(after) + [WHOLE] * len(back),
            compiler_params=pltpu.CompilerParams(vmem_limit_bytes=16 * 2**20),
            cost_estimate=cost(row_count * model, 2**20),
            name="join",
        )(near, *after, *back)

    def send(value, axes, pairs):
        return lax.ppermute(value.astype(BF16), axes, pairs).astype(F32)

    if ring == 4 and groups == 2:
        def ring_step(sign):
            return [
                (g * ranks + i, g * ranks + (i + sign * 4 * (1 - 2 * g)) % ranks)
                for g in range(2)
                for i in range(ranks)
            ]

        onward, backward, plane_swap = ring_step(1), ring_step(-1), [(0, 1), (1, 0)]
        near = lax.ppermute(packet, both_axes, onward)
        side = lax.ppermute(packet, "ep", side_swap)
        two = lax.ppermute(near, both_axes, onward)
        near_side = lax.ppermute(near, "ep", side_swap)
        far = lax.ppermute(near, "grp", plane_swap)
        two_side = lax.ppermute(two, "ep", side_swap)
        far_side = lax.ppermute(near_side, "grp", plane_swap)
        early = run_expert([packet, side, near], packet, packet)
        later = run_expert([far, near_side, two], early[0], packet)
        own_sum, side_sum, near_sum = join(*early, [F32, BF16, F32])
        side_in = lax.ppermute(side_sum, "ep", side_swap)
        last = run_expert([far_side, two_side], later[0], side_sum, 2)
        near_side_sum, two_sum = join(*later, [F32, F32], 1)
        far_side_sum, two_side_sum = join(*last, [BF16, BF16], 0, [side_in])
        far_side_in = lax.ppermute(far_side_sum, "grp", plane_swap)
        two_side_in = lax.ppermute(two_side_sum, "ep", side_swap)
        [near_side_sum] = join(near_side_sum, [far_side_in], [BF16])
        [two_sum] = join(two_sum, [two_side_in], [BF16])
        [far_sum] = join(*later, [BF16], 0, [far_side_in])
        far_in = lax.ppermute(far_sum, "grp", plane_swap)
        near_side_in = lax.ppermute(near_side_sum, "ep", side_swap)
        two_in = lax.ppermute(two_sum, both_axes, backward)
        part = (row_count, columns)

        def by_columns(kernel, first_type, *operands):
            return pl.pallas_call(
                kernel,
                out_shape=(
                    jax.ShapeDtypeStruct(part, first_type),
                    jax.ShapeDtypeStruct(part, BF16),
                ),
                compiler_params=pltpu.CompilerParams(vmem_limit_bytes=16 * 2**20),
                cost_estimate=cost(row_count * model, 2**20),
                name=kernel.__name__,
            )(*operands)

        def crossed(pairs):
            return [(source, (target + ranks) % (2 * ranks)) for source, target in pairs]

        base, own_other = by_columns(own_kernel, F32, state, own_sum, side_in)
        near_mine, near_other = by_columns(
            sum_kernel, BF16, near_sum, far_in, near_side_in, two_in
        )
        own_over = lax.ppermute(own_other, "grp", plane_swap)
        mine_in = lax.ppermute(near_mine, both_axes, backward)
        other_in = lax.ppermute(near_other, both_axes, crossed(backward))
        return pl.pallas_call(
            last_kernel,
            out_shape=jax.ShapeDtypeStruct(part, BF16),
            in_specs=[WHOLE] * 4,
            compiler_params=pltpu.CompilerParams(vmem_limit_bytes=16 * 2**20),
            cost_estimate=cost(0, 2**20),
            name="last",
        )(base, own_over, mine_in, other_in)

    line = [packet]
    for _ in range(1, ring):
        line.append(lax.ppermute(line[-1], "ep", ring_next))
    totals = []
    for part in line:
        sums = run_expert([lax.ppermute(part, "ep", side_swap), part], packet, packet)
        over, here = join(*sums, [BF16, F32])
        totals.append(here + send(over, "ep", side_swap))
    moving = totals[1 % ring]
    for hop in list(range(2, ring)) + [0]:
        moving = totals[hop] + send(moving, "ep", ring_next)

    result = state + lax.dynamic_slice_in_dim(moving, group * columns, columns, 1)
    for by in range(1, groups):
        to = (group + by) % groups
        part = lax.dynamic_slice_in_dim(moving, to * columns, columns, 1)
        result = result + send(part, "grp", turn(by))
    return result.astype(BF16)


def solution(mesh):
    in_specs = (
        P("ep", None),
        P("ep", "grp"),
        P("ep", "grp"),
        P("ep", None),
        P("ep", None),
        P("grp", None, None),
        P("grp", None, None),
        P("grp", None),
        P(),
        P(),
        P("ep", None),
        P("ep", None, "grp"),
        P("ep", None, "grp"),
        P("ep", "grp", None),
        P("ep", None),
        P("ep"),
        P("ep", None, None),
    )
    out_specs = P("ep", "grp")
    return jax.shard_map(local, mesh=mesh, in_specs=in_specs, out_specs=out_specs, check_vma=False)
```

```python
import functools

import jax
import jax.numpy as jnp
from jax import lax
from jax.experimental import pallas as pl
from jax.experimental.pallas import tpu as pltpu
from jax.sharding import PartitionSpec as P

F32 = jnp.float32
BF16 = jnp.bfloat16
HIDDEN = -1e30
VMEM = pltpu.VMEM
ANY = pl.BlockSpec(memory_space=pl.ANY)
WHOLE = pl.BlockSpec(memory_space=pltpu.VMEM)


def dot(a, b):
    return jnp.dot(a, b, preferred_element_type=F32)


def dot_rows(a, b):
    return lax.dot_general(a, b, (((1,), (1,)), ((), ())), preferred_element_type=F32)


def cost(products, moved_bytes):
    return pl.CostEstimate(flops=2 * products, bytes_accessed=moved_bytes, transcendentals=0)


def fetch_all(sources, buffers, sems):
    copies = []
    for at, (source, buffer) in enumerate(zip(sources, buffers)):
        copy = pltpu.make_async_copy(source, buffer, sems.at[at])
        copy.start()
        copies.append(copy)
    return copies


def lay_tokens(keys, start, ref, tokens, width):
    count = ref.shape[0]
    for token in range(tokens):
        keys[start : start + count, :width] = ref[:, token * width : (token + 1) * width]
        start += count
    return start


def pick_kernel(pieces, moves_any, cache_any, out_ref, moves_ref, cache, stacked, sems):
    got = fetch_all((moves_any, cache_any), (moves_ref, cache), sems)
    ranks, per_rank, wide = out_ref.shape
    slots = moves_ref.shape[0]
    resident = cache.shape[0]
    rows = ranks * per_rank
    row = lax.broadcasted_iota(jnp.int32, (rows, ranks), 0)
    rank = lax.broadcasted_iota(jnp.int32, (rows, ranks), 1)
    chosen = jnp.zeros((rows, ranks), jnp.int32)
    got[0].wait()
    for slot in range(slots):
        here = (row // per_rank == rank) & (row % per_rank // pieces == slot)
        chosen = chosen + jnp.where(here, moves_ref[slot : slot + 1, :], 0)
    block = jnp.clip(jnp.sum(chosen, axis=1, keepdims=True), 0, resident - 1)
    at = lax.broadcasted_iota(jnp.int32, (rows, pieces * resident), 0)
    source = lax.broadcasted_iota(jnp.int32, (rows, pieces * resident), 1)
    pick = (source // resident == at % pieces) & (source % resident == block)
    got[1].wait()
    for piece in range(pieces):
        stacked[piece * resident : (piece + 1) * resident, :] = cache[:, piece * wide : (piece + 1) * wide]
    picked = dot(pick.astype(F32).astype(BF16), stacked[...]).astype(BF16)
    out_ref[...] = picked.reshape(ranks, per_rank, wide)


def resident_kernel(
    dims, nope, rope_rows, fresh, cache, absorb, bias_ref,
    query_ref, mixed_ref,
    keys,
):
    head_count, nope_dim, latent, rope, block_size, steps = dims
    width = latent + rope
    rows = nope.shape[0]
    padding = keys.shape[1] - width
    keys[:, latent:] = jnp.zeros((keys.shape[0], keys.shape[1] - latent), BF16)
    start = lay_tokens(keys, 0, cache, block_size, width)
    lay_tokens(keys, start, fresh, steps, width)
    for head in range(head_count):
        q_latent = dot(nope[:, head * nope_dim : (head + 1) * nope_dim], absorb[head])
        q_rope = rope_rows[:, head * rope : (head + 1) * rope]
        fill = jnp.zeros((rows, padding), BF16)
        query_ref[head * rows : (head + 1) * rows, :] = jnp.concatenate(
            [q_latent.astype(BF16), q_rope, fill], axis=1
        )
    scale = (nope_dim + rope) ** (-0.5)
    part = min(4, head_count) * rows
    for first in range(0, head_count * rows, part):
        score = dot_rows(query_ref[first : first + part, :], keys[...])
        score = score.reshape(part // rows, rows, -1) * scale + bias_ref[...][None]
        score = score.reshape(part, -1)
        peak = jnp.max(score, axis=1, keepdims=True)
        weight = jnp.exp(score - peak)
        total = jnp.sum(weight, axis=1, keepdims=True)
        mixed_ref[first : first + part, :latent] = dot(weight.astype(BF16), keys[:, :latent])
        lane = lax.broadcasted_iota(jnp.int32, (part, 128), 1)
        mixed_ref[first : first + part, latent:] = jnp.where(lane < 64, peak, total)


def moved_kernel(
    dims, moved_any, query_any, bias_any, mixed_any, value_any, proj_any,
    share_ref,
    moved, query, bias, mixed, value, proj, keys, heads_out, sems,
):
    head_count, nope_dim, latent, rope, block_size, steps = dims
    width = latent + rope
    rows = heads_out.shape[0]
    got = fetch_all(
        (moved_any, query_any, bias_any, mixed_any, value_any, proj_any),
        (moved, query, bias, mixed, value, proj),
        sems,
    )
    keys[:, latent:] = jnp.zeros((keys.shape[0], keys.shape[1] - latent), BF16)
    scale = (nope_dim + rope) ** (-0.5)
    value_dim = value.shape[2]
    got[0].wait()
    count = moved.shape[0] * moved.shape[1]
    for half in range(2):
        part = moved[:, :, half * width : (half + 1) * width]
        keys[half * count : (half + 1) * count, :width] = part.reshape(count, width)
    got[1].wait()
    got[2].wait()
    group = min(4, head_count)
    for first in range(0, head_count, group):
        at = slice(first * rows, (first + group) * rows)
        score = dot_rows(query[at, :], keys[...])
        score = score.reshape(group, rows, -1) * scale + bias[...][None]
        score = score.reshape(group * rows, -1)
        if first == 0:
            got[3].wait()
        before = mixed[at, latent : latent + 1]
        peak = jnp.maximum(jnp.max(score, axis=1, keepdims=True), before)
        weight = jnp.exp(score - peak)
        keep = jnp.exp(before - peak)
        total = jnp.sum(weight, axis=1, keepdims=True) + mixed[at, latent + 64 : latent + 65] * keep
        joined = dot(weight.astype(BF16), keys[:, :latent]) + mixed[at, :latent] * keep
        joined = (joined / total).astype(BF16)
        if first == 0:
            got[4].wait()
        for head in range(first, first + group):
            own = joined[(head - first) * rows : (head - first + 1) * rows]
            heads_out[:, head * value_dim : (head + 1) * value_dim] = dot(own, value[head]).astype(BF16)
    got[5].wait()
    share_ref[...] = dot(heads_out[...], proj[...]).astype(BF16)


def own_columns(ref, shift):
    groups = lax.axis_size("grp")
    columns = ref.shape[1] // groups
    first = (lax.axis_index("grp") + shift) % groups * columns
    return ref[:, pl.ds(pl.multiple_of(first, 128), columns)]


def norm_kernel(experts, own_any, hidden_any, loaded_any, gain_ref, router_ref, ids_ref, *refs):
    parts, (state_ref, packet_ref, own, hidden, whole, sems) = refs[:-6], refs[-6:]
    got = fetch_all((own_any, hidden_any), (own, hidden), sems)
    rows, model = hidden.shape
    state = parts[0][...].astype(F32)
    for part in parts[1:]:
        state = state + part[...].astype(F32)
    for copy in got:
        copy.wait()
    state = state + own[...].astype(F32) + hidden[...].astype(F32)
    whole[...] = state
    state_ref[...] = own_columns(whole, 0)
    square = jnp.mean(state * state, axis=1, keepdims=True)
    normed = (state * lax.rsqrt(square + 1e-06) * gain_ref[...].astype(F32)).astype(BF16)
    packet_ref[:, :model] = normed
    logits = dot_rows(router_ref[...], normed)
    names = lax.broadcasted_iota(jnp.int32, (experts, rows), 0)
    named = names == ids_ref[0:1, :]
    for k in range(1, ids_ref.shape[0]):
        named = named | (names == ids_ref[k : k + 1, :])
    chosen = jnp.where(named, jax.nn.sigmoid(logits), 0.0)
    weight = chosen / jnp.sum(chosen, axis=0, keepdims=True)
    high = weight.astype(BF16)
    low = (weight - high.astype(F32)).astype(BF16)
    extra = packet_ref.shape[1] - model
    both = jnp.concatenate([high, low], axis=0)
    place = lax.broadcasted_iota(jnp.int32, (2 * experts, extra), 0)
    lane = lax.broadcasted_iota(jnp.int32, (2 * experts, extra), 1)
    turned = lax.dot_general(
        both, (place == lane).astype(BF16), (((0,), (0,)), ((), ())), preferred_element_type=F32
    )
    packet_ref[:, model:] = turned.astype(BF16)


def load_kernel(after_any, gate_any, up_any, down_any, gate_ref, up_ref, down_ref, sems):
    sources, targets = (gate_any, up_any, down_any), (gate_ref, up_ref, down_ref)
    for copy in fetch_all(sources, targets, sems):
        copy.wait()


def pack_kernel(after_any, *refs):
    count = refs[0].shape[0]
    for at, ref in enumerate(refs[:-1]):
        refs[-1][at * count : (at + 1) * count, :] = ref[...]


def expert_kernel(experts, after_any, here_ref, across_ref, gate_ref, up_ref, down_ref, *out_refs):
    near_ref, *far_refs = out_refs
    model = gate_ref.shape[1]
    packet = jnp.concatenate([here_ref[...], across_ref[...]], axis=0)
    rows = packet[:, :model]
    extra = packet[:, model:].astype(F32)
    names = lax.broadcasted_iota(jnp.int32, extra.shape, 1)
    me = lax.axis_index("ep")
    mine = (names == me) | (names == me + experts)
    weight = jnp.sum(jnp.where(mine, extra, 0.0), axis=1, keepdims=True)
    gate = dot_rows(rows, gate_ref[...])
    up = dot_rows(rows, up_ref[...])
    inner = (gate * jax.nn.sigmoid(gate) * up * weight).astype(BF16)
    result = dot(inner, down_ref[...]).astype(BF16)
    half = near_ref.shape[0]
    near_ref[...] = result[:half]
    height = half // len(far_refs)
    for at, far_ref in enumerate(far_refs):
        far_ref[...] = result[half + at * height : half + (at + 1) * height]


def join_kernel(first, back_count, after_count, near_ref, *refs):
    back_refs, out_refs = refs[after_count : after_count + back_count], refs[after_count + back_count :]
    count = out_refs[0].shape[0]
    height = back_refs[0].shape[0]
    step = min(count, height)
    for at, ref in enumerate(out_refs, first):
        for row in range(at * count, (at + 1) * count, step):
            back = back_refs[row // height][row % height : row % height + step, :].astype(F32)
            total = near_ref[row : row + step, :].astype(F32) + back
            ref[row - at * count : row - at * count + step, :] = total.astype(ref.dtype)


def own_kernel(state_ref, own_ref, side_ref, base_ref, other_ref):
    mine, other = (own_columns(own_ref, by) + own_columns(side_ref, by).astype(F32) for by in (0, 1))
    base_ref[...] = state_ref[...] + mine
    other_ref[...] = other.astype(BF16)


def last_kernel(base_ref, *refs):
    total = base_ref[...]
    for ref in refs[:-1]:
        total = total + ref[...].astype(F32)
    refs[-1][...] = total.astype(BF16)


def sum_kernel(*refs):
    parts, (mine_ref, other_ref) = refs[:-2], refs[-2:]
    for shift, ref in ((0, mine_ref), (1, other_ref)):
        total = own_columns(parts[0], shift).astype(F32)
        for part in parts[1:]:
            total = total + own_columns(part, shift).astype(F32)
        ref[...] = total.astype(BF16)


def local(
    hidden_in,
    query_nope,
    query_rope,
    new_latent,
    latent_cache,
    key_absorb,
    value_absorb,
    output_proj,
    norm_gain,
    router_proj,
    expert_ids,
    expert_gate,
    expert_up,
    expert_down,
    block_table,
    lengths,
    subtree_moves,
):
    head_count, nope_dim, latent = key_absorb.shape
    rope = query_rope.shape[1] // head_count
    width = latent + rope
    requests, table_len = block_table.shape
    steps = new_latent.shape[1] // width
    row_count, model = hidden_in.shape
    block_size = latent_cache.shape[1] // width
    resident = latent_cache.shape[0]
    experts = router_proj.shape[1]
    groups = lax.axis_size("grp")
    group = lax.axis_index("grp")
    ranks = lax.axis_size("ep")
    me = lax.axis_index("ep")
    ring = ranks // 4
    core_swap = [(i, i ^ 1) for i in range(ranks)]
    side_swap = [(i, i ^ 2) for i in range(ranks)]
    visit = list(range(0, ring, 2)) + list(range(ring - 1 - ring % 2, 0, -2))
    turn_of = {chip: at for at, chip in enumerate(visit)}

    def along(rank, by):
        return visit[(turn_of[rank // 4] + by) % ring] * 4 + rank % 4

    ring_next = [(i, along(i, 1)) for i in range(ranks)]
    both_axes = ("grp", "ep")

    def turn(by):
        return [(g, (g + by) % groups) for g in range(groups)]

    slots = subtree_moves.shape[2]
    pieces = block_size // 2
    outgoing = pl.pallas_call(
        functools.partial(pick_kernel, pieces),
        out_shape=jax.ShapeDtypeStruct((ranks, slots * pieces, 2 * width), BF16),
        in_specs=[ANY] * 2,
        scratch_shapes=[
            VMEM((slots, ranks), jnp.int32),
            VMEM(latent_cache.shape, BF16),
            VMEM((pieces * resident, 2 * width), BF16),
            pltpu.SemaphoreType.DMA((2,)),
        ],
        compiler_params=pltpu.CompilerParams(vmem_limit_bytes=60 * 2**20),
        cost_estimate=cost(0, 4 * 2**20),
        name="pick",
    )(subtree_moves[0].T, latent_cache)
    arrived = lax.all_to_all(outgoing, "ep", split_axis=0, concat_axis=0, tiled=True)

    place = jnp.arange(table_len, dtype=jnp.int32)
    usable = jnp.clip(lengths[:, None] - place[None, :] * block_size, 0, block_size)
    blocks = jnp.arange(resident + ranks * slots, dtype=jnp.int32)
    limit = jnp.sum(
        jnp.where(block_table[:, :, None] == blocks[None, None, :], usable[:, :, None], 0), axis=1
    )
    token = jnp.arange(block_size, dtype=jnp.int32)
    row = jnp.arange(row_count, dtype=jnp.int32)
    fresh = jnp.arange(steps * requests, dtype=jnp.int32)
    fresh_open = ((row // steps)[:, None] == (fresh % requests)[None, :]) & (
        (fresh // requests)[None, :] <= (row % steps)[:, None]
    )
    near_open = (limit[:, None, :resident] > token[None, :, None]).reshape(requests, -1)
    near_open = jnp.concatenate([jnp.repeat(near_open, steps, axis=0), fresh_open], axis=1)
    near_bias = jnp.where(near_open, 0.0, HIDDEN).astype(F32)
    by_key = jnp.repeat(limit[:, resident:], pieces, axis=1)
    at_token = 2 * (jnp.arange(ranks * slots * pieces, dtype=jnp.int32) % pieces)
    moved_open = jnp.concatenate([by_key > at_token[None], by_key > at_token[None] + 1], axis=1)
    moved_bias = jnp.repeat(jnp.where(moved_open, 0.0, HIDDEN).astype(F32), steps, axis=0)

    padded = -(-width // 128) * 128
    query_rows = head_count * row_count
    dims = (head_count, nope_dim, latent, rope, block_size, steps)
    query, mixed = pl.pallas_call(
        functools.partial(resident_kernel, dims),
        out_shape=(
            jax.ShapeDtypeStruct((query_rows, padded), BF16),
            jax.ShapeDtypeStruct((query_rows, latent + 128), F32),
        ),
        scratch_shapes=[VMEM((near_bias.shape[1], padded), BF16)],
        compiler_params=pltpu.CompilerParams(vmem_limit_bytes=16 * 2**20),
        cost_estimate=cost(query_rows * near_bias.shape[1] * (padded + latent), 8 * 2**20),
        name="attend_resident",
    )(query_nope, query_rope, new_latent, latent_cache, key_absorb, near_bias)
    share = pl.pallas_call(
        functools.partial(moved_kernel, dims),
        out_shape=jax.ShapeDtypeStruct((row_count, model), BF16),
        in_specs=[ANY] * 6,
        scratch_shapes=[
            VMEM(arrived.shape, BF16),
            VMEM(query.shape, BF16),
            VMEM(moved_bias.shape, F32),
            VMEM(mixed.shape, F32),
            VMEM(value_absorb.shape, BF16),
            VMEM(output_proj.shape, BF16),
            VMEM((moved_bias.shape[1], padded), BF16),
            VMEM((row_count, head_count * value_absorb.shape[2]), BF16),
            pltpu.SemaphoreType.DMA((6,)),
        ],
        compiler_params=pltpu.CompilerParams(vmem_limit_bytes=56 * 2**20),
        cost_estimate=cost(query_rows * moved_bias.shape[1] * (padded + latent), 10 * 2**20),
        name="attend_moved",
    )(arrived, query, moved_bias, mixed, value_absorb, output_proj)
    shares = [lax.ppermute(share, "grp", turn(by)) for by in range(1, groups)]

    held = [jnp.swapaxes(expert_gate[0], 0, 1), jnp.swapaxes(expert_up[0], 0, 1), expert_down[0]]
    gate_rows, up_rows, down_rows = pl.pallas_call(
        load_kernel,
        out_shape=[jax.ShapeDtypeStruct(array.shape, BF16) for array in held],
        in_specs=[ANY] * 4,
        out_specs=[WHOLE] * 3,
        scratch_shapes=[pltpu.SemaphoreType.DMA((3,))],
        compiler_params=pltpu.CompilerParams(vmem_limit_bytes=44 * 2**20),
        cost_estimate=cost(0, 12 * 2**20),
        name="load",
    )(share, *held)

    extra = -(-2 * experts // 128) * 128
    columns = model // groups
    state, packet = pl.pallas_call(
        functools.partial(norm_kernel, experts),
        out_shape=(
            jax.ShapeDtypeStruct((row_count, columns), F32),
            jax.ShapeDtypeStruct((row_count, model + extra), BF16),
        ),
        in_specs=[ANY] * 3 + [WHOLE] * (2 + groups),
        scratch_shapes=[
            VMEM((row_count, model), BF16),
            VMEM((row_count, model), BF16),
            VMEM((row_count, model), F32),
            pltpu.SemaphoreType.DMA((2,)),
        ],
        compiler_params=pltpu.CompilerParams(vmem_limit_bytes=16 * 2**20),
        cost_estimate=cost(row_count * model * 128, 4 * 2**20),
        name="norm",
    )(share, hidden_in, down_rows, norm_gain[None, :], router_proj.T, expert_ids.T, *shares)

    def run_expert(rows, after, run_after, back=1):
        half = len(rows) * row_count
        here = pl.pallas_call(
            pack_kernel,
            out_shape=jax.ShapeDtypeStruct((half, model + extra), BF16),
            in_specs=[ANY] + [WHOLE] * len(rows),
            compiler_params=pltpu.CompilerParams(vmem_limit_bytes=16 * 2**20),
            cost_estimate=cost(0, 2 * half * model * 2),
            name="pack",
        )(after, *rows)
        across = lax.ppermute(here, "ep", core_swap)
        near, *far = pl.pallas_call(
            functools.partial(expert_kernel, experts),
            out_shape=[
                jax.ShapeDtypeStruct((half // cuts, model), BF16) for cuts in [1] + [back] * back
            ],
            in_specs=[ANY] + [WHOLE] * 5,
            compiler_params=pltpu.CompilerParams(vmem_limit_bytes=24 * 2**20),
            cost_estimate=cost(6 * half * model * gate_rows.shape[0], 12 * 2**20),
            name="expert",
        )(run_after, here, across, gate_rows, up_rows, down_rows)
        return near, [lax.ppermute(part, "ep", core_swap) for part in far]

    def join(near, back, types, first=0, after=()):
        return pl.pallas_call(
            functools.partial(join_kernel, first, len(back), len(after)),
            out_shape=[jax.ShapeDtypeStruct((row_count, model), kind) for kind in types],
            in_specs=[WHOLE] + [ANY] * len(after) + [WHOLE] * len(back),
            compiler_params=pltpu.CompilerParams(vmem_limit_bytes=16 * 2**20),
            cost_estimate=cost(row_count * model, 2**20),
            name="join",
        )(near, *after, *back)

    def send(value, axes, pairs):
        return lax.ppermute(value.astype(BF16), axes, pairs).astype(F32)

    if ring == 4 and groups == 2:
        def ring_step(sign):
            return [
                (g * ranks + i, g * ranks + along(i, sign * (1 - 2 * g)))
                for g in range(2)
                for i in range(ranks)
            ]

        onward, backward, plane_swap = ring_step(1), ring_step(-1), [(0, 1), (1, 0)]
        near = lax.ppermute(packet, both_axes, onward)
        side = lax.ppermute(packet, "ep", side_swap)
        two = lax.ppermute(near, both_axes, onward)
        near_side = lax.ppermute(near, "ep", side_swap)
        far = lax.ppermute(near, "grp", plane_swap)
        two_side = lax.ppermute(two, "ep", side_swap)
        far_side = lax.ppermute(near_side, "grp", plane_swap)
        early = run_expert([packet, side, near], packet, packet)
        later = run_expert([far, near_side, two], early[0], packet)
        own_sum, side_sum, near_sum = join(*early, [F32, BF16, F32])
        side_in = lax.ppermute(side_sum, "ep", side_swap)
        last = run_expert([far_side, two_side], later[0], side_sum, 2)
        near_side_sum, two_sum = join(*later, [F32, F32], 1)
        far_side_sum, two_side_sum = join(*last, [BF16, BF16], 0, [side_in])
        far_side_in = lax.ppermute(far_side_sum, "grp", plane_swap)
        two_side_in = lax.ppermute(two_side_sum, "ep", side_swap)
        [near_side_sum] = join(near_side_sum, [far_side_in], [BF16])
        [two_sum] = join(two_sum, [two_side_in], [BF16])
        [far_sum] = join(*later, [BF16], 0, [far_side_in])
        far_in = lax.ppermute(far_sum, "grp", plane_swap)
        near_side_in = lax.ppermute(near_side_sum, "ep", side_swap)
        two_in = lax.ppermute(two_sum, both_axes, backward)
        part = (row_count, columns)

        def by_columns(kernel, first_type, *operands):
            return pl.pallas_call(
                kernel,
                out_shape=(
                    jax.ShapeDtypeStruct(part, first_type),
                    jax.ShapeDtypeStruct(part, BF16),
                ),
                compiler_params=pltpu.CompilerParams(vmem_limit_bytes=16 * 2**20),
                cost_estimate=cost(row_count * model, 2**20),
                name=kernel.__name__,
            )(*operands)

        def crossed(pairs):
            return [(source, (target + ranks) % (2 * ranks)) for source, target in pairs]

        base, own_other = by_columns(own_kernel, F32, state, own_sum, side_in)
        near_mine, near_other = by_columns(
            sum_kernel, BF16, near_sum, far_in, near_side_in, two_in
        )
        own_over = lax.ppermute(own_other, "grp", plane_swap)
        mine_in = lax.ppermute(near_mine, both_axes, backward)
        other_in = lax.ppermute(near_other, both_axes, crossed(backward))
        return pl.pallas_call(
            last_kernel,
            out_shape=jax.ShapeDtypeStruct(part, BF16),
            in_specs=[WHOLE] * 4,
            compiler_params=pltpu.CompilerParams(vmem_limit_bytes=16 * 2**20),
            cost_estimate=cost(0, 2**20),
            name="last",
        )(base, own_over, other_in, mine_in)

    line = [packet]
    for _ in range(1, ring):
        line.append(lax.ppermute(line[-1], "ep", ring_next))
    totals = []
    for part in line:
        sums = run_expert([lax.ppermute(part, "ep", side_swap), part], packet, packet)
        over, here = join(*sums, [BF16, F32])
        totals.append(here + send(over, "ep", side_swap))
    moving = totals[1 % ring]
    for hop in list(range(2, ring)) + [0]:
        moving = totals[hop] + send(moving, "ep", ring_next)

    result = state + lax.dynamic_slice_in_dim(moving, group * columns, columns, 1)
    for by in range(1, groups):
        to = (group + by) % groups
        part = lax.dynamic_slice_in_dim(moving, to * columns, columns, 1)
        result = result + send(part, "grp", turn(by))
    return result.astype(BF16)


def solution(mesh):
    in_specs = (
        P("ep", None),
        P("ep", "grp"),
        P("ep", "grp"),
        P("ep", None),
        P("ep", None),
        P("grp", None, None),
        P("grp", None, None),
        P("grp", None),
        P(),
        P(),
        P("ep", None),
        P("ep", None, "grp"),
        P("ep", None, "grp"),
        P("ep", "grp", None),
        P("ep", None),
        P("ep"),
        P("ep", None, None),
    )
    out_specs = P("ep", "grp")
    return jax.shard_map(local, mesh=mesh, in_specs=in_specs, out_specs=out_specs, check_vma=False)
```

```python
import functools

import jax
import jax.numpy as jnp
from jax import lax
from jax.experimental import pallas as pl
from jax.experimental.pallas import tpu as pltpu
from jax.sharding import PartitionSpec as P

F32 = jnp.float32
BF16 = jnp.bfloat16
HIDDEN = -1e30
VMEM = pltpu.VMEM
ANY = pl.BlockSpec(memory_space=pl.ANY)
WHOLE = pl.BlockSpec(memory_space=pltpu.VMEM)


def dot(a, b):
    return jnp.dot(a, b, preferred_element_type=F32)


def dot_rows(a, b):
    return lax.dot_general(a, b, (((1,), (1,)), ((), ())), preferred_element_type=F32)


def cost(products, moved_bytes):
    return pl.CostEstimate(flops=2 * products, bytes_accessed=moved_bytes, transcendentals=0)


def fetch_all(sources, buffers, sems):
    copies = []
    for at, (source, buffer) in enumerate(zip(sources, buffers)):
        copy = pltpu.make_async_copy(source, buffer, sems.at[at])
        copy.start()
        copies.append(copy)
    return copies


def lay_tokens(keys, start, ref, tokens, width):
    count = ref.shape[0]
    for token in range(tokens):
        keys[start : start + count, :width] = ref[:, token * width : (token + 1) * width]
        start += count
    return start


def pick_kernel(pieces, moves_any, cache_any, out_ref, moves_ref, cache, stacked, sems):
    got = fetch_all((moves_any, cache_any), (moves_ref, cache), sems)
    ranks, per_rank, wide = out_ref.shape
    slots = moves_ref.shape[0]
    resident = cache.shape[0]
    rows = ranks * per_rank
    row = lax.broadcasted_iota(jnp.int32, (rows, ranks), 0)
    rank = lax.broadcasted_iota(jnp.int32, (rows, ranks), 1)
    chosen = jnp.zeros((rows, ranks), jnp.int32)
    got[0].wait()
    for slot in range(slots):
        here = (row // per_rank == rank) & (row % per_rank // pieces == slot)
        chosen = chosen + jnp.where(here, moves_ref[slot : slot + 1, :], 0)
    block = jnp.clip(jnp.sum(chosen, axis=1, keepdims=True), 0, resident - 1)
    at = lax.broadcasted_iota(jnp.int32, (rows, pieces * resident), 0)
    source = lax.broadcasted_iota(jnp.int32, (rows, pieces * resident), 1)
    pick = (source // resident == at % pieces) & (source % resident == block)
    got[1].wait()
    for piece in range(pieces):
        stacked[piece * resident : (piece + 1) * resident, :] = cache[:, piece * wide : (piece + 1) * wide]
    picked = dot(pick.astype(F32).astype(BF16), stacked[...]).astype(BF16)
    out_ref[...] = picked.reshape(ranks, per_rank, wide)


def resident_kernel(
    dims, nope, rope_rows, fresh, cache, absorb, bias_ref,
    query_ref, mixed_ref,
    keys,
):
    head_count, nope_dim, latent, rope, block_size, steps = dims
    width = latent + rope
    rows = nope.shape[0]
    padding = keys.shape[1] - width
    keys[:, latent:] = jnp.zeros((keys.shape[0], keys.shape[1] - latent), BF16)
    start = lay_tokens(keys, 0, cache, block_size, width)
    lay_tokens(keys, start, fresh, steps, width)
    for head in range(head_count):
        q_latent = dot(nope[:, head * nope_dim : (head + 1) * nope_dim], absorb[head])
        q_rope = rope_rows[:, head * rope : (head + 1) * rope]
        fill = jnp.zeros((rows, padding), BF16)
        query_ref[head * rows : (head + 1) * rows, :] = jnp.concatenate(
            [q_latent.astype(BF16), q_rope, fill], axis=1
        )
    scale = (nope_dim + rope) ** (-0.5)
    part = min(4, head_count) * rows
    for first in range(0, head_count * rows, part):
        score = dot_rows(query_ref[first : first + part, :], keys[...])
        score = score.reshape(part // rows, rows, -1) * scale + bias_ref[...][None]
        score = score.reshape(part, -1)
        peak = jnp.max(score, axis=1, keepdims=True)
        weight = jnp.exp(score - peak)
        total = jnp.sum(weight, axis=1, keepdims=True)
        mixed_ref[first : first + part, :latent] = dot(weight.astype(BF16), keys[:, :latent])
        lane = lax.broadcasted_iota(jnp.int32, (part, 128), 1)
        mixed_ref[first : first + part, latent:] = jnp.where(lane < 64, peak, total)


def moved_kernel(
    dims, moved_any, query_any, bias_any, mixed_any, value_any, proj_any,
    share_ref,
    moved, query, bias, mixed, value, proj, keys, heads_out, sems,
):
    head_count, nope_dim, latent, rope, block_size, steps = dims
    width = latent + rope
    rows = heads_out.shape[0]
    got = fetch_all(
        (moved_any, query_any, bias_any, mixed_any, value_any, proj_any),
        (moved, query, bias, mixed, value, proj),
        sems,
    )
    keys[:, latent:] = jnp.zeros((keys.shape[0], keys.shape[1] - latent), BF16)
    scale = (nope_dim + rope) ** (-0.5)
    value_dim = value.shape[2]
    got[0].wait()
    count = moved.shape[0] * moved.shape[1]
    for half in range(2):
        part = moved[:, :, half * width : (half + 1) * width]
        keys[half * count : (half + 1) * count, :width] = part.reshape(count, width)
    got[1].wait()
    got[2].wait()
    group = min(4, head_count)
    for first in range(0, head_count, group):
        at = slice(first * rows, (first + group) * rows)
        score = dot_rows(query[at, :], keys[...])
        score = score.reshape(group, rows, -1) * scale + bias[...][None]
        score = score.reshape(group * rows, -1)
        if first == 0:
            got[3].wait()
        before = mixed[at, latent : latent + 1]
        peak = jnp.maximum(jnp.max(score, axis=1, keepdims=True), before)
        weight = jnp.exp(score - peak)
        keep = jnp.exp(before - peak)
        total = jnp.sum(weight, axis=1, keepdims=True) + mixed[at, latent + 64 : latent + 65] * keep
        joined = dot(weight.astype(BF16), keys[:, :latent]) + mixed[at, :latent] * keep
        joined = (joined / total).astype(BF16)
        if first == 0:
            got[4].wait()
        for head in range(first, first + group):
            own = joined[(head - first) * rows : (head - first + 1) * rows]
            heads_out[:, head * value_dim : (head + 1) * value_dim] = dot(own, value[head]).astype(BF16)
    got[5].wait()
    share_ref[...] = dot(heads_out[...], proj[...]).astype(BF16)


def own_columns(ref, shift):
    groups = lax.axis_size("grp")
    columns = ref.shape[1] // groups
    first = (lax.axis_index("grp") + shift) % groups * columns
    return ref[:, pl.ds(pl.multiple_of(first, 128), columns)]


def norm_kernel(experts, own_any, hidden_any, loaded_any, gain_ref, router_ref, ids_ref, *refs):
    parts, (state_ref, packet_ref, own, hidden, whole, sems) = refs[:-6], refs[-6:]
    got = fetch_all((own_any, hidden_any), (own, hidden), sems)
    rows, model = hidden.shape
    state = parts[0][...].astype(F32)
    for part in parts[1:]:
        state = state + part[...].astype(F32)
    for copy in got:
        copy.wait()
    state = state + own[...].astype(F32) + hidden[...].astype(F32)
    whole[...] = state
    state_ref[...] = own_columns(whole, 0)
    square = jnp.mean(state * state, axis=1, keepdims=True)
    normed = (state * lax.rsqrt(square + 1e-06) * gain_ref[...].astype(F32)).astype(BF16)
    packet_ref[:, :model] = normed
    logits = dot_rows(router_ref[...], normed)
    names = lax.broadcasted_iota(jnp.int32, (experts, rows), 0)
    named = names == ids_ref[0:1, :]
    for k in range(1, ids_ref.shape[0]):
        named = named | (names == ids_ref[k : k + 1, :])
    chosen = jnp.where(named, jax.nn.sigmoid(logits), 0.0)
    weight = chosen / jnp.sum(chosen, axis=0, keepdims=True)
    high = weight.astype(BF16)
    low = (weight - high.astype(F32)).astype(BF16)
    extra = packet_ref.shape[1] - model
    both = jnp.concatenate([high, low], axis=0)
    place = lax.broadcasted_iota(jnp.int32, (2 * experts, extra), 0)
    lane = lax.broadcasted_iota(jnp.int32, (2 * experts, extra), 1)
    turned = lax.dot_general(
        both, (place == lane).astype(BF16), (((0,), (0,)), ((), ())), preferred_element_type=F32
    )
    packet_ref[:, model:] = turned.astype(BF16)


def load_kernel(after_any, gate_any, up_any, down_any, gate_ref, up_ref, down_ref, sems):
    sources, targets = (gate_any, up_any, down_any), (gate_ref, up_ref, down_ref)
    for copy in fetch_all(sources, targets, sems):
        copy.wait()


def pack_kernel(after_any, *refs):
    count = refs[0].shape[0]
    for at, ref in enumerate(refs[:-1]):
        refs[-1][at * count : (at + 1) * count, :] = ref[...]


def expert_kernel(experts, after_any, here_ref, across_ref, gate_ref, up_ref, down_ref, *out_refs):
    near_ref, *far_refs = out_refs
    model = gate_ref.shape[1]
    packet = jnp.concatenate([here_ref[...], across_ref[...]], axis=0)
    rows = packet[:, :model]
    extra = packet[:, model:].astype(F32)
    names = lax.broadcasted_iota(jnp.int32, extra.shape, 1)
    me = lax.axis_index("ep")
    mine = (names == me) | (names == me + experts)
    weight = jnp.sum(jnp.where(mine, extra, 0.0), axis=1, keepdims=True)
    gate = dot_rows(rows, gate_ref[...])
    up = dot_rows(rows, up_ref[...])
    inner = (gate * jax.nn.sigmoid(gate) * up * weight).astype(BF16)
    result = dot(inner, down_ref[...]).astype(BF16)
    half = near_ref.shape[0]
    near_ref[...] = result[:half]
    height = half // len(far_refs)
    for at, far_ref in enumerate(far_refs):
        far_ref[...] = result[half + at * height : half + (at + 1) * height]


def join_kernel(first, back_count, after_count, near_ref, *refs):
    back_refs, out_refs = refs[after_count : after_count + back_count], refs[after_count + back_count :]
    count = out_refs[0].shape[0]
    height = back_refs[0].shape[0]
    step = min(count, height)
    for at, ref in enumerate(out_refs, first):
        for row in range(at * count, (at + 1) * count, step):
            back = back_refs[row // height][row % height : row % height + step, :].astype(F32)
            total = near_ref[row : row + step, :].astype(F32) + back
            ref[row - at * count : row - at * count + step, :] = total.astype(ref.dtype)


def own_kernel(after_any, state_ref, own_ref, side_ref, base_ref, other_ref):
    mine, other = (own_columns(own_ref, by) + own_columns(side_ref, by).astype(F32) for by in (0, 1))
    base_ref[...] = state_ref[...] + mine
    other_ref[...] = other.astype(BF16)


def last_kernel(base_ref, *refs):
    total = base_ref[...]
    for ref in refs[:-1]:
        total = total + ref[...].astype(F32)
    refs[-1][...] = total.astype(BF16)


def sum_kernel(*refs):
    parts, (mine_ref, other_ref) = refs[:-2], refs[-2:]
    for shift, ref in ((0, mine_ref), (1, other_ref)):
        total = own_columns(parts[0], shift).astype(F32)
        for part in parts[1:]:
            total = total + own_columns(part, shift).astype(F32)
        ref[...] = total.astype(BF16)


def local(
    hidden_in,
    query_nope,
    query_rope,
    new_latent,
    latent_cache,
    key_absorb,
    value_absorb,
    output_proj,
    norm_gain,
    router_proj,
    expert_ids,
    expert_gate,
    expert_up,
    expert_down,
    block_table,
    lengths,
    subtree_moves,
):
    head_count, nope_dim, latent = key_absorb.shape
    rope = query_rope.shape[1] // head_count
    width = latent + rope
    requests, table_len = block_table.shape
    steps = new_latent.shape[1] // width
    row_count, model = hidden_in.shape
    block_size = latent_cache.shape[1] // width
    resident = latent_cache.shape[0]
    experts = router_proj.shape[1]
    groups = lax.axis_size("grp")
    group = lax.axis_index("grp")
    ranks = lax.axis_size("ep")
    me = lax.axis_index("ep")
    ring = ranks // 4
    core_swap = [(i, i ^ 1) for i in range(ranks)]
    side_swap = [(i, i ^ 2) for i in range(ranks)]
    visit = list(range(0, ring, 2)) + list(range(ring - 1 - ring % 2, 0, -2))
    turn_of = {chip: at for at, chip in enumerate(visit)}

    def along(rank, by):
        return visit[(turn_of[rank // 4] + by) % ring] * 4 + rank % 4

    ring_next = [(i, along(i, 1)) for i in range(ranks)]
    both_axes = ("grp", "ep")

    def turn(by):
        return [(g, (g + by) % groups) for g in range(groups)]

    slots = subtree_moves.shape[2]
    pieces = block_size // 2
    outgoing = pl.pallas_call(
        functools.partial(pick_kernel, pieces),
        out_shape=jax.ShapeDtypeStruct((ranks, slots * pieces, 2 * width), BF16),
        in_specs=[ANY] * 2,
        scratch_shapes=[
            VMEM((slots, ranks), jnp.int32),
            VMEM(latent_cache.shape, BF16),
            VMEM((pieces * resident, 2 * width), BF16),
            pltpu.SemaphoreType.DMA((2,)),
        ],
        compiler_params=pltpu.CompilerParams(vmem_limit_bytes=60 * 2**20),
        cost_estimate=cost(0, 4 * 2**20),
        name="pick",
    )(subtree_moves[0].T, latent_cache)
    arrived = lax.all_to_all(outgoing, "ep", split_axis=0, concat_axis=0, tiled=True)

    place = jnp.arange(table_len, dtype=jnp.int32)
    usable = jnp.clip(lengths[:, None] - place[None, :] * block_size, 0, block_size)
    blocks = jnp.arange(resident + ranks * slots, dtype=jnp.int32)
    limit = jnp.sum(
        jnp.where(block_table[:, :, None] == blocks[None, None, :], usable[:, :, None], 0), axis=1
    )
    token = jnp.arange(block_size, dtype=jnp.int32)
    row = jnp.arange(row_count, dtype=jnp.int32)
    fresh = jnp.arange(steps * requests, dtype=jnp.int32)
    fresh_open = ((row // steps)[:, None] == (fresh % requests)[None, :]) & (
        (fresh // requests)[None, :] <= (row % steps)[:, None]
    )
    near_open = (limit[:, None, :resident] > token[None, :, None]).reshape(requests, -1)
    near_open = jnp.concatenate([jnp.repeat(near_open, steps, axis=0), fresh_open], axis=1)
    near_bias = jnp.where(near_open, 0.0, HIDDEN).astype(F32)
    by_key = jnp.repeat(limit[:, resident:], pieces, axis=1)
    at_token = 2 * (jnp.arange(ranks * slots * pieces, dtype=jnp.int32) % pieces)
    moved_open = jnp.concatenate([by_key > at_token[None], by_key > at_token[None] + 1], axis=1)
    moved_bias = jnp.repeat(jnp.where(moved_open, 0.0, HIDDEN).astype(F32), steps, axis=0)

    padded = -(-width // 128) * 128
    query_rows = head_count * row_count
    dims = (head_count, nope_dim, latent, rope, block_size, steps)
    query, mixed = pl.pallas_call(
        functools.partial(resident_kernel, dims),
        out_shape=(
            jax.ShapeDtypeStruct((query_rows, padded), BF16),
            jax.ShapeDtypeStruct((query_rows, latent + 128), F32),
        ),
        scratch_shapes=[VMEM((near_bias.shape[1], padded), BF16)],
        compiler_params=pltpu.CompilerParams(vmem_limit_bytes=16 * 2**20),
        cost_estimate=cost(query_rows * near_bias.shape[1] * (padded + latent), 8 * 2**20),
        name="attend_resident",
    )(query_nope, query_rope, new_latent, latent_cache, key_absorb, near_bias)
    share = pl.pallas_call(
        functools.partial(moved_kernel, dims),
        out_shape=jax.ShapeDtypeStruct((row_count, model), BF16),
        in_specs=[ANY] * 6,
        scratch_shapes=[
            VMEM(arrived.shape, BF16),
            VMEM(query.shape, BF16),
            VMEM(moved_bias.shape, F32),
            VMEM(mixed.shape, F32),
            VMEM(value_absorb.shape, BF16),
            VMEM(output_proj.shape, BF16),
            VMEM((moved_bias.shape[1], padded), BF16),
            VMEM((row_count, head_count * value_absorb.shape[2]), BF16),
            pltpu.SemaphoreType.DMA((6,)),
        ],
        compiler_params=pltpu.CompilerParams(vmem_limit_bytes=56 * 2**20),
        cost_estimate=cost(query_rows * moved_bias.shape[1] * (padded + latent), 10 * 2**20),
        name="attend_moved",
    )(arrived, query, moved_bias, mixed, value_absorb, output_proj)
    shares = [lax.ppermute(share, "grp", turn(by)) for by in range(1, groups)]

    held = [jnp.swapaxes(expert_gate[0], 0, 1), jnp.swapaxes(expert_up[0], 0, 1), expert_down[0]]
    gate_rows, up_rows, down_rows = pl.pallas_call(
        load_kernel,
        out_shape=[jax.ShapeDtypeStruct(array.shape, BF16) for array in held],
        in_specs=[ANY] * 4,
        out_specs=[WHOLE] * 3,
        scratch_shapes=[pltpu.SemaphoreType.DMA((3,))],
        compiler_params=pltpu.CompilerParams(vmem_limit_bytes=44 * 2**20),
        cost_estimate=cost(0, 12 * 2**20),
        name="load",
    )(share, *held)

    extra = -(-2 * experts // 128) * 128
    columns = model // groups
    state, packet = pl.pallas_call(
        functools.partial(norm_kernel, experts),
        out_shape=(
            jax.ShapeDtypeStruct((row_count, columns), F32),
            jax.ShapeDtypeStruct((row_count, model + extra), BF16),
        ),
        in_specs=[ANY] * 3 + [WHOLE] * (2 + groups),
        scratch_shapes=[
            VMEM((row_count, model), BF16),
            VMEM((row_count, model), BF16),
            VMEM((row_count, model), F32),
            pltpu.SemaphoreType.DMA((2,)),
        ],
        compiler_params=pltpu.CompilerParams(vmem_limit_bytes=16 * 2**20),
        cost_estimate=cost(row_count * model * 128, 4 * 2**20),
        name="norm",
    )(share, hidden_in, down_rows, norm_gain[None, :], router_proj.T, expert_ids.T, *shares)

    def run_expert(rows, after, run_after, back=1):
        half = len(rows) * row_count
        here = pl.pallas_call(
            pack_kernel,
            out_shape=jax.ShapeDtypeStruct((half, model + extra), BF16),
            in_specs=[ANY] + [WHOLE] * len(rows),
            compiler_params=pltpu.CompilerParams(vmem_limit_bytes=16 * 2**20),
            cost_estimate=cost(0, 2 * half * model * 2),
            name="pack",
        )(after, *rows)
        across = lax.ppermute(here, "ep", core_swap)
        near, *far = pl.pallas_call(
            functools.partial(expert_kernel, experts),
            out_shape=[
                jax.ShapeDtypeStruct((half // cuts, model), BF16) for cuts in [1] + [back] * back
            ],
            in_specs=[ANY] + [WHOLE] * 5,
            compiler_params=pltpu.CompilerParams(vmem_limit_bytes=24 * 2**20),
            cost_estimate=cost(6 * half * model * gate_rows.shape[0], 12 * 2**20),
            name="expert",
        )(run_after, here, across, gate_rows, up_rows, down_rows)
        return near, [lax.ppermute(part, "ep", core_swap) for part in far]

    def join(near, back, types, first=0, after=()):
        return pl.pallas_call(
            functools.partial(join_kernel, first, len(back), len(after)),
            out_shape=[jax.ShapeDtypeStruct((row_count, model), kind) for kind in types],
            in_specs=[WHOLE] + [ANY] * len(after) + [WHOLE] * len(back),
            compiler_params=pltpu.CompilerParams(vmem_limit_bytes=16 * 2**20),
            cost_estimate=cost(row_count * model, 2**20),
            name="join",
        )(near, *after, *back)

    def send(value, axes, pairs):
        return lax.ppermute(value.astype(BF16), axes, pairs).astype(F32)

    if ring == 4 and groups == 2:
        def ring_step(sign):
            return [
                (g * ranks + i, g * ranks + along(i, sign * (1 - 2 * g)))
                for g in range(2)
                for i in range(ranks)
            ]

        onward, backward, plane_swap = ring_step(1), ring_step(-1), [(0, 1), (1, 0)]
        near = lax.ppermute(packet, both_axes, onward)
        side = lax.ppermute(packet, "ep", side_swap)
        two = lax.ppermute(near, both_axes, onward)
        near_side = lax.ppermute(near, "ep", side_swap)
        far = lax.ppermute(near, "grp", plane_swap)
        two_side = lax.ppermute(two, "ep", side_swap)
        far_side = lax.ppermute(near_side, "grp", plane_swap)
        early = run_expert([packet, side, near], packet, packet)
        later = run_expert([far, near_side, two], early[0], packet)
        own_sum, side_sum, near_sum = join(*early, [F32, BF16, F32])
        side_in = lax.ppermute(side_sum, "ep", side_swap)
        last = run_expert([far_side, two_side], later[0], side_sum, 2)
        near_side_sum, two_sum = join(*later, [F32, F32], 1)
        far_side_sum, two_side_sum = join(*last, [BF16, BF16], 0, [side_in])
        far_side_in = lax.ppermute(far_side_sum, "grp", plane_swap)
        two_side_in = lax.ppermute(two_side_sum, "ep", side_swap)
        [near_side_sum] = join(near_side_sum, [far_side_in], [BF16])
        [two_sum] = join(two_sum, [two_side_in], [BF16])
        [far_sum] = join(*later, [BF16], 0, [far_side_in])
        far_in = lax.ppermute(far_sum, "grp", plane_swap)
        near_side_in = lax.ppermute(near_side_sum, "ep", side_swap)
        two_in = lax.ppermute(two_sum, both_axes, backward)
        part = (row_count, columns)

        def by_columns(kernel, first_type, after_count, *operands):
            return pl.pallas_call(
                kernel,
                out_shape=(
                    jax.ShapeDtypeStruct(part, first_type),
                    jax.ShapeDtypeStruct(part, BF16),
                ),
                in_specs=[ANY] * after_count + [WHOLE] * (len(operands) - after_count),
                compiler_params=pltpu.CompilerParams(vmem_limit_bytes=16 * 2**20),
                cost_estimate=cost(row_count * model, 2**20),
                name=kernel.__name__,
            )(*operands)

        def crossed(pairs):
            return [(source, (target + ranks) % (2 * ranks)) for source, target in pairs]

        near_mine, near_other = by_columns(
            sum_kernel, BF16, 0, near_sum, near_side_in, two_in, far_in
        )
        base, own_other = by_columns(own_kernel, F32, 1, near_mine, state, own_sum, side_in)
        own_over = lax.ppermute(own_other, "grp", plane_swap)
        mine_in = lax.ppermute(near_mine, both_axes, backward)
        other_in = lax.ppermute(near_other, both_axes, crossed(backward))
        return pl.pallas_call(
            last_kernel,
            out_shape=jax.ShapeDtypeStruct(part, BF16),
            in_specs=[WHOLE] * 4,
            compiler_params=pltpu.CompilerParams(vmem_limit_bytes=16 * 2**20),
            cost_estimate=cost(0, 2**20),
            name="last",
        )(base, other_in, mine_in, own_over)

    line = [packet]
    for _ in range(1, ring):
        line.append(lax.ppermute(line[-1], "ep", ring_next))
    totals = []
    for part in line:
        sums = run_expert([lax.ppermute(part, "ep", side_swap), part], packet, packet)
        over, here = join(*sums, [BF16, F32])
        totals.append(here + send(over, "ep", side_swap))
    moving = totals[1 % ring]
    for hop in list(range(2, ring)) + [0]:
        moving = totals[hop] + send(moving, "ep", ring_next)

    result = state + lax.dynamic_slice_in_dim(moving, group * columns, columns, 1)
    for by in range(1, groups):
        to = (group + by) % groups
        part = lax.dynamic_slice_in_dim(moving, to * columns, columns, 1)
        result = result + send(part, "grp", turn(by))
    return result.astype(BF16)


def solution(mesh):
    in_specs = (
        P("ep", None),
        P("ep", "grp"),
        P("ep", "grp"),
        P("ep", None),
        P("ep", None),
        P("grp", None, None),
        P("grp", None, None),
        P("grp", None),
        P(),
        P(),
        P("ep", None),
        P("ep", None, "grp"),
        P("ep", None, "grp"),
        P("ep", "grp", None),
        P("ep", None),
        P("ep"),
        P("ep", None, None),
    )
    out_specs = P("ep", "grp")
    return jax.shard_map(local, mesh=mesh, in_specs=in_specs, out_specs=out_specs, check_vma=False)
```

```python
import functools

import jax
import jax.numpy as jnp
from jax import lax
from jax.experimental import pallas as pl
from jax.experimental.pallas import tpu as pltpu
from jax.sharding import PartitionSpec as P

F32 = jnp.float32
BF16 = jnp.bfloat16
HIDDEN = -1e30
VMEM = pltpu.VMEM
ANY = pl.BlockSpec(memory_space=pl.ANY)
WHOLE = pl.BlockSpec(memory_space=pltpu.VMEM)


def dot(a, b):
    return jnp.dot(a, b, preferred_element_type=F32)


def dot_rows(a, b):
    return lax.dot_general(a, b, (((1,), (1,)), ((), ())), preferred_element_type=F32)


def cost(products, moved_bytes):
    return pl.CostEstimate(flops=2 * products, bytes_accessed=moved_bytes, transcendentals=0)


def fetch_all(sources, buffers, sems):
    copies = []
    for at, (source, buffer) in enumerate(zip(sources, buffers)):
        copy = pltpu.make_async_copy(source, buffer, sems.at[at])
        copy.start()
        copies.append(copy)
    return copies


def lay_tokens(keys, start, ref, tokens, width):
    count = ref.shape[0]
    for token in range(tokens):
        keys[start : start + count, :width] = ref[:, token * width : (token + 1) * width]
        start += count
    return start


def pick_kernel(pieces, moves_any, cache_any, out_ref, moves_ref, cache, stacked, sems):
    got = fetch_all((moves_any, cache_any), (moves_ref, cache), sems)
    ranks, per_rank, wide = out_ref.shape
    slots = moves_ref.shape[0]
    resident = cache.shape[0]
    rows = ranks * per_rank
    row = lax.broadcasted_iota(jnp.int32, (rows, ranks), 0)
    rank = lax.broadcasted_iota(jnp.int32, (rows, ranks), 1)
    chosen = jnp.zeros((rows, ranks), jnp.int32)
    got[0].wait()
    for slot in range(slots):
        here = (row // per_rank == rank) & (row % per_rank // pieces == slot)
        chosen = chosen + jnp.where(here, moves_ref[slot : slot + 1, :], 0)
    block = jnp.clip(jnp.sum(chosen, axis=1, keepdims=True), 0, resident - 1)
    at = lax.broadcasted_iota(jnp.int32, (rows, pieces * resident), 0)
    source = lax.broadcasted_iota(jnp.int32, (rows, pieces * resident), 1)
    pick = (source // resident == at % pieces) & (source % resident == block)
    got[1].wait()
    for piece in range(pieces):
        stacked[piece * resident : (piece + 1) * resident, :] = cache[:, piece * wide : (piece + 1) * wide]
    picked = dot(pick.astype(F32).astype(BF16), stacked[...]).astype(BF16)
    out_ref[...] = picked.reshape(ranks, per_rank, wide)


def resident_kernel(
    dims, nope, rope_rows, fresh, cache, absorb, value, bias_ref,
    query_ref, mixed_ref,
    keys,
):
    head_count, nope_dim, latent, rope, block_size, steps = dims
    width = latent + rope
    rows = nope.shape[0]
    padding = keys.shape[1] - width
    keys[:, latent:] = jnp.zeros((keys.shape[0], keys.shape[1] - latent), BF16)
    start = lay_tokens(keys, 0, cache, block_size, width)
    lay_tokens(keys, start, fresh, steps, width)
    for head in range(head_count):
        q_latent = dot(nope[:, head * nope_dim : (head + 1) * nope_dim], absorb[head])
        q_rope = rope_rows[:, head * rope : (head + 1) * rope]
        fill = jnp.zeros((rows, padding), BF16)
        query_ref[head * rows : (head + 1) * rows, :] = jnp.concatenate(
            [q_latent.astype(BF16), q_rope, fill], axis=1
        )
    scale = (nope_dim + rope) ** (-0.5)
    part = min(4, head_count) * rows
    for first in range(0, head_count * rows, part):
        score = dot_rows(query_ref[first : first + part, :], keys[...])
        score = score.reshape(part // rows, rows, -1) * scale + bias_ref[...][None]
        score = score.reshape(part, -1)
        peak = jnp.max(score, axis=1, keepdims=True)
        weight = jnp.exp(score - peak)
        total = jnp.sum(weight, axis=1, keepdims=True)
        mixed = dot(weight.astype(BF16), keys[:, :latent]).astype(BF16)
        value_dim = value.shape[2]
        for at in range(0, part, rows):
            here = slice(first + at, first + at + rows)
            mixed_ref[here, :value_dim] = dot(mixed[at : at + rows], value[(first + at) // rows])
        lane = lax.broadcasted_iota(jnp.int32, (part, 128), 1)
        mixed_ref[first : first + part, value_dim:] = jnp.where(lane < 64, peak, total)


def moved_kernel(
    dims, moved_any, query_any, bias_any, mixed_any, value_any, proj_any,
    share_ref,
    moved, query, bias, mixed, value, proj, keys, heads_out, sems,
):
    head_count, nope_dim, latent, rope, block_size, steps = dims
    width = latent + rope
    rows = heads_out.shape[0]
    got = fetch_all(
        (moved_any, query_any, bias_any, mixed_any, value_any, proj_any),
        (moved, query, bias, mixed, value, proj),
        sems,
    )
    keys[:, latent:] = jnp.zeros((keys.shape[0], keys.shape[1] - latent), BF16)
    scale = (nope_dim + rope) ** (-0.5)
    value_dim = value.shape[2]
    got[0].wait()
    count = moved.shape[0] * moved.shape[1]
    for half in range(2):
        part = moved[:, :, half * width : (half + 1) * width]
        keys[half * count : (half + 1) * count, :width] = part.reshape(count, width)
    got[1].wait()
    got[2].wait()
    group = min(4, head_count)
    for first in range(0, head_count, group):
        at = slice(first * rows, (first + group) * rows)
        score = dot_rows(query[at, :], keys[...])
        score = score.reshape(group, rows, -1) * scale + bias[...][None]
        score = score.reshape(group * rows, -1)
        if first == 0:
            got[3].wait()
        before = mixed[at, value_dim : value_dim + 1]
        peak = jnp.maximum(jnp.max(score, axis=1, keepdims=True), before)
        weight = jnp.exp(score - peak)
        keep = jnp.exp(before - peak)
        total = jnp.sum(weight, axis=1, keepdims=True)
        total = total + mixed[at, value_dim + 64 : value_dim + 65] * keep
        joined = dot(weight.astype(BF16), keys[:, :latent]).astype(BF16)
        if first == 0:
            got[4].wait()
        for head in range(first, first + group):
            own = slice((head - first) * rows, (head - first + 1) * rows)
            both = dot(joined[own], value[head])
            both = both + mixed[head * rows : (head + 1) * rows, :value_dim] * keep[own]
            heads_out[:, head * value_dim : (head + 1) * value_dim] = (both / total[own]).astype(BF16)
    got[5].wait()
    share_ref[...] = dot(heads_out[...], proj[...]).astype(BF16)


def own_columns(ref, shift):
    groups = lax.axis_size("grp")
    columns = ref.shape[1] // groups
    first = (lax.axis_index("grp") + shift) % groups * columns
    return ref[:, pl.ds(pl.multiple_of(first, 128), columns)]


def norm_kernel(experts, own_any, hidden_any, loaded_any, gain_ref, router_ref, ids_ref, *refs):
    parts, (state_ref, packet_ref, own, hidden, whole, sems) = refs[:-6], refs[-6:]
    got = fetch_all((own_any, hidden_any), (own, hidden), sems)
    rows, model = hidden.shape
    state = parts[0][...].astype(F32)
    for part in parts[1:]:
        state = state + part[...].astype(F32)
    for copy in got:
        copy.wait()
    state = state + own[...].astype(F32) + hidden[...].astype(F32)
    whole[...] = state
    state_ref[...] = own_columns(whole, 0)
    square = jnp.mean(state * state, axis=1, keepdims=True)
    normed = (state * lax.rsqrt(square + 1e-06) * gain_ref[...].astype(F32)).astype(BF16)
    packet_ref[:, :model] = normed
    logits = dot_rows(router_ref[...], normed)
    names = lax.broadcasted_iota(jnp.int32, (experts, rows), 0)
    named = names == ids_ref[0:1, :]
    for k in range(1, ids_ref.shape[0]):
        named = named | (names == ids_ref[k : k + 1, :])
    chosen = jnp.where(named, jax.nn.sigmoid(logits), 0.0)
    weight = chosen / jnp.sum(chosen, axis=0, keepdims=True)
    high = weight.astype(BF16)
    low = (weight - high.astype(F32)).astype(BF16)
    extra = packet_ref.shape[1] - model
    both = jnp.concatenate([high, low], axis=0)
    place = lax.broadcasted_iota(jnp.int32, (2 * experts, extra), 0)
    lane = lax.broadcasted_iota(jnp.int32, (2 * experts, extra), 1)
    turned = lax.dot_general(
        both, (place == lane).astype(BF16), (((0,), (0,)), ((), ())), preferred_element_type=F32
    )
    packet_ref[:, model:] = turned.astype(BF16)


def load_kernel(after_any, gate_any, up_any, down_any, gate_ref, up_ref, down_ref, sems):
    sources, targets = (gate_any, up_any, down_any), (gate_ref, up_ref, down_ref)
    for copy in fetch_all(sources, targets, sems):
        copy.wait()


def pack_kernel(after_any, *refs):
    count = refs[0].shape[0]
    for at, ref in enumerate(refs[:-1]):
        refs[-1][at * count : (at + 1) * count, :] = ref[...]


def expert_kernel(experts, after_any, here_ref, across_ref, gate_ref, up_ref, down_ref, *out_refs):
    near_ref, *far_refs = out_refs
    model = gate_ref.shape[1]
    packet = jnp.concatenate([here_ref[...], across_ref[...]], axis=0)
    rows = packet[:, :model]
    extra = packet[:, model:].astype(F32)
    names = lax.broadcasted_iota(jnp.int32, extra.shape, 1)
    me = lax.axis_index("ep")
    mine = (names == me) | (names == me + experts)
    weight = jnp.sum(jnp.where(mine, extra, 0.0), axis=1, keepdims=True)
    gate = dot_rows(rows, gate_ref[...])
    up = dot_rows(rows, up_ref[...])
    inner = (gate * jax.nn.sigmoid(gate) * up * weight).astype(BF16)
    result = dot(inner, down_ref[...]).astype(BF16)
    half = near_ref.shape[0]
    near_ref[...] = result[:half]
    height = half // len(far_refs)
    for at, far_ref in enumerate(far_refs):
        far_ref[...] = result[half + at * height : half + (at + 1) * height]


def join_kernel(first, back_count, after_count, near_ref, *refs):
    back_refs, out_refs = refs[after_count : after_count + back_count], refs[after_count + back_count :]
    count = out_refs[0].shape[0]
    height = back_refs[0].shape[0]
    step = min(count, height)
    for at, ref in enumerate(out_refs, first):
        for row in range(at * count, (at + 1) * count, step):
            back = back_refs[row // height][row % height : row % height + step, :].astype(F32)
            total = near_ref[row : row + step, :].astype(F32) + back
            ref[row - at * count : row - at * count + step, :] = total.astype(ref.dtype)


def own_kernel(after_any, state_ref, own_ref, side_ref, base_ref, other_ref):
    mine, other = (own_columns(own_ref, by) + own_columns(side_ref, by).astype(F32) for by in (0, 1))
    base_ref[...] = state_ref[...] + mine
    other_ref[...] = other.astype(BF16)


def last_kernel(base_ref, *refs):
    total = base_ref[...]
    for ref in refs[:-1]:
        total = total + ref[...].astype(F32)
    refs[-1][...] = total.astype(BF16)


def sum_kernel(*refs):
    parts, (mine_ref, other_ref) = refs[:-2], refs[-2:]
    for shift, ref in ((0, mine_ref), (1, other_ref)):
        total = own_columns(parts[0], shift).astype(F32)
        for part in parts[1:]:
            total = total + own_columns(part, shift).astype(F32)
        ref[...] = total.astype(BF16)


def local(
    hidden_in,
    query_nope,
    query_rope,
    new_latent,
    latent_cache,
    key_absorb,
    value_absorb,
    output_proj,
    norm_gain,
    router_proj,
    expert_ids,
    expert_gate,
    expert_up,
    expert_down,
    block_table,
    lengths,
    subtree_moves,
):
    head_count, nope_dim, latent = key_absorb.shape
    rope = query_rope.shape[1] // head_count
    width = latent + rope
    requests, table_len = block_table.shape
    steps = new_latent.shape[1] // width
    row_count, model = hidden_in.shape
    block_size = latent_cache.shape[1] // width
    resident = latent_cache.shape[0]
    experts = router_proj.shape[1]
    groups = lax.axis_size("grp")
    group = lax.axis_index("grp")
    ranks = lax.axis_size("ep")
    me = lax.axis_index("ep")
    ring = ranks // 4
    core_swap = [(i, i ^ 1) for i in range(ranks)]
    side_swap = [(i, i ^ 2) for i in range(ranks)]
    visit = list(range(0, ring, 2)) + list(range(ring - 1 - ring % 2, 0, -2))
    turn_of = {chip: at for at, chip in enumerate(visit)}

    def along(rank, by):
        return visit[(turn_of[rank // 4] + by) % ring] * 4 + rank % 4

    ring_next = [(i, along(i, 1)) for i in range(ranks)]
    both_axes = ("grp", "ep")

    def turn(by):
        return [(g, (g + by) % groups) for g in range(groups)]

    slots = subtree_moves.shape[2]
    pieces = block_size // 2
    outgoing = pl.pallas_call(
        functools.partial(pick_kernel, pieces),
        out_shape=jax.ShapeDtypeStruct((ranks, slots * pieces, 2 * width), BF16),
        in_specs=[ANY] * 2,
        scratch_shapes=[
            VMEM((slots, ranks), jnp.int32),
            VMEM(latent_cache.shape, BF16),
            VMEM((pieces * resident, 2 * width), BF16),
            pltpu.SemaphoreType.DMA((2,)),
        ],
        compiler_params=pltpu.CompilerParams(vmem_limit_bytes=60 * 2**20),
        cost_estimate=cost(0, 4 * 2**20),
        name="pick",
    )(subtree_moves[0].T, latent_cache)
    arrived = lax.all_to_all(outgoing, "ep", split_axis=0, concat_axis=0, tiled=True)

    place = jnp.arange(table_len, dtype=jnp.int32)
    usable = jnp.clip(lengths[:, None] - place[None, :] * block_size, 0, block_size)
    blocks = jnp.arange(resident + ranks * slots, dtype=jnp.int32)
    limit = jnp.sum(
        jnp.where(block_table[:, :, None] == blocks[None, None, :], usable[:, :, None], 0), axis=1
    )
    token = jnp.arange(block_size, dtype=jnp.int32)
    row = jnp.arange(row_count, dtype=jnp.int32)
    fresh = jnp.arange(steps * requests, dtype=jnp.int32)
    fresh_open = ((row // steps)[:, None] == (fresh % requests)[None, :]) & (
        (fresh // requests)[None, :] <= (row % steps)[:, None]
    )
    near_open = (limit[:, None, :resident] > token[None, :, None]).reshape(requests, -1)
    near_open = jnp.concatenate([jnp.repeat(near_open, steps, axis=0), fresh_open], axis=1)
    near_bias = jnp.where(near_open, 0.0, HIDDEN).astype(F32)
    by_key = jnp.repeat(limit[:, resident:], pieces, axis=1)
    at_token = 2 * (jnp.arange(ranks * slots * pieces, dtype=jnp.int32) % pieces)
    moved_open = jnp.concatenate([by_key > at_token[None], by_key > at_token[None] + 1], axis=1)
    moved_bias = jnp.repeat(jnp.where(moved_open, 0.0, HIDDEN).astype(F32), steps, axis=0)

    padded = -(-width // 128) * 128
    query_rows = head_count * row_count
    dims = (head_count, nope_dim, latent, rope, block_size, steps)
    query, mixed = pl.pallas_call(
        functools.partial(resident_kernel, dims),
        out_shape=(
            jax.ShapeDtypeStruct((query_rows, padded), BF16),
            jax.ShapeDtypeStruct((query_rows, value_absorb.shape[2] + 128), F32),
        ),
        scratch_shapes=[VMEM((near_bias.shape[1], padded), BF16)],
        compiler_params=pltpu.CompilerParams(vmem_limit_bytes=16 * 2**20),
        cost_estimate=cost(query_rows * near_bias.shape[1] * (padded + latent), 8 * 2**20),
        name="attend_resident",
    )(query_nope, query_rope, new_latent, latent_cache, key_absorb, value_absorb, near_bias)
    share = pl.pallas_call(
        functools.partial(moved_kernel, dims),
        out_shape=jax.ShapeDtypeStruct((row_count, model), BF16),
        in_specs=[ANY] * 6,
        scratch_shapes=[
            VMEM(arrived.shape, BF16),
            VMEM(query.shape, BF16),
            VMEM(moved_bias.shape, F32),
            VMEM(mixed.shape, F32),
            VMEM(value_absorb.shape, BF16),
            VMEM(output_proj.shape, BF16),
            VMEM((moved_bias.shape[1], padded), BF16),
            VMEM((row_count, head_count * value_absorb.shape[2]), BF16),
            pltpu.SemaphoreType.DMA((6,)),
        ],
        compiler_params=pltpu.CompilerParams(vmem_limit_bytes=56 * 2**20),
        cost_estimate=cost(query_rows * moved_bias.shape[1] * (padded + latent), 10 * 2**20),
        name="attend_moved",
    )(arrived, query, moved_bias, mixed, value_absorb, output_proj)
    shares = [lax.ppermute(share, "grp", turn(by)) for by in range(1, groups)]

    held = [jnp.swapaxes(expert_gate[0], 0, 1), jnp.swapaxes(expert_up[0], 0, 1), expert_down[0]]
    gate_rows, up_rows, down_rows = pl.pallas_call(
        load_kernel,
        out_shape=[jax.ShapeDtypeStruct(array.shape, BF16) for array in held],
        in_specs=[ANY] * 4,
        out_specs=[WHOLE] * 3,
        scratch_shapes=[pltpu.SemaphoreType.DMA((3,))],
        compiler_params=pltpu.CompilerParams(vmem_limit_bytes=44 * 2**20),
        cost_estimate=cost(0, 12 * 2**20),
        name="load",
    )(share, *held)

    extra = -(-2 * experts // 128) * 128
    columns = model // groups
    state, packet = pl.pallas_call(
        functools.partial(norm_kernel, experts),
        out_shape=(
            jax.ShapeDtypeStruct((row_count, columns), F32),
            jax.ShapeDtypeStruct((row_count, model + extra), BF16),
        ),
        in_specs=[ANY] * 3 + [WHOLE] * (2 + groups),
        scratch_shapes=[
            VMEM((row_count, model), BF16),
            VMEM((row_count, model), BF16),
            VMEM((row_count, model), F32),
            pltpu.SemaphoreType.DMA((2,)),
        ],
        compiler_params=pltpu.CompilerParams(vmem_limit_bytes=16 * 2**20),
        cost_estimate=cost(row_count * model * 128, 4 * 2**20),
        name="norm",
    )(share, hidden_in, down_rows, norm_gain[None, :], router_proj.T, expert_ids.T, *shares)

    def run_expert(rows, after, run_after, back=1):
        half = len(rows) * row_count
        here = pl.pallas_call(
            pack_kernel,
            out_shape=jax.ShapeDtypeStruct((half, model + extra), BF16),
            in_specs=[ANY] + [WHOLE] * len(rows),
            compiler_params=pltpu.CompilerParams(vmem_limit_bytes=16 * 2**20),
            cost_estimate=cost(0, 2 * half * model * 2),
            name="pack",
        )(after, *rows)
        across = lax.ppermute(here, "ep", core_swap)
        near, *far = pl.pallas_call(
            functools.partial(expert_kernel, experts),
            out_shape=[
                jax.ShapeDtypeStruct((half // cuts, model), BF16) for cuts in [1] + [back] * back
            ],
            in_specs=[ANY] + [WHOLE] * 5,
            compiler_params=pltpu.CompilerParams(vmem_limit_bytes=24 * 2**20),
            cost_estimate=cost(6 * half * model * gate_rows.shape[0], 12 * 2**20),
            name="expert",
        )(run_after, here, across, gate_rows, up_rows, down_rows)
        return near, [lax.ppermute(part, "ep", core_swap) for part in far]

    def join(near, back, types, first=0, after=()):
        return pl.pallas_call(
            functools.partial(join_kernel, first, len(back), len(after)),
            out_shape=[jax.ShapeDtypeStruct((row_count, model), kind) for kind in types],
            in_specs=[WHOLE] + [ANY] * len(after) + [WHOLE] * len(back),
            compiler_params=pltpu.CompilerParams(vmem_limit_bytes=16 * 2**20),
            cost_estimate=cost(row_count * model, 2**20),
            name="join",
        )(near, *after, *back)

    def send(value, axes, pairs):
        return lax.ppermute(value.astype(BF16), axes, pairs).astype(F32)

    if ring == 4 and groups == 2:
        def ring_step(sign):
            return [
                (g * ranks + i, g * ranks + along(i, sign * (1 - 2 * g)))
                for g in range(2)
                for i in range(ranks)
            ]

        onward, backward, plane_swap = ring_step(1), ring_step(-1), [(0, 1), (1, 0)]
        near = lax.ppermute(packet, both_axes, onward)
        side = lax.ppermute(packet, "ep", side_swap)
        two = lax.ppermute(near, both_axes, onward)
        near_side = lax.ppermute(near, "ep", side_swap)
        far = lax.ppermute(near, "grp", plane_swap)
        two_side = lax.ppermute(two, "ep", side_swap)
        far_side = lax.ppermute(near_side, "grp", plane_swap)
        early = run_expert([packet, side, near], packet, packet)
        later = run_expert([far, near_side, two], early[0], packet)
        own_sum, side_sum, near_sum = join(*early, [F32, BF16, F32])
        side_in = lax.ppermute(side_sum, "ep", side_swap)
        last = run_expert([far_side, two_side], later[0], side_sum, 2)
        near_side_sum, two_sum = join(*later, [F32, F32], 1)
        far_side_sum, two_side_sum = join(*last, [BF16, BF16], 0, [side_in])
        far_side_in = lax.ppermute(far_side_sum, "grp", plane_swap)
        two_side_in = lax.ppermute(two_side_sum, "ep", side_swap)
        [near_side_sum] = join(near_side_sum, [far_side_in], [BF16])
        [two_sum] = join(two_sum, [two_side_in], [BF16])
        [far_sum] = join(*later, [BF16], 0, [far_side_in])
        far_in = lax.ppermute(far_sum, "grp", plane_swap)
        near_side_in = lax.ppermute(near_side_sum, "ep", side_swap)
        two_in = lax.ppermute(two_sum, both_axes, backward)
        part = (row_count, columns)

        def by_columns(kernel, first_type, after_count, *operands):
            return pl.pallas_call(
                kernel,
                out_shape=(
                    jax.ShapeDtypeStruct(part, first_type),
                    jax.ShapeDtypeStruct(part, BF16),
                ),
                in_specs=[ANY] * after_count + [WHOLE] * (len(operands) - after_count),
                compiler_params=pltpu.CompilerParams(vmem_limit_bytes=16 * 2**20),
                cost_estimate=cost(row_count * model, 2**20),
                name=kernel.__name__,
            )(*operands)

        def crossed(pairs):
            return [(source, (target + ranks) % (2 * ranks)) for source, target in pairs]

        near_mine, near_other = by_columns(
            sum_kernel, BF16, 0, near_sum, near_side_in, two_in, far_in
        )
        base, own_other = by_columns(own_kernel, F32, 1, near_mine, state, own_sum, side_in)
        own_over = lax.ppermute(own_other, "grp", plane_swap)
        mine_in = lax.ppermute(near_mine, both_axes, backward)
        other_in = lax.ppermute(near_other, both_axes, crossed(backward))
        return pl.pallas_call(
            last_kernel,
            out_shape=jax.ShapeDtypeStruct(part, BF16),
            in_specs=[WHOLE] * 4,
            compiler_params=pltpu.CompilerParams(vmem_limit_bytes=16 * 2**20),
            cost_estimate=cost(0, 2**20),
            name="last",
        )(base, other_in, mine_in, own_over)

    line = [packet]
    for _ in range(1, ring):
        line.append(lax.ppermute(line[-1], "ep", ring_next))
    totals = []
    for part in line:
        sums = run_expert([lax.ppermute(part, "ep", side_swap), part], packet, packet)
        over, here = join(*sums, [BF16, F32])
        totals.append(here + send(over, "ep", side_swap))
    moving = totals[1 % ring]
    for hop in list(range(2, ring)) + [0]:
        moving = totals[hop] + send(moving, "ep", ring_next)

    result = state + lax.dynamic_slice_in_dim(moving, group * columns, columns, 1)
    for by in range(1, groups):
        to = (group + by) % groups
        part = lax.dynamic_slice_in_dim(moving, to * columns, columns, 1)
        result = result + send(part, "grp", turn(by))
    return result.astype(BF16)


def solution(mesh):
    in_specs = (
        P("ep", None),
        P("ep", "grp"),
        P("ep", "grp"),
        P("ep", None),
        P("ep", None),
        P("grp", None, None),
        P("grp", None, None),
        P("grp", None),
        P(),
        P(),
        P("ep", None),
        P("ep", None, "grp"),
        P("ep", None, "grp"),
        P("ep", "grp", None),
        P("ep", None),
        P("ep"),
        P("ep", None, None),
    )
    out_specs = P("ep", "grp")
    return jax.shard_map(local, mesh=mesh, in_specs=in_specs, out_specs=out_specs, check_vma=False)
```

```python
import functools

import jax
import jax.numpy as jnp
from jax import lax
from jax.experimental import pallas as pl
from jax.experimental.pallas import tpu as pltpu
from jax.sharding import PartitionSpec as P

F32 = jnp.float32
BF16 = jnp.bfloat16
HIDDEN = -1e30
VMEM = pltpu.VMEM
ANY = pl.BlockSpec(memory_space=pl.ANY)
WHOLE = pl.BlockSpec(memory_space=pltpu.VMEM)


def dot(a, b):
    return jnp.dot(a, b, preferred_element_type=F32)


def dot_rows(a, b):
    return lax.dot_general(a, b, (((1,), (1,)), ((), ())), preferred_element_type=F32)


def cost(products, moved_bytes):
    return pl.CostEstimate(flops=2 * products, bytes_accessed=moved_bytes, transcendentals=0)


def fetch_all(sources, buffers, sems):
    copies = []
    for at, (source, buffer) in enumerate(zip(sources, buffers)):
        copy = pltpu.make_async_copy(source, buffer, sems.at[at])
        copy.start()
        copies.append(copy)
    return copies


def lay_tokens(keys, start, ref, tokens, width):
    count = ref.shape[0]
    for token in range(tokens):
        keys[start : start + count, :width] = ref[:, token * width : (token + 1) * width]
        start += count
    return start


def pick_kernel(pieces, moves_any, cache_any, out_ref, moves_ref, cache, stacked, sems):
    got = fetch_all((moves_any, cache_any), (moves_ref, cache), sems)
    ranks, per_rank, wide = out_ref.shape
    slots = moves_ref.shape[0]
    resident = cache.shape[0]
    rows = ranks * per_rank
    row = lax.broadcasted_iota(jnp.int32, (rows, ranks), 0)
    rank = lax.broadcasted_iota(jnp.int32, (rows, ranks), 1)
    chosen = jnp.zeros((rows, ranks), jnp.int32)
    got[0].wait()
    for slot in range(slots):
        here = (row // per_rank == rank) & (row % per_rank // pieces == slot)
        chosen = chosen + jnp.where(here, moves_ref[slot : slot + 1, :], 0)
    block = jnp.clip(jnp.sum(chosen, axis=1, keepdims=True), 0, resident - 1)
    at = lax.broadcasted_iota(jnp.int32, (rows, pieces * resident), 0)
    source = lax.broadcasted_iota(jnp.int32, (rows, pieces * resident), 1)
    pick = (source // resident == at % pieces) & (source % resident == block)
    got[1].wait()
    for piece in range(pieces):
        stacked[piece * resident : (piece + 1) * resident, :] = cache[:, piece * wide : (piece + 1) * wide]
    picked = dot(pick.astype(F32).astype(BF16), stacked[...]).astype(BF16)
    out_ref[...] = picked.reshape(ranks, per_rank, wide)


def resident_kernel(
    dims, nope, rope_rows, fresh, cache, absorb, bias_ref,
    query_ref, mixed_ref,
    keys,
):
    head_count, nope_dim, latent, rope, block_size, steps = dims
    width = latent + rope
    rows = nope.shape[0]
    padding = keys.shape[1] - width
    keys[:, latent:] = jnp.zeros((keys.shape[0], keys.shape[1] - latent), BF16)
    start = lay_tokens(keys, 0, cache, block_size, width)
    lay_tokens(keys, start, fresh, steps, width)
    for head in range(head_count):
        q_latent = dot(nope[:, head * nope_dim : (head + 1) * nope_dim], absorb[head])
        q_rope = rope_rows[:, head * rope : (head + 1) * rope]
        fill = jnp.zeros((rows, padding), BF16)
        query_ref[head * rows : (head + 1) * rows, :] = jnp.concatenate(
            [q_latent.astype(BF16), q_rope, fill], axis=1
        )
    scale = (nope_dim + rope) ** (-0.5)
    part = min(4, head_count) * rows
    for first in range(0, head_count * rows, part):
        score = dot_rows(query_ref[first : first + part, :], keys[...])
        score = score.reshape(part // rows, rows, -1) * scale + bias_ref[...][None]
        score = score.reshape(part, -1)
        peak = jnp.max(score, axis=1, keepdims=True)
        weight = jnp.exp(score - peak)
        total = jnp.sum(weight, axis=1, keepdims=True)
        mixed_ref[first : first + part, :latent] = dot(weight.astype(BF16), keys[:, :latent])
        lane = lax.broadcasted_iota(jnp.int32, (part, 128), 1)
        mixed_ref[first : first + part, latent:] = jnp.where(lane < 64, peak, total)


def moved_kernel(
    dims, moved_any, query_any, bias_any, mixed_any, value_any, proj_any,
    share_ref,
    moved, query, bias, mixed, value, proj, keys, heads_out, sems,
):
    head_count, nope_dim, latent, rope, block_size, steps = dims
    width = latent + rope
    rows = heads_out.shape[0]
    got = fetch_all(
        (moved_any, query_any, bias_any, mixed_any, value_any, proj_any),
        (moved, query, bias, mixed, value, proj),
        sems,
    )
    keys[:, latent:] = jnp.zeros((keys.shape[0], keys.shape[1] - latent), BF16)
    scale = (nope_dim + rope) ** (-0.5)
    value_dim = value.shape[2]
    got[0].wait()
    count = moved.shape[0] * moved.shape[1]
    for half in range(2):
        part = moved[:, :, half * width : (half + 1) * width]
        keys[half * count : (half + 1) * count, :width] = part.reshape(count, width)
    got[1].wait()
    got[2].wait()
    group = min(4, head_count)
    for first in range(0, head_count, group):
        at = slice(first * rows, (first + group) * rows)
        score = dot_rows(query[at, :], keys[...])
        score = score.reshape(group, rows, -1) * scale + bias[...][None]
        score = score.reshape(group * rows, -1)
        if first == 0:
            got[3].wait()
        before = mixed[at, latent : latent + 1]
        peak = jnp.maximum(jnp.max(score, axis=1, keepdims=True), before)
        weight = jnp.exp(score - peak)
        keep = jnp.exp(before - peak)
        total = jnp.sum(weight, axis=1, keepdims=True) + mixed[at, latent + 64 : latent + 65] * keep
        joined = dot(weight.astype(BF16), keys[:, :latent]) + mixed[at, :latent] * keep
        joined = (joined / total).astype(BF16)
        if first == 0:
            got[4].wait()
        for head in range(first, first + group):
            own = joined[(head - first) * rows : (head - first + 1) * rows]
            heads_out[:, head * value_dim : (head + 1) * value_dim] = dot(own, value[head]).astype(BF16)
    got[5].wait()
    share_ref[...] = dot(heads_out[...], proj[...]).astype(BF16)


def own_columns(ref, shift):
    groups = lax.axis_size("grp")
    columns = ref.shape[1] // groups
    first = (lax.axis_index("grp") + shift) % groups * columns
    return ref[:, pl.ds(pl.multiple_of(first, 128), columns)]


def norm_kernel(experts, own_any, hidden_any, loaded_any, gain_ref, router_ref, ids_ref, *refs):
    parts, (state_ref, packet_ref, own, hidden, whole, sems) = refs[:-6], refs[-6:]
    got = fetch_all((own_any, hidden_any), (own, hidden), sems)
    rows, model = hidden.shape
    state = parts[0][...].astype(F32)
    for part in parts[1:]:
        state = state + part[...].astype(F32)
    for copy in got:
        copy.wait()
    state = state + own[...].astype(F32) + hidden[...].astype(F32)
    whole[...] = state
    state_ref[...] = own_columns(whole, 0)
    square = jnp.mean(state * state, axis=1, keepdims=True)
    normed = (state * lax.rsqrt(square + 1e-06) * gain_ref[...].astype(F32)).astype(BF16)
    packet_ref[:, :model] = normed
    logits = dot_rows(router_ref[...], normed)
    names = lax.broadcasted_iota(jnp.int32, (experts, rows), 0)
    named = names == ids_ref[0:1, :]
    for k in range(1, ids_ref.shape[0]):
        named = named | (names == ids_ref[k : k + 1, :])
    chosen = jnp.where(named, jax.nn.sigmoid(logits), 0.0)
    weight = chosen / jnp.sum(chosen, axis=0, keepdims=True)
    high = weight.astype(BF16)
    low = (weight - high.astype(F32)).astype(BF16)
    extra = packet_ref.shape[1] - model
    both = jnp.concatenate([high, low], axis=0)
    place = lax.broadcasted_iota(jnp.int32, (2 * experts, extra), 0)
    lane = lax.broadcasted_iota(jnp.int32, (2 * experts, extra), 1)
    turned = lax.dot_general(
        both, (place == lane).astype(BF16), (((0,), (0,)), ((), ())), preferred_element_type=F32
    )
    packet_ref[:, model:] = turned.astype(BF16)


def load_kernel(after_any, gate_any, up_any, down_any, gate_ref, up_ref, down_ref, sems):
    sources, targets = (gate_any, up_any, down_any), (gate_ref, up_ref, down_ref)
    for copy in fetch_all(sources, targets, sems):
        copy.wait()


def pack_kernel(after_any, *refs):
    count = refs[0].shape[0]
    for at, ref in enumerate(refs[:-1]):
        refs[-1][at * count : (at + 1) * count, :] = ref[...]


def expert_kernel(experts, after_any, here_ref, across_ref, gate_ref, up_ref, down_ref, *out_refs):
    near_ref, *far_refs = out_refs
    model = gate_ref.shape[1]
    packet = jnp.concatenate([here_ref[...], across_ref[...]], axis=0)
    rows = packet[:, :model]
    extra = packet[:, model:].astype(F32)
    names = lax.broadcasted_iota(jnp.int32, extra.shape, 1)
    me = lax.axis_index("ep")
    mine = (names == me) | (names == me + experts)
    weight = jnp.sum(jnp.where(mine, extra, 0.0), axis=1, keepdims=True)
    gate = dot_rows(rows, gate_ref[...])
    up = dot_rows(rows, up_ref[...])
    inner = (gate * jax.nn.sigmoid(gate) * up * weight).astype(BF16)
    result = dot(inner, down_ref[...]).astype(BF16)
    half = near_ref.shape[0]
    near_ref[...] = result[:half]
    height = half // len(far_refs)
    for at, far_ref in enumerate(far_refs):
        far_ref[...] = result[half + at * height : half + (at + 1) * height]


def join_kernel(first, back_count, after_count, near_ref, *refs):
    back_refs, out_refs = refs[after_count : after_count + back_count], refs[after_count + back_count :]
    count = out_refs[0].shape[0]
    height = back_refs[0].shape[0]
    step = min(count, height)
    for at, ref in enumerate(out_refs, first):
        for row in range(at * count, (at + 1) * count, step):
            back = back_refs[row // height][row % height : row % height + step, :].astype(F32)
            total = near_ref[row : row + step, :].astype(F32) + back
            ref[row - at * count : row - at * count + step, :] = total.astype(ref.dtype)


def own_kernel(after_any, state_ref, own_ref, side_ref, base_ref, other_ref):
    mine, other = (own_columns(own_ref, by) + own_columns(side_ref, by).astype(F32) for by in (0, 1))
    base_ref[...] = state_ref[...] + mine
    other_ref[...] = other.astype(BF16)


def last_kernel(base_ref, other_ref, mine_ref, upper_ref, lower_ref, out_ref):
    middle = upper_ref.shape[0]
    for rows, ref in ((slice(0, middle), upper_ref), (slice(middle, 2 * middle), lower_ref)):
        total = base_ref[rows, :] + other_ref[rows, :].astype(F32) + mine_ref[rows, :].astype(F32)
        out_ref[rows, :] = (total + ref[...].astype(F32)).astype(BF16)


def sum_kernel(*refs):
    parts, (mine_ref, other_ref) = refs[:-2], refs[-2:]
    for shift, ref in ((0, mine_ref), (1, other_ref)):
        total = own_columns(parts[0], shift).astype(F32)
        for part in parts[1:]:
            total = total + own_columns(part, shift).astype(F32)
        ref[...] = total.astype(BF16)


def local(
    hidden_in,
    query_nope,
    query_rope,
    new_latent,
    latent_cache,
    key_absorb,
    value_absorb,
    output_proj,
    norm_gain,
    router_proj,
    expert_ids,
    expert_gate,
    expert_up,
    expert_down,
    block_table,
    lengths,
    subtree_moves,
):
    head_count, nope_dim, latent = key_absorb.shape
    rope = query_rope.shape[1] // head_count
    width = latent + rope
    requests, table_len = block_table.shape
    steps = new_latent.shape[1] // width
    row_count, model = hidden_in.shape
    block_size = latent_cache.shape[1] // width
    resident = latent_cache.shape[0]
    experts = router_proj.shape[1]
    groups = lax.axis_size("grp")
    group = lax.axis_index("grp")
    ranks = lax.axis_size("ep")
    me = lax.axis_index("ep")
    ring = ranks // 4
    core_swap = [(i, i ^ 1) for i in range(ranks)]
    side_swap = [(i, i ^ 2) for i in range(ranks)]
    visit = list(range(0, ring, 2)) + list(range(ring - 1 - ring % 2, 0, -2))
    turn_of = {chip: at for at, chip in enumerate(visit)}

    def along(rank, by):
        return visit[(turn_of[rank // 4] + by) % ring] * 4 + rank % 4

    ring_next = [(i, along(i, 1)) for i in range(ranks)]
    both_axes = ("grp", "ep")

    def turn(by):
        return [(g, (g + by) % groups) for g in range(groups)]

    slots = subtree_moves.shape[2]
    pieces = block_size // 2
    outgoing = pl.pallas_call(
        functools.partial(pick_kernel, pieces),
        out_shape=jax.ShapeDtypeStruct((ranks, slots * pieces, 2 * width), BF16),
        in_specs=[ANY] * 2,
        scratch_shapes=[
            VMEM((slots, ranks), jnp.int32),
            VMEM(latent_cache.shape, BF16),
            VMEM((pieces * resident, 2 * width), BF16),
            pltpu.SemaphoreType.DMA((2,)),
        ],
        compiler_params=pltpu.CompilerParams(vmem_limit_bytes=60 * 2**20),
        cost_estimate=cost(0, 4 * 2**20),
        name="pick",
    )(subtree_moves[0].T, latent_cache)
    arrived = lax.all_to_all(outgoing, "ep", split_axis=0, concat_axis=0, tiled=True)

    place = jnp.arange(table_len, dtype=jnp.int32)
    usable = jnp.clip(lengths[:, None] - place[None, :] * block_size, 0, block_size)
    blocks = jnp.arange(resident + ranks * slots, dtype=jnp.int32)
    limit = jnp.sum(
        jnp.where(block_table[:, :, None] == blocks[None, None, :], usable[:, :, None], 0), axis=1
    )
    token = jnp.arange(block_size, dtype=jnp.int32)
    row = jnp.arange(row_count, dtype=jnp.int32)
    fresh = jnp.arange(steps * requests, dtype=jnp.int32)
    fresh_open = ((row // steps)[:, None] == (fresh % requests)[None, :]) & (
        (fresh // requests)[None, :] <= (row % steps)[:, None]
    )
    near_open = (limit[:, None, :resident] > token[None, :, None]).reshape(requests, -1)
    near_open = jnp.concatenate([jnp.repeat(near_open, steps, axis=0), fresh_open], axis=1)
    near_bias = jnp.where(near_open, 0.0, HIDDEN).astype(F32)
    by_key = jnp.repeat(limit[:, resident:], pieces, axis=1)
    at_token = 2 * (jnp.arange(ranks * slots * pieces, dtype=jnp.int32) % pieces)
    moved_open = jnp.concatenate([by_key > at_token[None], by_key > at_token[None] + 1], axis=1)
    moved_bias = jnp.repeat(jnp.where(moved_open, 0.0, HIDDEN).astype(F32), steps, axis=0)

    padded = -(-width // 128) * 128
    query_rows = head_count * row_count
    dims = (head_count, nope_dim, latent, rope, block_size, steps)
    query, mixed = pl.pallas_call(
        functools.partial(resident_kernel, dims),
        out_shape=(
            jax.ShapeDtypeStruct((query_rows, padded), BF16),
            jax.ShapeDtypeStruct((query_rows, latent + 128), F32),
        ),
        scratch_shapes=[VMEM((near_bias.shape[1], padded), BF16)],
        compiler_params=pltpu.CompilerParams(vmem_limit_bytes=16 * 2**20),
        cost_estimate=cost(query_rows * near_bias.shape[1] * (padded + latent), 8 * 2**20),
        name="attend_resident",
    )(query_nope, query_rope, new_latent, latent_cache, key_absorb, near_bias)
    share = pl.pallas_call(
        functools.partial(moved_kernel, dims),
        out_shape=jax.ShapeDtypeStruct((row_count, model), BF16),
        in_specs=[ANY] * 6,
        scratch_shapes=[
            VMEM(arrived.shape, BF16),
            VMEM(query.shape, BF16),
            VMEM(moved_bias.shape, F32),
            VMEM(mixed.shape, F32),
            VMEM(value_absorb.shape, BF16),
            VMEM(output_proj.shape, BF16),
            VMEM((moved_bias.shape[1], padded), BF16),
            VMEM((row_count, head_count * value_absorb.shape[2]), BF16),
            pltpu.SemaphoreType.DMA((6,)),
        ],
        compiler_params=pltpu.CompilerParams(vmem_limit_bytes=56 * 2**20),
        cost_estimate=cost(query_rows * moved_bias.shape[1] * (padded + latent), 10 * 2**20),
        name="attend_moved",
    )(arrived, query, moved_bias, mixed, value_absorb, output_proj)
    shares = [lax.ppermute(share, "grp", turn(by)) for by in range(1, groups)]

    held = [jnp.swapaxes(expert_gate[0], 0, 1), jnp.swapaxes(expert_up[0], 0, 1), expert_down[0]]
    gate_rows, up_rows, down_rows = pl.pallas_call(
        load_kernel,
        out_shape=[jax.ShapeDtypeStruct(array.shape, BF16) for array in held],
        in_specs=[ANY] * 4,
        out_specs=[WHOLE] * 3,
        scratch_shapes=[pltpu.SemaphoreType.DMA((3,))],
        compiler_params=pltpu.CompilerParams(vmem_limit_bytes=44 * 2**20),
        cost_estimate=cost(0, 12 * 2**20),
        name="load",
    )(share, *held)

    extra = -(-2 * experts // 128) * 128
    columns = model // groups
    state, packet = pl.pallas_call(
        functools.partial(norm_kernel, experts),
        out_shape=(
            jax.ShapeDtypeStruct((row_count, columns), F32),
            jax.ShapeDtypeStruct((row_count, model + extra), BF16),
        ),
        in_specs=[ANY] * 3 + [WHOLE] * (2 + groups),
        scratch_shapes=[
            VMEM((row_count, model), BF16),
            VMEM((row_count, model), BF16),
            VMEM((row_count, model), F32),
            pltpu.SemaphoreType.DMA((2,)),
        ],
        compiler_params=pltpu.CompilerParams(vmem_limit_bytes=16 * 2**20),
        cost_estimate=cost(row_count * model * 128, 4 * 2**20),
        name="norm",
    )(share, hidden_in, down_rows, norm_gain[None, :], router_proj.T, expert_ids.T, *shares)

    def run_expert(rows, after, run_after, back=1):
        half = len(rows) * row_count
        here = pl.pallas_call(
            pack_kernel,
            out_shape=jax.ShapeDtypeStruct((half, model + extra), BF16),
            in_specs=[ANY] + [WHOLE] * len(rows),
            compiler_params=pltpu.CompilerParams(vmem_limit_bytes=16 * 2**20),
            cost_estimate=cost(0, 2 * half * model * 2),
            name="pack",
        )(after, *rows)
        across = lax.ppermute(here, "ep", core_swap)
        near, *far = pl.pallas_call(
            functools.partial(expert_kernel, experts),
            out_shape=[
                jax.ShapeDtypeStruct((half // cuts, model), BF16) for cuts in [1] + [back] * back
            ],
            in_specs=[ANY] + [WHOLE] * 5,
            compiler_params=pltpu.CompilerParams(vmem_limit_bytes=24 * 2**20),
            cost_estimate=cost(6 * half * model * gate_rows.shape[0], 12 * 2**20),
            name="expert",
        )(run_after, here, across, gate_rows, up_rows, down_rows)
        return near, [lax.ppermute(part, "ep", core_swap) for part in far]

    def join(near, back, types, first=0, after=()):
        return pl.pallas_call(
            functools.partial(join_kernel, first, len(back), len(after)),
            out_shape=[jax.ShapeDtypeStruct((row_count, model), kind) for kind in types],
            in_specs=[WHOLE] + [ANY] * len(after) + [WHOLE] * len(back),
            compiler_params=pltpu.CompilerParams(vmem_limit_bytes=16 * 2**20),
            cost_estimate=cost(row_count * model, 2**20),
            name="join",
        )(near, *after, *back)

    def send(value, axes, pairs):
        return lax.ppermute(value.astype(BF16), axes, pairs).astype(F32)

    if ring == 4 and groups == 2:
        def ring_step(sign):
            return [
                (g * ranks + i, g * ranks + along(i, sign * (1 - 2 * g)))
                for g in range(2)
                for i in range(ranks)
            ]

        onward, backward, plane_swap = ring_step(1), ring_step(-1), [(0, 1), (1, 0)]
        near = lax.ppermute(packet, both_axes, onward)
        side = lax.ppermute(packet, "ep", side_swap)
        two = lax.ppermute(near, both_axes, onward)
        near_side = lax.ppermute(near, "ep", side_swap)
        far = lax.ppermute(near, "grp", plane_swap)
        two_side = lax.ppermute(two, "ep", side_swap)
        far_side = lax.ppermute(near_side, "grp", plane_swap)
        early = run_expert([packet, side, near], packet, packet)
        later = run_expert([far, near_side, two], early[0], packet)
        own_sum, side_sum, near_sum = join(*early, [F32, BF16, F32])
        side_in = lax.ppermute(side_sum, "ep", side_swap)
        last = run_expert([far_side, two_side], later[0], side_sum, 2)
        near_side_sum, two_sum = join(*later, [F32, F32], 1)
        far_side_sum, two_side_sum = join(*last, [BF16, BF16], 0, [side_in])
        far_side_in = lax.ppermute(far_side_sum, "grp", plane_swap)
        two_side_in = lax.ppermute(two_side_sum, "ep", side_swap)
        [near_side_sum] = join(near_side_sum, [far_side_in], [BF16])
        [two_sum] = join(two_sum, [two_side_in], [BF16])
        [far_sum] = join(*later, [BF16], 0, [far_side_in])
        far_in = lax.ppermute(far_sum, "grp", plane_swap)
        near_side_in = lax.ppermute(near_side_sum, "ep", side_swap)
        two_in = lax.ppermute(two_sum, both_axes, backward)
        part = (row_count, columns)

        def by_columns(kernel, first_type, after_count, *operands):
            return pl.pallas_call(
                kernel,
                out_shape=(
                    jax.ShapeDtypeStruct(part, first_type),
                    jax.ShapeDtypeStruct(part, BF16),
                ),
                in_specs=[ANY] * after_count + [WHOLE] * (len(operands) - after_count),
                compiler_params=pltpu.CompilerParams(vmem_limit_bytes=16 * 2**20),
                cost_estimate=cost(row_count * model, 2**20),
                name=kernel.__name__,
            )(*operands)

        def crossed(pairs):
            return [(source, (target + ranks) % (2 * ranks)) for source, target in pairs]

        near_mine, near_other = by_columns(
            sum_kernel, BF16, 0, near_sum, near_side_in, two_in, far_in
        )
        base, own_other = by_columns(own_kernel, F32, 1, near_mine, state, own_sum, side_in)
        middle = row_count // 2
        own_over = [
            lax.ppermute(own_other[half : half + middle], "grp", plane_swap) for half in (0, middle)
        ]
        mine_in = lax.ppermute(near_mine, both_axes, backward)
        other_in = lax.ppermute(near_other, both_axes, crossed(backward))
        return pl.pallas_call(
            last_kernel,
            out_shape=jax.ShapeDtypeStruct(part, BF16),
            in_specs=[WHOLE] * 5,
            compiler_params=pltpu.CompilerParams(vmem_limit_bytes=16 * 2**20),
            cost_estimate=cost(0, 2**20),
            name="last",
        )(base, other_in, mine_in, *own_over)

    line = [packet]
    for _ in range(1, ring):
        line.append(lax.ppermute(line[-1], "ep", ring_next))
    totals = []
    for part in line:
        sums = run_expert([lax.ppermute(part, "ep", side_swap), part], packet, packet)
        over, here = join(*sums, [BF16, F32])
        totals.append(here + send(over, "ep", side_swap))
    moving = totals[1 % ring]
    for hop in list(range(2, ring)) + [0]:
        moving = totals[hop] + send(moving, "ep", ring_next)

    result = state + lax.dynamic_slice_in_dim(moving, group * columns, columns, 1)
    for by in range(1, groups):
        to = (group + by) % groups
        part = lax.dynamic_slice_in_dim(moving, to * columns, columns, 1)
        result = result + send(part, "grp", turn(by))
    return result.astype(BF16)


def solution(mesh):
    in_specs = (
        P("ep", None),
        P("ep", "grp"),
        P("ep", "grp"),
        P("ep", None),
        P("ep", None),
        P("grp", None, None),
        P("grp", None, None),
        P("grp", None),
        P(),
        P(),
        P("ep", None),
        P("ep", None, "grp"),
        P("ep", None, "grp"),
        P("ep", "grp", None),
        P("ep", None),
        P("ep"),
        P("ep", None, None),
    )
    out_specs = P("ep", "grp")
    return jax.shard_map(local, mesh=mesh, in_specs=in_specs, out_specs=out_specs, check_vma=False)
```

```python
import functools

import jax
import jax.numpy as jnp
from jax import lax
from jax.experimental import pallas as pl
from jax.experimental.pallas import tpu as pltpu
from jax.sharding import PartitionSpec as P

F32 = jnp.float32
BF16 = jnp.bfloat16
HIDDEN = -1e30
VMEM = pltpu.VMEM
ANY = pl.BlockSpec(memory_space=pl.ANY)
WHOLE = pl.BlockSpec(memory_space=pltpu.VMEM)


def dot(a, b):
    return jnp.dot(a, b, preferred_element_type=F32)


def dot_rows(a, b):
    return lax.dot_general(a, b, (((1,), (1,)), ((), ())), preferred_element_type=F32)


def cost(products, moved_bytes):
    return pl.CostEstimate(flops=2 * products, bytes_accessed=moved_bytes, transcendentals=0)


def fetch_all(sources, buffers, sems):
    copies = []
    for at, (source, buffer) in enumerate(zip(sources, buffers)):
        copy = pltpu.make_async_copy(source, buffer, sems.at[at])
        copy.start()
        copies.append(copy)
    return copies


def lay_tokens(keys, start, ref, tokens, width):
    count = ref.shape[0]
    for token in range(tokens):
        keys[start : start + count, :width] = ref[:, token * width : (token + 1) * width]
        start += count
    return start


def pick_kernel(pieces, moves_any, cache_any, out_ref, moves_ref, cache, stacked, sems):
    got = fetch_all((moves_any, cache_any), (moves_ref, cache), sems)
    ranks, per_rank, wide = out_ref.shape
    slots = moves_ref.shape[0]
    resident = cache.shape[0]
    rows = ranks * per_rank
    row = lax.broadcasted_iota(jnp.int32, (rows, ranks), 0)
    rank = lax.broadcasted_iota(jnp.int32, (rows, ranks), 1)
    chosen = jnp.zeros((rows, ranks), jnp.int32)
    got[0].wait()
    for slot in range(slots):
        here = (row // per_rank == rank) & (row % per_rank // pieces == slot)
        chosen = chosen + jnp.where(here, moves_ref[slot : slot + 1, :], 0)
    block = jnp.clip(jnp.sum(chosen, axis=1, keepdims=True), 0, resident - 1)
    at = lax.broadcasted_iota(jnp.int32, (rows, pieces * resident), 0)
    source = lax.broadcasted_iota(jnp.int32, (rows, pieces * resident), 1)
    pick = (source // resident == at % pieces) & (source % resident == block)
    got[1].wait()
    for piece in range(pieces):
        stacked[piece * resident : (piece + 1) * resident, :] = cache[:, piece * wide : (piece + 1) * wide]
    picked = dot(pick.astype(F32).astype(BF16), stacked[...]).astype(BF16)
    out_ref[...] = picked.reshape(ranks, per_rank, wide)


def resident_kernel(
    dims, nope, rope_rows, fresh, cache, absorb, bias_ref,
    query_ref, mixed_ref,
    keys,
):
    head_count, nope_dim, latent, rope, block_size, steps = dims
    width = latent + rope
    rows = nope.shape[0]
    padding = keys.shape[1] - width
    keys[:, latent:] = jnp.zeros((keys.shape[0], keys.shape[1] - latent), BF16)
    start = lay_tokens(keys, 0, cache, block_size, width)
    lay_tokens(keys, start, fresh, steps, width)
    for head in range(head_count):
        q_latent = dot(nope[:, head * nope_dim : (head + 1) * nope_dim], absorb[head])
        q_rope = rope_rows[:, head * rope : (head + 1) * rope]
        fill = jnp.zeros((rows, padding), BF16)
        query_ref[head * rows : (head + 1) * rows, :] = jnp.concatenate(
            [q_latent.astype(BF16), q_rope, fill], axis=1
        )
    scale = (nope_dim + rope) ** (-0.5)
    part = min(4, head_count) * rows
    for first in range(0, head_count * rows, part):
        score = dot_rows(query_ref[first : first + part, :], keys[...])
        score = score.reshape(part // rows, rows, -1) * scale + bias_ref[...][None]
        score = score.reshape(part, -1)
        peak = jnp.max(score, axis=1, keepdims=True)
        weight = jnp.exp(score - peak)
        total = jnp.sum(weight, axis=1, keepdims=True)
        mixed_ref[first : first + part, :latent] = dot(weight.astype(BF16), keys[:, :latent])
        lane = lax.broadcasted_iota(jnp.int32, (part, 128), 1)
        mixed_ref[first : first + part, latent:] = jnp.where(lane < 64, peak, total)


def moved_kernel(
    dims, moved, query_any, bias_any, mixed_any, value_any, proj_any,
    share_ref,
    query, bias, mixed, value, proj, keys, heads_out, sems,
):
    head_count, nope_dim, latent, rope, block_size, steps = dims
    width = latent + rope
    rows = heads_out.shape[0]
    got = fetch_all(
        (query_any, bias_any, mixed_any, value_any, proj_any),
        (query, bias, mixed, value, proj),
        sems,
    )
    keys[:, latent:] = jnp.zeros((keys.shape[0], keys.shape[1] - latent), BF16)
    scale = (nope_dim + rope) ** (-0.5)
    value_dim = value.shape[2]
    count = moved.shape[0] * moved.shape[1]
    for half in range(2):
        part = moved[:, :, half * width : (half + 1) * width]
        keys[half * count : (half + 1) * count, :width] = part.reshape(count, width)
    got[0].wait()
    got[1].wait()
    group = min(4, head_count)
    for first in range(0, head_count, group):
        at = slice(first * rows, (first + group) * rows)
        score = dot_rows(query[at, :], keys[...])
        score = score.reshape(group, rows, -1) * scale + bias[...][None]
        score = score.reshape(group * rows, -1)
        if first == 0:
            got[2].wait()
        before = mixed[at, latent : latent + 1]
        peak = jnp.maximum(jnp.max(score, axis=1, keepdims=True), before)
        weight = jnp.exp(score - peak)
        keep = jnp.exp(before - peak)
        total = jnp.sum(weight, axis=1, keepdims=True) + mixed[at, latent + 64 : latent + 65] * keep
        joined = dot(weight.astype(BF16), keys[:, :latent]) + mixed[at, :latent] * keep
        joined = (joined / total).astype(BF16)
        if first == 0:
            got[3].wait()
        for head in range(first, first + group):
            own = joined[(head - first) * rows : (head - first + 1) * rows]
            heads_out[:, head * value_dim : (head + 1) * value_dim] = dot(own, value[head]).astype(BF16)
    got[4].wait()
    share_ref[...] = dot(heads_out[...], proj[...]).astype(BF16)


def own_columns(ref, shift):
    groups = lax.axis_size("grp")
    columns = ref.shape[1] // groups
    first = (lax.axis_index("grp") + shift) % groups * columns
    return ref[:, pl.ds(pl.multiple_of(first, 128), columns)]


def norm_kernel(experts, own_any, hidden_any, loaded_any, gain_ref, router_ref, ids_ref, *refs):
    parts, (state_ref, packet_ref, own, hidden, whole, sems) = refs[:-6], refs[-6:]
    got = fetch_all((own_any, hidden_any), (own, hidden), sems)
    rows, model = hidden.shape
    state = parts[0][...].astype(F32)
    for part in parts[1:]:
        state = state + part[...].astype(F32)
    for copy in got:
        copy.wait()
    state = state + own[...].astype(F32) + hidden[...].astype(F32)
    whole[...] = state
    state_ref[...] = own_columns(whole, 0)
    square = jnp.mean(state * state, axis=1, keepdims=True)
    normed = (state * lax.rsqrt(square + 1e-06) * gain_ref[...].astype(F32)).astype(BF16)
    packet_ref[:, :model] = normed
    logits = dot_rows(router_ref[...], normed)
    names = lax.broadcasted_iota(jnp.int32, (experts, rows), 0)
    named = names == ids_ref[0:1, :]
    for k in range(1, ids_ref.shape[0]):
        named = named | (names == ids_ref[k : k + 1, :])
    chosen = jnp.where(named, jax.nn.sigmoid(logits), 0.0)
    weight = chosen / jnp.sum(chosen, axis=0, keepdims=True)
    high = weight.astype(BF16)
    low = (weight - high.astype(F32)).astype(BF16)
    extra = packet_ref.shape[1] - model
    both = jnp.concatenate([high, low], axis=0)
    place = lax.broadcasted_iota(jnp.int32, (2 * experts, extra), 0)
    lane = lax.broadcasted_iota(jnp.int32, (2 * experts, extra), 1)
    turned = lax.dot_general(
        both, (place == lane).astype(BF16), (((0,), (0,)), ((), ())), preferred_element_type=F32
    )
    packet_ref[:, model:] = turned.astype(BF16)


def load_kernel(after_any, gate_any, up_any, down_any, gate_ref, up_ref, down_ref, sems):
    sources, targets = (gate_any, up_any, down_any), (gate_ref, up_ref, down_ref)
    for copy in fetch_all(sources, targets, sems):
        copy.wait()


def pack_kernel(after_any, *refs):
    count = refs[0].shape[0]
    for at, ref in enumerate(refs[:-1]):
        refs[-1][at * count : (at + 1) * count, :] = ref[...]


def expert_kernel(experts, after_any, here_ref, across_ref, gate_ref, up_ref, down_ref, *out_refs):
    near_ref, *far_refs = out_refs
    model = gate_ref.shape[1]
    packet = jnp.concatenate([here_ref[...], across_ref[...]], axis=0)
    rows = packet[:, :model]
    extra = packet[:, model:].astype(F32)
    names = lax.broadcasted_iota(jnp.int32, extra.shape, 1)
    me = lax.axis_index("ep")
    mine = (names == me) | (names == me + experts)
    weight = jnp.sum(jnp.where(mine, extra, 0.0), axis=1, keepdims=True)
    gate = dot_rows(rows, gate_ref[...])
    up = dot_rows(rows, up_ref[...])
    inner = (gate * jax.nn.sigmoid(gate) * up * weight).astype(BF16)
    result = dot(inner, down_ref[...]).astype(BF16)
    half = near_ref.shape[0]
    near_ref[...] = result[:half]
    height = half // len(far_refs)
    for at, far_ref in enumerate(far_refs):
        far_ref[...] = result[half + at * height : half + (at + 1) * height]


def join_kernel(first, back_count, after_count, near_ref, *refs):
    back_refs, out_refs = refs[after_count : after_count + back_count], refs[after_count + back_count :]
    count = out_refs[0].shape[0]
    height = back_refs[0].shape[0]
    step = min(count, height)
    for at, ref in enumerate(out_refs, first):
        for row in range(at * count, (at + 1) * count, step):
            back = back_refs[row // height][row % height : row % height + step, :].astype(F32)
            total = near_ref[row : row + step, :].astype(F32) + back
            ref[row - at * count : row - at * count + step, :] = total.astype(ref.dtype)


def own_kernel(after_any, state_ref, own_ref, side_ref, base_ref, other_ref):
    mine, other = (own_columns(own_ref, by) + own_columns(side_ref, by).astype(F32) for by in (0, 1))
    base_ref[...] = state_ref[...] + mine
    other_ref[...] = other.astype(BF16)


def last_kernel(base_ref, other_ref, mine_ref, upper_ref, lower_ref, out_ref):
    middle = upper_ref.shape[0]
    for rows, ref in ((slice(0, middle), upper_ref), (slice(middle, 2 * middle), lower_ref)):
        total = base_ref[rows, :] + other_ref[rows, :].astype(F32) + mine_ref[rows, :].astype(F32)
        out_ref[rows, :] = (total + ref[...].astype(F32)).astype(BF16)


def sum_kernel(*refs):
    parts, (mine_ref, other_ref) = refs[:-2], refs[-2:]
    for shift, ref in ((0, mine_ref), (1, other_ref)):
        total = own_columns(parts[0], shift).astype(F32)
        for part in parts[1:]:
            total = total + own_columns(part, shift).astype(F32)
        ref[...] = total.astype(BF16)


def local(
    hidden_in,
    query_nope,
    query_rope,
    new_latent,
    latent_cache,
    key_absorb,
    value_absorb,
    output_proj,
    norm_gain,
    router_proj,
    expert_ids,
    expert_gate,
    expert_up,
    expert_down,
    block_table,
    lengths,
    subtree_moves,
):
    head_count, nope_dim, latent = key_absorb.shape
    rope = query_rope.shape[1] // head_count
    width = latent + rope
    requests, table_len = block_table.shape
    steps = new_latent.shape[1] // width
    row_count, model = hidden_in.shape
    block_size = latent_cache.shape[1] // width
    resident = latent_cache.shape[0]
    experts = router_proj.shape[1]
    groups = lax.axis_size("grp")
    group = lax.axis_index("grp")
    ranks = lax.axis_size("ep")
    me = lax.axis_index("ep")
    ring = ranks // 4
    core_swap = [(i, i ^ 1) for i in range(ranks)]
    side_swap = [(i, i ^ 2) for i in range(ranks)]
    visit = list(range(0, ring, 2)) + list(range(ring - 1 - ring % 2, 0, -2))
    turn_of = {chip: at for at, chip in enumerate(visit)}

    def along(rank, by):
        return visit[(turn_of[rank // 4] + by) % ring] * 4 + rank % 4

    ring_next = [(i, along(i, 1)) for i in range(ranks)]
    both_axes = ("grp", "ep")

    def turn(by):
        return [(g, (g + by) % groups) for g in range(groups)]

    slots = subtree_moves.shape[2]
    pieces = block_size // 2
    outgoing = pl.pallas_call(
        functools.partial(pick_kernel, pieces),
        out_shape=jax.ShapeDtypeStruct((ranks, slots * pieces, 2 * width), BF16),
        in_specs=[ANY] * 2,
        scratch_shapes=[
            VMEM((slots, ranks), jnp.int32),
            VMEM(latent_cache.shape, BF16),
            VMEM((pieces * resident, 2 * width), BF16),
            pltpu.SemaphoreType.DMA((2,)),
        ],
        compiler_params=pltpu.CompilerParams(vmem_limit_bytes=60 * 2**20),
        cost_estimate=cost(0, 4 * 2**20),
        name="pick",
    )(subtree_moves[0].T, latent_cache)
    arrived = lax.all_to_all(outgoing, "ep", split_axis=0, concat_axis=0, tiled=True)

    place = jnp.arange(table_len, dtype=jnp.int32)
    usable = jnp.clip(lengths[:, None] - place[None, :] * block_size, 0, block_size)
    blocks = jnp.arange(resident + ranks * slots, dtype=jnp.int32)
    limit = jnp.sum(
        jnp.where(block_table[:, :, None] == blocks[None, None, :], usable[:, :, None], 0), axis=1
    )
    token = jnp.arange(block_size, dtype=jnp.int32)
    row = jnp.arange(row_count, dtype=jnp.int32)
    fresh = jnp.arange(steps * requests, dtype=jnp.int32)
    fresh_open = ((row // steps)[:, None] == (fresh % requests)[None, :]) & (
        (fresh // requests)[None, :] <= (row % steps)[:, None]
    )
    near_open = (limit[:, None, :resident] > token[None, :, None]).reshape(requests, -1)
    near_open = jnp.concatenate([jnp.repeat(near_open, steps, axis=0), fresh_open], axis=1)
    near_bias = jnp.where(near_open, 0.0, HIDDEN).astype(F32)
    by_key = jnp.repeat(limit[:, resident:], pieces, axis=1)
    at_token = 2 * (jnp.arange(ranks * slots * pieces, dtype=jnp.int32) % pieces)
    moved_open = jnp.concatenate([by_key > at_token[None], by_key > at_token[None] + 1], axis=1)
    moved_bias = jnp.repeat(jnp.where(moved_open, 0.0, HIDDEN).astype(F32), steps, axis=0)

    padded = -(-width // 128) * 128
    query_rows = head_count * row_count
    dims = (head_count, nope_dim, latent, rope, block_size, steps)
    query, mixed = pl.pallas_call(
        functools.partial(resident_kernel, dims),
        out_shape=(
            jax.ShapeDtypeStruct((query_rows, padded), BF16),
            jax.ShapeDtypeStruct((query_rows, latent + 128), F32),
        ),
        scratch_shapes=[VMEM((near_bias.shape[1], padded), BF16)],
        compiler_params=pltpu.CompilerParams(vmem_limit_bytes=16 * 2**20),
        cost_estimate=cost(query_rows * near_bias.shape[1] * (padded + latent), 8 * 2**20),
        name="attend_resident",
    )(query_nope, query_rope, new_latent, latent_cache, key_absorb, near_bias)
    share = pl.pallas_call(
        functools.partial(moved_kernel, dims),
        out_shape=jax.ShapeDtypeStruct((row_count, model), BF16),
        in_specs=[WHOLE] + [ANY] * 5,
        scratch_shapes=[
            VMEM(query.shape, BF16),
            VMEM(moved_bias.shape, F32),
            VMEM(mixed.shape, F32),
            VMEM(value_absorb.shape, BF16),
            VMEM(output_proj.shape, BF16),
            VMEM((moved_bias.shape[1], padded), BF16),
            VMEM((row_count, head_count * value_absorb.shape[2]), BF16),
            pltpu.SemaphoreType.DMA((5,)),
        ],
        compiler_params=pltpu.CompilerParams(vmem_limit_bytes=56 * 2**20),
        cost_estimate=cost(query_rows * moved_bias.shape[1] * (padded + latent), 10 * 2**20),
        name="attend_moved",
    )(arrived, query, moved_bias, mixed, value_absorb, output_proj)
    shares = [lax.ppermute(share, "grp", turn(by)) for by in range(1, groups)]

    held = [jnp.swapaxes(expert_gate[0], 0, 1), jnp.swapaxes(expert_up[0], 0, 1), expert_down[0]]
    gate_rows, up_rows, down_rows = pl.pallas_call(
        load_kernel,
        out_shape=[jax.ShapeDtypeStruct(array.shape, BF16) for array in held],
        in_specs=[ANY] * 4,
        out_specs=[WHOLE] * 3,
        scratch_shapes=[pltpu.SemaphoreType.DMA((3,))],
        compiler_params=pltpu.CompilerParams(vmem_limit_bytes=44 * 2**20),
        cost_estimate=cost(0, 12 * 2**20),
        name="load",
    )(share, *held)

    extra = -(-2 * experts // 128) * 128
    columns = model // groups
    state, packet = pl.pallas_call(
        functools.partial(norm_kernel, experts),
        out_shape=(
            jax.ShapeDtypeStruct((row_count, columns), F32),
            jax.ShapeDtypeStruct((row_count, model + extra), BF16),
        ),
        in_specs=[ANY] * 3 + [WHOLE] * (2 + groups),
        scratch_shapes=[
            VMEM((row_count, model), BF16),
            VMEM((row_count, model), BF16),
            VMEM((row_count, model), F32),
            pltpu.SemaphoreType.DMA((2,)),
        ],
        compiler_params=pltpu.CompilerParams(vmem_limit_bytes=16 * 2**20),
        cost_estimate=cost(row_count * model * 128, 4 * 2**20),
        name="norm",
    )(share, hidden_in, down_rows, norm_gain[None, :], router_proj.T, expert_ids.T, *shares)

    def run_expert(rows, after, run_after, back=1):
        half = len(rows) * row_count
        here = pl.pallas_call(
            pack_kernel,
            out_shape=jax.ShapeDtypeStruct((half, model + extra), BF16),
            in_specs=[ANY] + [WHOLE] * len(rows),
            compiler_params=pltpu.CompilerParams(vmem_limit_bytes=16 * 2**20),
            cost_estimate=cost(0, 2 * half * model * 2),
            name="pack",
        )(after, *rows)
        across = lax.ppermute(here, "ep", core_swap)
        near, *far = pl.pallas_call(
            functools.partial(expert_kernel, experts),
            out_shape=[
                jax.ShapeDtypeStruct((half // cuts, model), BF16) for cuts in [1] + [back] * back
            ],
            in_specs=[ANY] + [WHOLE] * 5,
            compiler_params=pltpu.CompilerParams(vmem_limit_bytes=24 * 2**20),
            cost_estimate=cost(6 * half * model * gate_rows.shape[0], 12 * 2**20),
            name="expert",
        )(run_after, here, across, gate_rows, up_rows, down_rows)
        return near, [lax.ppermute(part, "ep", core_swap) for part in far]

    def join(near, back, types, first=0, after=()):
        return pl.pallas_call(
            functools.partial(join_kernel, first, len(back), len(after)),
            out_shape=[jax.ShapeDtypeStruct((row_count, model), kind) for kind in types],
            in_specs=[WHOLE] + [ANY] * len(after) + [WHOLE] * len(back),
            compiler_params=pltpu.CompilerParams(vmem_limit_bytes=16 * 2**20),
            cost_estimate=cost(row_count * model, 2**20),
            name="join",
        )(near, *after, *back)

    def send(value, axes, pairs):
        return lax.ppermute(value.astype(BF16), axes, pairs).astype(F32)

    if ring == 4 and groups == 2:
        def ring_step(sign):
            return [
                (g * ranks + i, g * ranks + along(i, sign * (1 - 2 * g)))
                for g in range(2)
                for i in range(ranks)
            ]

        onward, backward, plane_swap = ring_step(1), ring_step(-1), [(0, 1), (1, 0)]
        near = lax.ppermute(packet, both_axes, onward)
        side = lax.ppermute(packet, "ep", side_swap)
        two = lax.ppermute(near, both_axes, onward)
        near_side = lax.ppermute(near, "ep", side_swap)
        far = lax.ppermute(near, "grp", plane_swap)
        two_side = lax.ppermute(two, "ep", side_swap)
        far_side = lax.ppermute(near_side, "grp", plane_swap)
        early = run_expert([packet, side, near], packet, packet)
        later = run_expert([far, near_side, two], early[0], packet)
        own_sum, side_sum, near_sum = join(*early, [F32, BF16, F32])
        side_in = lax.ppermute(side_sum, "ep", side_swap)
        last = run_expert([far_side, two_side], later[0], side_sum, 2)
        near_side_sum, two_sum = join(*later, [F32, F32], 1)
        far_side_sum, two_side_sum = join(*last, [BF16, BF16], 0, [side_in])
        far_side_in = lax.ppermute(far_side_sum, "grp", plane_swap)
        two_side_in = lax.ppermute(two_side_sum, "ep", side_swap)
        [near_side_sum] = join(near_side_sum, [far_side_in], [BF16])
        [two_sum] = join(two_sum, [two_side_in], [BF16])
        [far_sum] = join(*later, [BF16], 0, [far_side_in])
        far_in = lax.ppermute(far_sum, "grp", plane_swap)
        near_side_in = lax.ppermute(near_side_sum, "ep", side_swap)
        two_in = lax.ppermute(two_sum, both_axes, backward)
        part = (row_count, columns)

        def by_columns(kernel, first_type, after_count, *operands):
            return pl.pallas_call(
                kernel,
                out_shape=(
                    jax.ShapeDtypeStruct(part, first_type),
                    jax.ShapeDtypeStruct(part, BF16),
                ),
                in_specs=[ANY] * after_count + [WHOLE] * (len(operands) - after_count),
                compiler_params=pltpu.CompilerParams(vmem_limit_bytes=16 * 2**20),
                cost_estimate=cost(row_count * model, 2**20),
                name=kernel.__name__,
            )(*operands)

        def crossed(pairs):
            return [(source, (target + ranks) % (2 * ranks)) for source, target in pairs]

        near_mine, near_other = by_columns(
            sum_kernel, BF16, 0, near_sum, near_side_in, two_in, far_in
        )
        base, own_other = by_columns(own_kernel, F32, 1, near_mine, state, own_sum, side_in)
        middle = row_count // 2
        own_over = [
            lax.ppermute(own_other[half : half + middle], "grp", plane_swap) for half in (0, middle)
        ]
        mine_in = lax.ppermute(near_mine, both_axes, backward)
        other_in = lax.ppermute(near_other, both_axes, crossed(backward))
        return pl.pallas_call(
            last_kernel,
            out_shape=jax.ShapeDtypeStruct(part, BF16),
            in_specs=[WHOLE] * 5,
            compiler_params=pltpu.CompilerParams(vmem_limit_bytes=16 * 2**20),
            cost_estimate=cost(0, 2**20),
            name="last",
        )(base, other_in, mine_in, *own_over)

    line = [packet]
    for _ in range(1, ring):
        line.append(lax.ppermute(line[-1], "ep", ring_next))
    totals = []
    for part in line:
        sums = run_expert([lax.ppermute(part, "ep", side_swap), part], packet, packet)
        over, here = join(*sums, [BF16, F32])
        totals.append(here + send(over, "ep", side_swap))
    moving = totals[1 % ring]
    for hop in list(range(2, ring)) + [0]:
        moving = totals[hop] + send(moving, "ep", ring_next)

    result = state + lax.dynamic_slice_in_dim(moving, group * columns, columns, 1)
    for by in range(1, groups):
        to = (group + by) % groups
        part = lax.dynamic_slice_in_dim(moving, to * columns, columns, 1)
        result = result + send(part, "grp", turn(by))
    return result.astype(BF16)


def solution(mesh):
    in_specs = (
        P("ep", None),
        P("ep", "grp"),
        P("ep", "grp"),
        P("ep", None),
        P("ep", None),
        P("grp", None, None),
        P("grp", None, None),
        P("grp", None),
        P(),
        P(),
        P("ep", None),
        P("ep", None, "grp"),
        P("ep", None, "grp"),
        P("ep", "grp", None),
        P("ep", None),
        P("ep"),
        P("ep", None, None),
    )
    out_specs = P("ep", "grp")
    return jax.shard_map(local, mesh=mesh, in_specs=in_specs, out_specs=out_specs, check_vma=False)
```

```python
import functools

import jax
import jax.numpy as jnp
from jax import lax
from jax.experimental import pallas as pl
from jax.experimental.pallas import tpu as pltpu
from jax.sharding import PartitionSpec as P

F32 = jnp.float32
BF16 = jnp.bfloat16
HIDDEN = -1e30
VMEM = pltpu.VMEM
ANY = pl.BlockSpec(memory_space=pl.ANY)
WHOLE = pl.BlockSpec(memory_space=pltpu.VMEM)


def dot(a, b):
    return jnp.dot(a, b, preferred_element_type=F32)


def dot_rows(a, b):
    return lax.dot_general(a, b, (((1,), (1,)), ((), ())), preferred_element_type=F32)


def cost(products, moved_bytes):
    return pl.CostEstimate(flops=2 * products, bytes_accessed=moved_bytes, transcendentals=0)


def fetch_all(sources, buffers, sems):
    copies = []
    for at, (source, buffer) in enumerate(zip(sources, buffers)):
        copy = pltpu.make_async_copy(source, buffer, sems.at[at])
        copy.start()
        copies.append(copy)
    return copies


def lay_tokens(keys, start, ref, tokens, width):
    count = ref.shape[0]
    for token in range(tokens):
        keys[start : start + count, :width] = ref[:, token * width : (token + 1) * width]
        start += count
    return start


def pick_kernel(pieces, moves_any, cache_any, out_ref, moves_ref, stacked, sems):
    ranks, per_rank, wide = out_ref.shape
    slots = moves_ref.shape[0]
    resident = cache_any.shape[0]
    got = fetch_all(
        [moves_any] + [cache_any.at[:, piece * wide : (piece + 1) * wide] for piece in range(pieces)],
        [moves_ref]
        + [stacked.at[piece * resident : (piece + 1) * resident] for piece in range(pieces)],
        sems,
    )
    rows = ranks * per_rank
    row = lax.broadcasted_iota(jnp.int32, (rows, ranks), 0)
    rank = lax.broadcasted_iota(jnp.int32, (rows, ranks), 1)
    chosen = jnp.zeros((rows, ranks), jnp.int32)
    got[0].wait()
    for slot in range(slots):
        here = (row // per_rank == rank) & (row % per_rank // pieces == slot)
        chosen = chosen + jnp.where(here, moves_ref[slot : slot + 1, :], 0)
    block = jnp.clip(jnp.sum(chosen, axis=1, keepdims=True), 0, resident - 1)
    at = lax.broadcasted_iota(jnp.int32, (rows, pieces * resident), 0)
    source = lax.broadcasted_iota(jnp.int32, (rows, pieces * resident), 1)
    pick = (source // resident == at % pieces) & (source % resident == block)
    for copy in got[1:]:
        copy.wait()
    picked = dot(pick.astype(F32).astype(BF16), stacked[...]).astype(BF16)
    out_ref[...] = picked.reshape(ranks, per_rank, wide)


def resident_kernel(
    dims, nope, rope_rows, fresh, cache, absorb, bias_ref,
    query_ref, mixed_ref,
    keys,
):
    head_count, nope_dim, latent, rope, block_size, steps = dims
    width = latent + rope
    rows = nope.shape[0]
    padding = keys.shape[1] - width
    keys[:, latent:] = jnp.zeros((keys.shape[0], keys.shape[1] - latent), BF16)
    start = lay_tokens(keys, 0, cache, block_size, width)
    lay_tokens(keys, start, fresh, steps, width)
    for head in range(head_count):
        q_latent = dot(nope[:, head * nope_dim : (head + 1) * nope_dim], absorb[head])
        q_rope = rope_rows[:, head * rope : (head + 1) * rope]
        fill = jnp.zeros((rows, padding), BF16)
        query_ref[head * rows : (head + 1) * rows, :] = jnp.concatenate(
            [q_latent.astype(BF16), q_rope, fill], axis=1
        )
    scale = (nope_dim + rope) ** (-0.5)
    part = min(4, head_count) * rows
    for first in range(0, head_count * rows, part):
        score = dot_rows(query_ref[first : first + part, :], keys[...])
        score = score.reshape(part // rows, rows, -1) * scale + bias_ref[...][None]
        score = score.reshape(part, -1)
        peak = jnp.max(score, axis=1, keepdims=True)
        weight = jnp.exp(score - peak)
        total = jnp.sum(weight, axis=1, keepdims=True)
        mixed_ref[first : first + part, :latent] = dot(weight.astype(BF16), keys[:, :latent])
        lane = lax.broadcasted_iota(jnp.int32, (part, 128), 1)
        mixed_ref[first : first + part, latent:] = jnp.where(lane < 64, peak, total)


def moved_kernel(
    dims, moved_any, query_any, bias_any, mixed_any, value_any, proj_any,
    share_ref,
    moved, query, bias, mixed, value, proj, keys, heads_out, sems,
):
    head_count, nope_dim, latent, rope, block_size, steps = dims
    width = latent + rope
    rows = heads_out.shape[0]
    middle = proj.shape[1] // 2
    halves = (slice(0, middle), slice(middle, 2 * middle))
    got = fetch_all(
        [moved_any, query_any, bias_any, mixed_any, value_any] + [proj_any.at[:, at] for at in halves],
        [moved, query, bias, mixed, value] + [proj.at[:, at] for at in halves],
        sems,
    )
    keys[:, latent:] = jnp.zeros((keys.shape[0], keys.shape[1] - latent), BF16)
    scale = (nope_dim + rope) ** (-0.5)
    value_dim = value.shape[2]
    got[0].wait()
    count = moved.shape[0] * moved.shape[1]
    for half in range(2):
        part = moved[:, :, half * width : (half + 1) * width]
        keys[half * count : (half + 1) * count, :width] = part.reshape(count, width)
    got[1].wait()
    got[2].wait()
    group = min(4, head_count)
    for first in range(0, head_count, group):
        at = slice(first * rows, (first + group) * rows)
        score = dot_rows(query[at, :], keys[...])
        score = score.reshape(group, rows, -1) * scale + bias[...][None]
        score = score.reshape(group * rows, -1)
        if first == 0:
            got[3].wait()
        before = mixed[at, latent : latent + 1]
        peak = jnp.maximum(jnp.max(score, axis=1, keepdims=True), before)
        weight = jnp.exp(score - peak)
        keep = jnp.exp(before - peak)
        total = jnp.sum(weight, axis=1, keepdims=True) + mixed[at, latent + 64 : latent + 65] * keep
        joined = dot(weight.astype(BF16), keys[:, :latent]) + mixed[at, :latent] * keep
        joined = (joined / total).astype(BF16)
        if first == 0:
            got[4].wait()
        for head in range(first, first + group):
            own = joined[(head - first) * rows : (head - first + 1) * rows]
            heads_out[:, head * value_dim : (head + 1) * value_dim] = dot(own, value[head]).astype(BF16)
    for at, copy in zip(halves, got[5:]):
        copy.wait()
        share_ref[:, at] = dot(heads_out[...], proj[:, at]).astype(BF16)


def own_columns(ref, shift):
    groups = lax.axis_size("grp")
    columns = ref.shape[1] // groups
    first = (lax.axis_index("grp") + shift) % groups * columns
    return ref[:, pl.ds(pl.multiple_of(first, 128), columns)]


def norm_kernel(experts, own_any, hidden_any, loaded_any, gain_ref, router_ref, ids_ref, *refs):
    parts, (state_ref, packet_ref, own, hidden, whole, sems) = refs[:-6], refs[-6:]
    got = fetch_all((own_any, hidden_any), (own, hidden), sems)
    rows, model = hidden.shape
    state = parts[0][...].astype(F32)
    for part in parts[1:]:
        state = state + part[...].astype(F32)
    for copy in got:
        copy.wait()
    state = state + own[...].astype(F32) + hidden[...].astype(F32)
    whole[...] = state
    state_ref[...] = own_columns(whole, 0)
    square = jnp.mean(state * state, axis=1, keepdims=True)
    normed = (state * lax.rsqrt(square + 1e-06) * gain_ref[...].astype(F32)).astype(BF16)
    packet_ref[:, :model] = normed
    logits = dot_rows(router_ref[...], normed)
    names = lax.broadcasted_iota(jnp.int32, (experts, rows), 0)
    named = names == ids_ref[0:1, :]
    for k in range(1, ids_ref.shape[0]):
        named = named | (names == ids_ref[k : k + 1, :])
    chosen = jnp.where(named, jax.nn.sigmoid(logits), 0.0)
    weight = chosen / jnp.sum(chosen, axis=0, keepdims=True)
    high = weight.astype(BF16)
    low = (weight - high.astype(F32)).astype(BF16)
    extra = packet_ref.shape[1] - model
    both = jnp.concatenate([high, low], axis=0)
    place = lax.broadcasted_iota(jnp.int32, (2 * experts, extra), 0)
    lane = lax.broadcasted_iota(jnp.int32, (2 * experts, extra), 1)
    turned = lax.dot_general(
        both, (place == lane).astype(BF16), (((0,), (0,)), ((), ())), preferred_element_type=F32
    )
    packet_ref[:, model:] = turned.astype(BF16)


def load_kernel(after_any, gate_any, up_any, down_any, gate_ref, up_ref, down_ref, sems):
    sources, targets = (gate_any, up_any, down_any), (gate_ref, up_ref, down_ref)
    for copy in fetch_all(sources, targets, sems):
        copy.wait()


def pack_kernel(after_any, *refs):
    count = refs[0].shape[0]
    for at, ref in enumerate(refs[:-1]):
        refs[-1][at * count : (at + 1) * count, :] = ref[...]


def expert_kernel(experts, after_any, here_ref, across_ref, gate_ref, up_ref, down_ref, *out_refs):
    near_ref, *far_refs = out_refs
    model = gate_ref.shape[1]
    packet = jnp.concatenate([here_ref[...], across_ref[...]], axis=0)
    rows = packet[:, :model]
    extra = packet[:, model:].astype(F32)
    names = lax.broadcasted_iota(jnp.int32, extra.shape, 1)
    me = lax.axis_index("ep")
    mine = (names == me) | (names == me + experts)
    weight = jnp.sum(jnp.where(mine, extra, 0.0), axis=1, keepdims=True)
    gate = dot_rows(rows, gate_ref[...])
    up = dot_rows(rows, up_ref[...])
    inner = (gate * jax.nn.sigmoid(gate) * up * weight).astype(BF16)
    result = dot(inner, down_ref[...]).astype(BF16)
    half = near_ref.shape[0]
    near_ref[...] = result[:half]
    height = half // len(far_refs)
    for at, far_ref in enumerate(far_refs):
        far_ref[...] = result[half + at * height : half + (at + 1) * height]


def join_kernel(first, back_count, after_count, near_ref, *refs):
    back_refs, out_refs = refs[after_count : after_count + back_count], refs[after_count + back_count :]
    count = out_refs[0].shape[0]
    height = back_refs[0].shape[0]
    step = min(count, height)
    for at, ref in enumerate(out_refs, first):
        for row in range(at * count, (at + 1) * count, step):
            back = back_refs[row // height][row % height : row % height + step, :].astype(F32)
            total = near_ref[row : row + step, :].astype(F32) + back
            ref[row - at * count : row - at * count + step, :] = total.astype(ref.dtype)


def own_kernel(after_any, state_ref, own_ref, side_ref, base_ref, other_ref):
    mine, other = (own_columns(own_ref, by) + own_columns(side_ref, by).astype(F32) for by in (0, 1))
    base_ref[...] = state_ref[...] + mine
    other_ref[...] = other.astype(BF16)


def last_kernel(base_ref, other_ref, mine_ref, upper_ref, lower_ref, out_ref):
    middle = upper_ref.shape[0]
    for rows, ref in ((slice(0, middle), upper_ref), (slice(middle, 2 * middle), lower_ref)):
        total = base_ref[rows, :] + other_ref[rows, :].astype(F32) + mine_ref[rows, :].astype(F32)
        out_ref[rows, :] = (total + ref[...].astype(F32)).astype(BF16)


def sum_kernel(*refs):
    parts, (mine_ref, other_ref) = refs[:-2], refs[-2:]
    for shift, ref in ((0, mine_ref), (1, other_ref)):
        total = own_columns(parts[0], shift).astype(F32)
        for part in parts[1:]:
            total = total + own_columns(part, shift).astype(F32)
        ref[...] = total.astype(BF16)


def local(
    hidden_in,
    query_nope,
    query_rope,
    new_latent,
    latent_cache,
    key_absorb,
    value_absorb,
    output_proj,
    norm_gain,
    router_proj,
    expert_ids,
    expert_gate,
    expert_up,
    expert_down,
    block_table,
    lengths,
    subtree_moves,
):
    head_count, nope_dim, latent = key_absorb.shape
    rope = query_rope.shape[1] // head_count
    width = latent + rope
    requests, table_len = block_table.shape
    steps = new_latent.shape[1] // width
    row_count, model = hidden_in.shape
    block_size = latent_cache.shape[1] // width
    resident = latent_cache.shape[0]
    experts = router_proj.shape[1]
    groups = lax.axis_size("grp")
    group = lax.axis_index("grp")
    ranks = lax.axis_size("ep")
    me = lax.axis_index("ep")
    ring = ranks // 4
    core_swap = [(i, i ^ 1) for i in range(ranks)]
    side_swap = [(i, i ^ 2) for i in range(ranks)]
    visit = list(range(0, ring, 2)) + list(range(ring - 1 - ring % 2, 0, -2))
    turn_of = {chip: at for at, chip in enumerate(visit)}

    def along(rank, by):
        return visit[(turn_of[rank // 4] + by) % ring] * 4 + rank % 4

    ring_next = [(i, along(i, 1)) for i in range(ranks)]
    both_axes = ("grp", "ep")

    def turn(by):
        return [(g, (g + by) % groups) for g in range(groups)]

    slots = subtree_moves.shape[2]
    pieces = block_size // 2
    outgoing = pl.pallas_call(
        functools.partial(pick_kernel, pieces),
        out_shape=jax.ShapeDtypeStruct((ranks, slots * pieces, 2 * width), BF16),
        in_specs=[ANY] * 2,
        scratch_shapes=[
            VMEM((slots, ranks), jnp.int32),
            VMEM((pieces * resident, 2 * width), BF16),
            pltpu.SemaphoreType.DMA((1 + pieces,)),
        ],
        compiler_params=pltpu.CompilerParams(vmem_limit_bytes=60 * 2**20),
        cost_estimate=cost(0, 4 * 2**20),
        name="pick",
    )(subtree_moves[0].T, latent_cache)
    arrived = lax.all_to_all(outgoing, "ep", split_axis=0, concat_axis=0, tiled=True)

    place = jnp.arange(table_len, dtype=jnp.int32)
    usable = jnp.clip(lengths[:, None] - place[None, :] * block_size, 0, block_size)
    blocks = jnp.arange(resident + ranks * slots, dtype=jnp.int32)
    limit = jnp.sum(
        jnp.where(block_table[:, :, None] == blocks[None, None, :], usable[:, :, None], 0), axis=1
    )
    token = jnp.arange(block_size, dtype=jnp.int32)
    row = jnp.arange(row_count, dtype=jnp.int32)
    fresh = jnp.arange(steps * requests, dtype=jnp.int32)
    fresh_open = ((row // steps)[:, None] == (fresh % requests)[None, :]) & (
        (fresh // requests)[None, :] <= (row % steps)[:, None]
    )
    near_open = (limit[:, None, :resident] > token[None, :, None]).reshape(requests, -1)
    near_open = jnp.concatenate([jnp.repeat(near_open, steps, axis=0), fresh_open], axis=1)
    near_bias = jnp.where(near_open, 0.0, HIDDEN).astype(F32)
    by_key = jnp.repeat(limit[:, resident:], pieces, axis=1)
    at_token = 2 * (jnp.arange(ranks * slots * pieces, dtype=jnp.int32) % pieces)
    moved_open = jnp.concatenate([by_key > at_token[None], by_key > at_token[None] + 1], axis=1)
    moved_bias = jnp.repeat(jnp.where(moved_open, 0.0, HIDDEN).astype(F32), steps, axis=0)

    padded = -(-width // 128) * 128
    query_rows = head_count * row_count
    dims = (head_count, nope_dim, latent, rope, block_size, steps)
    query, mixed = pl.pallas_call(
        functools.partial(resident_kernel, dims),
        out_shape=(
            jax.ShapeDtypeStruct((query_rows, padded), BF16),
            jax.ShapeDtypeStruct((query_rows, latent + 128), F32),
        ),
        scratch_shapes=[VMEM((near_bias.shape[1], padded), BF16)],
        compiler_params=pltpu.CompilerParams(vmem_limit_bytes=16 * 2**20),
        cost_estimate=cost(query_rows * near_bias.shape[1] * (padded + latent), 8 * 2**20),
        name="attend_resident",
    )(query_nope, query_rope, new_latent, latent_cache, key_absorb, near_bias)
    share = pl.pallas_call(
        functools.partial(moved_kernel, dims),
        out_shape=jax.ShapeDtypeStruct((row_count, model), BF16),
        in_specs=[ANY] * 6,
        scratch_shapes=[
            VMEM(arrived.shape, BF16),
            VMEM(query.shape, BF16),
            VMEM(moved_bias.shape, F32),
            VMEM(mixed.shape, F32),
            VMEM(value_absorb.shape, BF16),
            VMEM(output_proj.shape, BF16),
            VMEM((moved_bias.shape[1], padded), BF16),
            VMEM((row_count, head_count * value_absorb.shape[2]), BF16),
            pltpu.SemaphoreType.DMA((7,)),
        ],
        compiler_params=pltpu.CompilerParams(vmem_limit_bytes=56 * 2**20),
        cost_estimate=cost(query_rows * moved_bias.shape[1] * (padded + latent), 10 * 2**20),
        name="attend_moved",
    )(arrived, query, moved_bias, mixed, value_absorb, output_proj)
    shares = [lax.ppermute(share, "grp", turn(by)) for by in range(1, groups)]

    held = [jnp.swapaxes(expert_gate[0], 0, 1), jnp.swapaxes(expert_up[0], 0, 1), expert_down[0]]
    gate_rows, up_rows, down_rows = pl.pallas_call(
        load_kernel,
        out_shape=[jax.ShapeDtypeStruct(array.shape, BF16) for array in held],
        in_specs=[ANY] * 4,
        out_specs=[WHOLE] * 3,
        scratch_shapes=[pltpu.SemaphoreType.DMA((3,))],
        compiler_params=pltpu.CompilerParams(vmem_limit_bytes=44 * 2**20),
        cost_estimate=cost(0, 12 * 2**20),
        name="load",
    )(share, *held)

    extra = -(-2 * experts // 128) * 128
    columns = model // groups
    state, packet = pl.pallas_call(
        functools.partial(norm_kernel, experts),
        out_shape=(
            jax.ShapeDtypeStruct((row_count, columns), F32),
            jax.ShapeDtypeStruct((row_count, model + extra), BF16),
        ),
        in_specs=[ANY] * 3 + [WHOLE] * (2 + groups),
        scratch_shapes=[
            VMEM((row_count, model), BF16),
            VMEM((row_count, model), BF16),
            VMEM((row_count, model), F32),
            pltpu.SemaphoreType.DMA((2,)),
        ],
        compiler_params=pltpu.CompilerParams(vmem_limit_bytes=16 * 2**20),
        cost_estimate=cost(row_count * model * 128, 4 * 2**20),
        name="norm",
    )(share, hidden_in, down_rows, norm_gain[None, :], router_proj.T, expert_ids.T, *shares)

    def run_expert(rows, after, run_after, back=1):
        half = len(rows) * row_count
        here = pl.pallas_call(
            pack_kernel,
            out_shape=jax.ShapeDtypeStruct((half, model + extra), BF16),
            in_specs=[ANY] + [WHOLE] * len(rows),
            compiler_params=pltpu.CompilerParams(vmem_limit_bytes=16 * 2**20),
            cost_estimate=cost(0, 2 * half * model * 2),
            name="pack",
        )(after, *rows)
        across = lax.ppermute(here, "ep", core_swap)
        near, *far = pl.pallas_call(
            functools.partial(expert_kernel, experts),
            out_shape=[
                jax.ShapeDtypeStruct((half // cuts, model), BF16) for cuts in [1] + [back] * back
            ],
            in_specs=[ANY] + [WHOLE] * 5,
            compiler_params=pltpu.CompilerParams(vmem_limit_bytes=24 * 2**20),
            cost_estimate=cost(6 * half * model * gate_rows.shape[0], 12 * 2**20),
            name="expert",
        )(run_after, here, across, gate_rows, up_rows, down_rows)
        return near, [lax.ppermute(part, "ep", core_swap) for part in far]

    def join(near, back, types, first=0, after=()):
        return pl.pallas_call(
            functools.partial(join_kernel, first, len(back), len(after)),
            out_shape=[jax.ShapeDtypeStruct((row_count, model), kind) for kind in types],
            in_specs=[WHOLE] + [ANY] * len(after) + [WHOLE] * len(back),
            compiler_params=pltpu.CompilerParams(vmem_limit_bytes=16 * 2**20),
            cost_estimate=cost(row_count * model, 2**20),
            name="join",
        )(near, *after, *back)

    def send(value, axes, pairs):
        return lax.ppermute(value.astype(BF16), axes, pairs).astype(F32)

    if ring == 4 and groups == 2:
        def ring_step(sign):
            return [
                (g * ranks + i, g * ranks + along(i, sign * (1 - 2 * g)))
                for g in range(2)
                for i in range(ranks)
            ]

        onward, backward, plane_swap = ring_step(1), ring_step(-1), [(0, 1), (1, 0)]
        near = lax.ppermute(packet, both_axes, onward)
        side = lax.ppermute(packet, "ep", side_swap)
        two = lax.ppermute(near, both_axes, onward)
        near_side = lax.ppermute(near, "ep", side_swap)
        far = lax.ppermute(near, "grp", plane_swap)
        two_side = lax.ppermute(two, "ep", side_swap)
        far_side = lax.ppermute(near_side, "grp", plane_swap)
        early = run_expert([packet, side, near], packet, packet)
        later = run_expert([far, near_side, two], early[0], packet)
        own_sum, side_sum, near_sum = join(*early, [F32, BF16, F32])
        side_in = lax.ppermute(side_sum, "ep", side_swap)
        last = run_expert([far_side, two_side], later[0], side_sum, 2)
        near_side_sum, two_sum = join(*later, [F32, F32], 1)
        far_side_sum, two_side_sum = join(*last, [BF16, BF16], 0, [side_in])
        far_side_in = lax.ppermute(far_side_sum, "grp", plane_swap)
        two_side_in = lax.ppermute(two_side_sum, "ep", side_swap)
        [near_side_sum] = join(near_side_sum, [far_side_in], [BF16])
        [two_sum] = join(two_sum, [two_side_in], [BF16])
        [far_sum] = join(*later, [BF16], 0, [far_side_in])
        far_in = lax.ppermute(far_sum, "grp", plane_swap)
        near_side_in = lax.ppermute(near_side_sum, "ep", side_swap)
        two_in = lax.ppermute(two_sum, both_axes, backward)
        part = (row_count, columns)

        def by_columns(kernel, first_type, after_count, *operands):
            return pl.pallas_call(
                kernel,
                out_shape=(
                    jax.ShapeDtypeStruct(part, first_type),
                    jax.ShapeDtypeStruct(part, BF16),
                ),
                in_specs=[ANY] * after_count + [WHOLE] * (len(operands) - after_count),
                compiler_params=pltpu.CompilerParams(vmem_limit_bytes=16 * 2**20),
                cost_estimate=cost(row_count * model, 2**20),
                name=kernel.__name__,
            )(*operands)

        def crossed(pairs):
            return [(source, (target + ranks) % (2 * ranks)) for source, target in pairs]

        near_mine, near_other = by_columns(
            sum_kernel, BF16, 0, near_sum, near_side_in, two_in, far_in
        )
        base, own_other = by_columns(own_kernel, F32, 1, near_mine, state, own_sum, side_in)
        middle = row_count // 2
        own_over = [
            lax.ppermute(own_other[half : half + middle], "grp", plane_swap) for half in (0, middle)
        ]
        mine_in = lax.ppermute(near_mine, both_axes, backward)
        other_in = lax.ppermute(near_other, both_axes, crossed(backward))
        return pl.pallas_call(
            last_kernel,
            out_shape=jax.ShapeDtypeStruct(part, BF16),
            in_specs=[WHOLE] * 5,
            compiler_params=pltpu.CompilerParams(vmem_limit_bytes=16 * 2**20),
            cost_estimate=cost(0, 2**20),
            name="last",
        )(base, other_in, mine_in, *own_over)

    line = [packet]
    for _ in range(1, ring):
        line.append(lax.ppermute(line[-1], "ep", ring_next))
    totals = []
    for part in line:
        sums = run_expert([lax.ppermute(part, "ep", side_swap), part], packet, packet)
        over, here = join(*sums, [BF16, F32])
        totals.append(here + send(over, "ep", side_swap))
    moving = totals[1 % ring]
    for hop in list(range(2, ring)) + [0]:
        moving = totals[hop] + send(moving, "ep", ring_next)

    result = state + lax.dynamic_slice_in_dim(moving, group * columns, columns, 1)
    for by in range(1, groups):
        to = (group + by) % groups
        part = lax.dynamic_slice_in_dim(moving, to * columns, columns, 1)
        result = result + send(part, "grp", turn(by))
    return result.astype(BF16)


def solution(mesh):
    in_specs = (
        P("ep", None),
        P("ep", "grp"),
        P("ep", "grp"),
        P("ep", None),
        P("ep", None),
        P("grp", None, None),
        P("grp", None, None),
        P("grp", None),
        P(),
        P(),
        P("ep", None),
        P("ep", None, "grp"),
        P("ep", None, "grp"),
        P("ep", "grp", None),
        P("ep", None),
        P("ep"),
        P("ep", None, None),
    )
    out_specs = P("ep", "grp")
    return jax.shard_map(local, mesh=mesh, in_specs=in_specs, out_specs=out_specs, check_vma=False)
```

```python
import functools

import jax
import jax.numpy as jnp
from jax import lax
from jax.experimental import pallas as pl
from jax.experimental.pallas import tpu as pltpu
from jax.sharding import PartitionSpec as P

F32 = jnp.float32
BF16 = jnp.bfloat16
HIDDEN = -1e30
VMEM = pltpu.VMEM
ANY = pl.BlockSpec(memory_space=pl.ANY)
WHOLE = pl.BlockSpec(memory_space=pltpu.VMEM)


def dot(a, b):
    return jnp.dot(a, b, preferred_element_type=F32)


def dot_rows(a, b):
    return lax.dot_general(a, b, (((1,), (1,)), ((), ())), preferred_element_type=F32)


def cost(products, moved_bytes):
    return pl.CostEstimate(flops=2 * products, bytes_accessed=moved_bytes, transcendentals=0)


def fetch_all(sources, buffers, sems):
    copies = []
    for at, (source, buffer) in enumerate(zip(sources, buffers)):
        copy = pltpu.make_async_copy(source, buffer, sems.at[at])
        copy.start()
        copies.append(copy)
    return copies


def lay_tokens(keys, start, ref, tokens, width):
    count = ref.shape[0]
    for token in range(tokens):
        keys[start : start + count, :width] = ref[:, token * width : (token + 1) * width]
        start += count
    return start


def pick_kernel(pieces, moves_any, cache_any, out_ref, moves_ref, cache, stacked, sems):
    got = fetch_all((moves_any, cache_any), (moves_ref, cache), sems)
    ranks, per_rank, wide = out_ref.shape
    slots = moves_ref.shape[0]
    resident = cache.shape[0]
    rows = ranks * per_rank
    row = lax.broadcasted_iota(jnp.int32, (rows, ranks), 0)
    rank = lax.broadcasted_iota(jnp.int32, (rows, ranks), 1)
    chosen = jnp.zeros((rows, ranks), jnp.int32)
    got[0].wait()
    for slot in range(slots):
        here = (row // per_rank == rank) & (row % per_rank // pieces == slot)
        chosen = chosen + jnp.where(here, moves_ref[slot : slot + 1, :], 0)
    block = jnp.clip(jnp.sum(chosen, axis=1, keepdims=True), 0, resident - 1)
    at = lax.broadcasted_iota(jnp.int32, (rows, pieces * resident), 0)
    source = lax.broadcasted_iota(jnp.int32, (rows, pieces * resident), 1)
    pick = (source // resident == at % pieces) & (source % resident == block)
    got[1].wait()
    for piece in range(pieces):
        stacked[piece * resident : (piece + 1) * resident, :] = cache[:, piece * wide : (piece + 1) * wide]
    picked = dot(pick.astype(F32).astype(BF16), stacked[...]).astype(BF16)
    out_ref[...] = picked.reshape(ranks, per_rank, wide)


def resident_kernel(
    dims, nope, rope_rows, fresh, cache, absorb, bias_ref,
    query_ref, mixed_ref,
    keys,
):
    head_count, nope_dim, latent, rope, block_size, steps = dims
    width = latent + rope
    rows = nope.shape[0]
    padding = keys.shape[1] - width
    keys[:, latent:] = jnp.zeros((keys.shape[0], keys.shape[1] - latent), BF16)
    start = lay_tokens(keys, 0, cache, block_size, width)
    lay_tokens(keys, start, fresh, steps, width)
    for head in range(head_count):
        q_latent = dot(nope[:, head * nope_dim : (head + 1) * nope_dim], absorb[head])
        q_rope = rope_rows[:, head * rope : (head + 1) * rope]
        fill = jnp.zeros((rows, padding), BF16)
        query_ref[head * rows : (head + 1) * rows, :] = jnp.concatenate(
            [q_latent.astype(BF16), q_rope, fill], axis=1
        )
    scale = (nope_dim + rope) ** (-0.5)
    part = min(4, head_count) * rows
    for first in range(0, head_count * rows, part):
        score = dot_rows(query_ref[first : first + part, :], keys[...])
        score = score.reshape(part // rows, rows, -1) * scale + bias_ref[...][None]
        score = score.reshape(part, -1)
        peak = jnp.max(score, axis=1, keepdims=True)
        weight = jnp.exp(score - peak)
        total = jnp.sum(weight, axis=1, keepdims=True)
        mixed_ref[first : first + part, :latent] = dot(weight.astype(BF16), keys[:, :latent])
        lane = lax.broadcasted_iota(jnp.int32, (part, 128), 1)
        mixed_ref[first : first + part, latent:] = jnp.where(lane < 64, peak, total)


def moved_kernel(
    dims, moved_any, query_any, bias_any, mixed_any, value_any, proj_any,
    share_ref,
    moved, query, bias, mixed, value, proj, keys, heads_out, sems,
):
    head_count, nope_dim, latent, rope, block_size, steps = dims
    width = latent + rope
    rows = heads_out.shape[0]
    got = fetch_all(
        (moved_any, query_any, bias_any, mixed_any, value_any, proj_any),
        (moved, query, bias, mixed, value, proj),
        sems,
    )
    keys[:, latent:] = jnp.zeros((keys.shape[0], keys.shape[1] - latent), BF16)
    scale = (nope_dim + rope) ** (-0.5)
    value_dim = value.shape[2]
    got[0].wait()
    count = moved.shape[0] * moved.shape[1]
    for half in range(2):
        part = moved[:, :, half * width : (half + 1) * width]
        keys[half * count : (half + 1) * count, :width] = part.reshape(count, width)
    got[1].wait()
    got[2].wait()
    group = min(8, head_count)
    for first in range(0, head_count, group):
        at = slice(first * rows, (first + group) * rows)
        score = dot_rows(query[at, :], keys[...])
        score = score.reshape(group, rows, -1) * scale + bias[...][None]
        score = score.reshape(group * rows, -1)
        if first == 0:
            got[3].wait()
        before = mixed[at, latent : latent + 1]
        peak = jnp.maximum(jnp.max(score, axis=1, keepdims=True), before)
        weight = jnp.exp(score - peak)
        keep = jnp.exp(before - peak)
        total = jnp.sum(weight, axis=1, keepdims=True) + mixed[at, latent + 64 : latent + 65] * keep
        joined = dot(weight.astype(BF16), keys[:, :latent]) + mixed[at, :latent] * keep
        joined = (joined / total).astype(BF16)
        if first == 0:
            got[4].wait()
        for head in range(first, first + group):
            own = joined[(head - first) * rows : (head - first + 1) * rows]
            heads_out[:, head * value_dim : (head + 1) * value_dim] = dot(own, value[head]).astype(BF16)
    got[5].wait()
    share_ref[...] = dot(heads_out[...], proj[...]).astype(BF16)


def own_columns(ref, shift):
    groups = lax.axis_size("grp")
    columns = ref.shape[1] // groups
    first = (lax.axis_index("grp") + shift) % groups * columns
    return ref[:, pl.ds(pl.multiple_of(first, 128), columns)]


def norm_kernel(experts, own_any, hidden_any, loaded_any, gain_ref, router_ref, ids_ref, *refs):
    parts, (state_ref, packet_ref, own, hidden, whole, sems) = refs[:-6], refs[-6:]
    got = fetch_all((own_any, hidden_any), (own, hidden), sems)
    rows, model = hidden.shape
    state = parts[0][...].astype(F32)
    for part in parts[1:]:
        state = state + part[...].astype(F32)
    for copy in got:
        copy.wait()
    state = state + own[...].astype(F32) + hidden[...].astype(F32)
    whole[...] = state
    state_ref[...] = own_columns(whole, 0)
    square = jnp.mean(state * state, axis=1, keepdims=True)
    normed = (state * lax.rsqrt(square + 1e-06) * gain_ref[...].astype(F32)).astype(BF16)
    packet_ref[:, :model] = normed
    logits = dot_rows(router_ref[...], normed)
    names = lax.broadcasted_iota(jnp.int32, (experts, rows), 0)
    named = names == ids_ref[0:1, :]
    for k in range(1, ids_ref.shape[0]):
        named = named | (names == ids_ref[k : k + 1, :])
    chosen = jnp.where(named, jax.nn.sigmoid(logits), 0.0)
    weight = chosen / jnp.sum(chosen, axis=0, keepdims=True)
    high = weight.astype(BF16)
    low = (weight - high.astype(F32)).astype(BF16)
    extra = packet_ref.shape[1] - model
    both = jnp.concatenate([high, low], axis=0)
    place = lax.broadcasted_iota(jnp.int32, (2 * experts, extra), 0)
    lane = lax.broadcasted_iota(jnp.int32, (2 * experts, extra), 1)
    turned = lax.dot_general(
        both, (place == lane).astype(BF16), (((0,), (0,)), ((), ())), preferred_element_type=F32
    )
    packet_ref[:, model:] = turned.astype(BF16)


def load_kernel(after_any, gate_any, up_any, down_any, gate_ref, up_ref, down_ref, sems):
    sources, targets = (gate_any, up_any, down_any), (gate_ref, up_ref, down_ref)
    for copy in fetch_all(sources, targets, sems):
        copy.wait()


def pack_kernel(after_any, *refs):
    count = refs[0].shape[0]
    for at, ref in enumerate(refs[:-1]):
        refs[-1][at * count : (at + 1) * count, :] = ref[...]


def expert_kernel(experts, after_any, here_ref, across_ref, gate_ref, up_ref, down_ref, *out_refs):
    near_ref, *far_refs = out_refs
    model = gate_ref.shape[1]
    packet = jnp.concatenate([here_ref[...], across_ref[...]], axis=0)
    rows = packet[:, :model]
    extra = packet[:, model:].astype(F32)
    names = lax.broadcasted_iota(jnp.int32, extra.shape, 1)
    me = lax.axis_index("ep")
    mine = (names == me) | (names == me + experts)
    weight = jnp.sum(jnp.where(mine, extra, 0.0), axis=1, keepdims=True)
    gate = dot_rows(rows, gate_ref[...])
    up = dot_rows(rows, up_ref[...])
    inner = (gate * jax.nn.sigmoid(gate) * up * weight).astype(BF16)
    result = dot(inner, down_ref[...]).astype(BF16)
    half = near_ref.shape[0]
    near_ref[...] = result[:half]
    height = half // len(far_refs)
    for at, far_ref in enumerate(far_refs):
        far_ref[...] = result[half + at * height : half + (at + 1) * height]


def join_kernel(first, back_count, after_count, near_ref, *refs):
    back_refs, out_refs = refs[after_count : after_count + back_count], refs[after_count + back_count :]
    count = out_refs[0].shape[0]
    height = back_refs[0].shape[0]
    step = min(count, height)
    for at, ref in enumerate(out_refs, first):
        for row in range(at * count, (at + 1) * count, step):
            back = back_refs[row // height][row % height : row % height + step, :].astype(F32)
            total = near_ref[row : row + step, :].astype(F32) + back
            ref[row - at * count : row - at * count + step, :] = total.astype(ref.dtype)


def own_kernel(after_any, state_ref, own_ref, side_ref, base_ref, other_ref):
    mine, other = (own_columns(own_ref, by) + own_columns(side_ref, by).astype(F32) for by in (0, 1))
    base_ref[...] = state_ref[...] + mine
    other_ref[...] = other.astype(BF16)


def last_kernel(base_ref, other_ref, mine_ref, upper_ref, lower_ref, out_ref):
    middle = upper_ref.shape[0]
    for rows, ref in ((slice(0, middle), upper_ref), (slice(middle, 2 * middle), lower_ref)):
        total = base_ref[rows, :] + other_ref[rows, :].astype(F32) + mine_ref[rows, :].astype(F32)
        out_ref[rows, :] = (total + ref[...].astype(F32)).astype(BF16)


def sum_kernel(*refs):
    parts, (mine_ref, other_ref) = refs[:-2], refs[-2:]
    for shift, ref in ((0, mine_ref), (1, other_ref)):
        total = own_columns(parts[0], shift).astype(F32)
        for part in parts[1:]:
            total = total + own_columns(part, shift).astype(F32)
        ref[...] = total.astype(BF16)


def local(
    hidden_in,
    query_nope,
    query_rope,
    new_latent,
    latent_cache,
    key_absorb,
    value_absorb,
    output_proj,
    norm_gain,
    router_proj,
    expert_ids,
    expert_gate,
    expert_up,
    expert_down,
    block_table,
    lengths,
    subtree_moves,
):
    head_count, nope_dim, latent = key_absorb.shape
    rope = query_rope.shape[1] // head_count
    width = latent + rope
    requests, table_len = block_table.shape
    steps = new_latent.shape[1] // width
    row_count, model = hidden_in.shape
    block_size = latent_cache.shape[1] // width
    resident = latent_cache.shape[0]
    experts = router_proj.shape[1]
    groups = lax.axis_size("grp")
    group = lax.axis_index("grp")
    ranks = lax.axis_size("ep")
    me = lax.axis_index("ep")
    ring = ranks // 4
    core_swap = [(i, i ^ 1) for i in range(ranks)]
    side_swap = [(i, i ^ 2) for i in range(ranks)]
    visit = list(range(0, ring, 2)) + list(range(ring - 1 - ring % 2, 0, -2))
    turn_of = {chip: at for at, chip in enumerate(visit)}

    def along(rank, by):
        return visit[(turn_of[rank // 4] + by) % ring] * 4 + rank % 4

    ring_next = [(i, along(i, 1)) for i in range(ranks)]
    both_axes = ("grp", "ep")

    def turn(by):
        return [(g, (g + by) % groups) for g in range(groups)]

    slots = subtree_moves.shape[2]
    pieces = block_size // 2
    outgoing = pl.pallas_call(
        functools.partial(pick_kernel, pieces),
        out_shape=jax.ShapeDtypeStruct((ranks, slots * pieces, 2 * width), BF16),
        in_specs=[ANY] * 2,
        scratch_shapes=[
            VMEM((slots, ranks), jnp.int32),
            VMEM(latent_cache.shape, BF16),
            VMEM((pieces * resident, 2 * width), BF16),
            pltpu.SemaphoreType.DMA((2,)),
        ],
        compiler_params=pltpu.CompilerParams(vmem_limit_bytes=60 * 2**20),
        cost_estimate=cost(0, 4 * 2**20),
        name="pick",
    )(subtree_moves[0].T, latent_cache)
    arrived = lax.all_to_all(outgoing, "ep", split_axis=0, concat_axis=0, tiled=True)

    place = jnp.arange(table_len, dtype=jnp.int32)
    usable = jnp.clip(lengths[:, None] - place[None, :] * block_size, 0, block_size)
    blocks = jnp.arange(resident + ranks * slots, dtype=jnp.int32)
    limit = jnp.sum(
        jnp.where(block_table[:, :, None] == blocks[None, None, :], usable[:, :, None], 0), axis=1
    )
    token = jnp.arange(block_size, dtype=jnp.int32)
    row = jnp.arange(row_count, dtype=jnp.int32)
    fresh = jnp.arange(steps * requests, dtype=jnp.int32)
    fresh_open = ((row // steps)[:, None] == (fresh % requests)[None, :]) & (
        (fresh // requests)[None, :] <= (row % steps)[:, None]
    )
    near_open = (limit[:, None, :resident] > token[None, :, None]).reshape(requests, -1)
    near_open = jnp.concatenate([jnp.repeat(near_open, steps, axis=0), fresh_open], axis=1)
    near_bias = jnp.where(near_open, 0.0, HIDDEN).astype(F32)
    by_key = jnp.repeat(limit[:, resident:], pieces, axis=1)
    at_token = 2 * (jnp.arange(ranks * slots * pieces, dtype=jnp.int32) % pieces)
    moved_open = jnp.concatenate([by_key > at_token[None], by_key > at_token[None] + 1], axis=1)
    moved_bias = jnp.repeat(jnp.where(moved_open, 0.0, HIDDEN).astype(F32), steps, axis=0)

    padded = -(-width // 128) * 128
    query_rows = head_count * row_count
    dims = (head_count, nope_dim, latent, rope, block_size, steps)
    query, mixed = pl.pallas_call(
        functools.partial(resident_kernel, dims),
        out_shape=(
            jax.ShapeDtypeStruct((query_rows, padded), BF16),
            jax.ShapeDtypeStruct((query_rows, latent + 128), F32),
        ),
        scratch_shapes=[VMEM((near_bias.shape[1], padded), BF16)],
        compiler_params=pltpu.CompilerParams(vmem_limit_bytes=16 * 2**20),
        cost_estimate=cost(query_rows * near_bias.shape[1] * (padded + latent), 8 * 2**20),
        name="attend_resident",
    )(query_nope, query_rope, new_latent, latent_cache, key_absorb, near_bias)
    share = pl.pallas_call(
        functools.partial(moved_kernel, dims),
        out_shape=jax.ShapeDtypeStruct((row_count, model), BF16),
        in_specs=[ANY] * 6,
        scratch_shapes=[
            VMEM(arrived.shape, BF16),
            VMEM(query.shape, BF16),
            VMEM(moved_bias.shape, F32),
            VMEM(mixed.shape, F32),
            VMEM(value_absorb.shape, BF16),
            VMEM(output_proj.shape, BF16),
            VMEM((moved_bias.shape[1], padded), BF16),
            VMEM((row_count, head_count * value_absorb.shape[2]), BF16),
            pltpu.SemaphoreType.DMA((6,)),
        ],
        compiler_params=pltpu.CompilerParams(vmem_limit_bytes=56 * 2**20),
        cost_estimate=cost(query_rows * moved_bias.shape[1] * (padded + latent), 10 * 2**20),
        name="attend_moved",
    )(arrived, query, moved_bias, mixed, value_absorb, output_proj)
    shares = [lax.ppermute(share, "grp", turn(by)) for by in range(1, groups)]

    held = [jnp.swapaxes(expert_gate[0], 0, 1), jnp.swapaxes(expert_up[0], 0, 1), expert_down[0]]
    gate_rows, up_rows, down_rows = pl.pallas_call(
        load_kernel,
        out_shape=[jax.ShapeDtypeStruct(array.shape, BF16) for array in held],
        in_specs=[ANY] * 4,
        out_specs=[WHOLE] * 3,
        scratch_shapes=[pltpu.SemaphoreType.DMA((3,))],
        compiler_params=pltpu.CompilerParams(vmem_limit_bytes=44 * 2**20),
        cost_estimate=cost(0, 12 * 2**20),
        name="load",
    )(share, *held)

    extra = -(-2 * experts // 128) * 128
    columns = model // groups
    state, packet = pl.pallas_call(
        functools.partial(norm_kernel, experts),
        out_shape=(
            jax.ShapeDtypeStruct((row_count, columns), F32),
            jax.ShapeDtypeStruct((row_count, model + extra), BF16),
        ),
        in_specs=[ANY] * 3 + [WHOLE] * (2 + groups),
        scratch_shapes=[
            VMEM((row_count, model), BF16),
            VMEM((row_count, model), BF16),
            VMEM((row_count, model), F32),
            pltpu.SemaphoreType.DMA((2,)),
        ],
        compiler_params=pltpu.CompilerParams(vmem_limit_bytes=16 * 2**20),
        cost_estimate=cost(row_count * model * 128, 4 * 2**20),
        name="norm",
    )(share, hidden_in, down_rows, norm_gain[None, :], router_proj.T, expert_ids.T, *shares)

    def run_expert(rows, after, run_after, back=1):
        half = len(rows) * row_count
        here = pl.pallas_call(
            pack_kernel,
            out_shape=jax.ShapeDtypeStruct((half, model + extra), BF16),
            in_specs=[ANY] + [WHOLE] * len(rows),
            compiler_params=pltpu.CompilerParams(vmem_limit_bytes=16 * 2**20),
            cost_estimate=cost(0, 2 * half * model * 2),
            name="pack",
        )(after, *rows)
        across = lax.ppermute(here, "ep", core_swap)
        near, *far = pl.pallas_call(
            functools.partial(expert_kernel, experts),
            out_shape=[
                jax.ShapeDtypeStruct((half // cuts, model), BF16) for cuts in [1] + [back] * back
            ],
            in_specs=[ANY] + [WHOLE] * 5,
            compiler_params=pltpu.CompilerParams(vmem_limit_bytes=24 * 2**20),
            cost_estimate=cost(6 * half * model * gate_rows.shape[0], 12 * 2**20),
            name="expert",
        )(run_after, here, across, gate_rows, up_rows, down_rows)
        return near, [lax.ppermute(part, "ep", core_swap) for part in far]

    def join(near, back, types, first=0, after=()):
        return pl.pallas_call(
            functools.partial(join_kernel, first, len(back), len(after)),
            out_shape=[jax.ShapeDtypeStruct((row_count, model), kind) for kind in types],
            in_specs=[WHOLE] + [ANY] * len(after) + [WHOLE] * len(back),
            compiler_params=pltpu.CompilerParams(vmem_limit_bytes=16 * 2**20),
            cost_estimate=cost(row_count * model, 2**20),
            name="join",
        )(near, *after, *back)

    def send(value, axes, pairs):
        return lax.ppermute(value.astype(BF16), axes, pairs).astype(F32)

    if ring == 4 and groups == 2:
        def ring_step(sign):
            return [
                (g * ranks + i, g * ranks + along(i, sign * (1 - 2 * g)))
                for g in range(2)
                for i in range(ranks)
            ]

        onward, backward, plane_swap = ring_step(1), ring_step(-1), [(0, 1), (1, 0)]
        near = lax.ppermute(packet, both_axes, onward)
        side = lax.ppermute(packet, "ep", side_swap)
        two = lax.ppermute(near, both_axes, onward)
        near_side = lax.ppermute(near, "ep", side_swap)
        far = lax.ppermute(near, "grp", plane_swap)
        two_side = lax.ppermute(two, "ep", side_swap)
        far_side = lax.ppermute(near_side, "grp", plane_swap)
        early = run_expert([packet, side, near], packet, packet)
        later = run_expert([far, near_side, two], early[0], packet)
        own_sum, side_sum, near_sum = join(*early, [F32, BF16, F32])
        side_in = lax.ppermute(side_sum, "ep", side_swap)
        last = run_expert([far_side, two_side], later[0], side_sum, 2)
        near_side_sum, two_sum = join(*later, [F32, F32], 1)
        far_side_sum, two_side_sum = join(*last, [BF16, BF16], 0, [side_in])
        far_side_in = lax.ppermute(far_side_sum, "grp", plane_swap)
        two_side_in = lax.ppermute(two_side_sum, "ep", side_swap)
        [near_side_sum] = join(near_side_sum, [far_side_in], [BF16])
        [two_sum] = join(two_sum, [two_side_in], [BF16])
        [far_sum] = join(*later, [BF16], 0, [far_side_in])
        far_in = lax.ppermute(far_sum, "grp", plane_swap)
        near_side_in = lax.ppermute(near_side_sum, "ep", side_swap)
        two_in = lax.ppermute(two_sum, both_axes, backward)
        part = (row_count, columns)

        def by_columns(kernel, first_type, after_count, *operands):
            return pl.pallas_call(
                kernel,
                out_shape=(
                    jax.ShapeDtypeStruct(part, first_type),
                    jax.ShapeDtypeStruct(part, BF16),
                ),
                in_specs=[ANY] * after_count + [WHOLE] * (len(operands) - after_count),
                compiler_params=pltpu.CompilerParams(vmem_limit_bytes=16 * 2**20),
                cost_estimate=cost(row_count * model, 2**20),
                name=kernel.__name__,
            )(*operands)

        def crossed(pairs):
            return [(source, (target + ranks) % (2 * ranks)) for source, target in pairs]

        near_mine, near_other = by_columns(
            sum_kernel, BF16, 0, near_sum, near_side_in, two_in, far_in
        )
        base, own_other = by_columns(own_kernel, F32, 1, near_mine, state, own_sum, side_in)
        middle = row_count // 2
        own_over = [
            lax.ppermute(own_other[half : half + middle], "grp", plane_swap) for half in (0, middle)
        ]
        mine_in = lax.ppermute(near_mine, both_axes, backward)
        other_in = lax.ppermute(near_other, both_axes, crossed(backward))
        return pl.pallas_call(
            last_kernel,
            out_shape=jax.ShapeDtypeStruct(part, BF16),
            in_specs=[WHOLE] * 5,
            compiler_params=pltpu.CompilerParams(vmem_limit_bytes=16 * 2**20),
            cost_estimate=cost(0, 2**20),
            name="last",
        )(base, other_in, mine_in, *own_over)

    line = [packet]
    for _ in range(1, ring):
        line.append(lax.ppermute(line[-1], "ep", ring_next))
    totals = []
    for part in line:
        sums = run_expert([lax.ppermute(part, "ep", side_swap), part], packet, packet)
        over, here = join(*sums, [BF16, F32])
        totals.append(here + send(over, "ep", side_swap))
    moving = totals[1 % ring]
    for hop in list(range(2, ring)) + [0]:
        moving = totals[hop] + send(moving, "ep", ring_next)

    result = state + lax.dynamic_slice_in_dim(moving, group * columns, columns, 1)
    for by in range(1, groups):
        to = (group + by) % groups
        part = lax.dynamic_slice_in_dim(moving, to * columns, columns, 1)
        result = result + send(part, "grp", turn(by))
    return result.astype(BF16)


def solution(mesh):
    in_specs = (
        P("ep", None),
        P("ep", "grp"),
        P("ep", "grp"),
        P("ep", None),
        P("ep", None),
        P("grp", None, None),
        P("grp", None, None),
        P("grp", None),
        P(),
        P(),
        P("ep", None),
        P("ep", None, "grp"),
        P("ep", None, "grp"),
        P("ep", "grp", None),
        P("ep", None),
        P("ep"),
        P("ep", None, None),
    )
    out_specs = P("ep", "grp")
    return jax.shard_map(local, mesh=mesh, in_specs=in_specs, out_specs=out_specs, check_vma=False)
```
